512 devices in a mesh: blk: 64 (over z, y), mode: 8 (over x, core).
Axes of the slice: x: 4, y: 8, z: 8, core: 2. Of those that a mesh axis runs over, the one named last changes fastest.
Arguments:
- start_modes: float32 [64, 3, 256, 16, 128], P('mode', None, 'blk'), may hold values from -6 to 6
- materials: int32 [256, 16, 128], P('blk'), may hold values from 0 to 7
- stiffness_table: float32 [8], replicated, may hold values from 0.25 to 4
Outputs:
- basis: float32 [64, 3, 256, 16, 128], P('mode', None, 'blk')
- projected: float32 [64, 64], replicated
The draws below stay inside these ranges and needn't reach their ends.
All inputs are finite; a program needn't handle non-finite values.
Results may differ from the reference program's by a relative error of at most 0.00007.
Values sent between devices are 32-bit elements; how exact they have to be, the bound alone decides.
A program may use at most 64 MiB of HBM per device.

```python
import math
import jax
import jax.numpy as jnp
from jax import lax

MODES = 64
COMP = 3
NMAT = 8
NY = 16
NZ = 128
NX = 256


def place_ends(drawn, stream_key, smallest, top_value):
    spot = [jax.random.randint(jax.random.fold_in(stream_key, axis), (), 0, length) for axis, length in enumerate(drawn.shape)]
    main_axis = drawn.shape.index(max(drawn.shape))
    beside = spot[:main_axis] + [(spot[main_axis] + 1) % drawn.shape[main_axis]] + spot[main_axis + 1:]
    return drawn.at[tuple(spot)].set(smallest).at[tuple(beside)].set(top_value)


def block_scale(own_key, dims, split, low, high):
    def one(axis_at, parts):
        draws = jax.random.uniform(jax.random.fold_in(jax.random.fold_in(own_key, 6), axis_at), (parts,), jnp.float32, low / len(split), high / len(split))
        return jnp.repeat(jnp.exp(draws), dims[axis_at] // parts).reshape((-1,) + (1,) * (len(dims) - axis_at - 1))

    factor_of = one(*split[0])
    for cut in split[1:]:
        factor_of = factor_of * one(*cut)
    return factor_of


def noise(own_key, extent, deviation, bound, split=(), kind=jnp.bfloat16):
    gain = block_scale(own_key, extent, split, -0.22, 0.18) if split else 1.0
    array = jax.random.normal(own_key, extent, jnp.float32) * deviation * gain
    return jnp.minimum(jnp.maximum(array, -bound), bound).astype(kind)


def setup_inputs(seed: int = 0) -> dict:
    streams_of = jax.random.split(jax.random.key(seed), 4)
    start_modes = noise(streams_of[0], (MODES, COMP, NX, NY, NZ), 1.0, 6.0, ((0, 8), (2, 64)), jnp.float32)
    materials = place_ends(jax.random.randint(streams_of[1], (NX, NY, NZ), 0, NMAT), jax.random.fold_in(streams_of[1], 1), 0, NMAT - 1).astype(jnp.int32)
    stiffness_table = jnp.clip(jnp.exp(jax.random.uniform(streams_of[2], (NMAT,), jnp.float32, math.log(0.25), math.log(4.0))), 0.25, 4.0)
    return {"start_modes": start_modes, "materials": materials, "stiffness_table": stiffness_table}


CENTER = 64.0
HALF_WIDTH = 56.0
MASS_SHIFT = 0.5

def stiffness_root(materials, stiffness_table):
    count = stiffness_table.shape[0]
    labels = jnp.arange(count, dtype=jnp.int32).reshape((count, 1, 1, 1))
    indicator = (materials[None] == labels).astype(jnp.float32)
    return jnp.sqrt(lax.optimization_barrier(jnp.sum(indicator * stiffness_table.reshape((count, 1, 1, 1)), axis=0)))

def box_sum(padded):
    along_x = padded[..., :-2, 1:-1, 1:-1] + padded[..., 1:-1, 1:-1, 1:-1] + padded[..., 2:, 1:-1, 1:-1]
    wide_y = jnp.pad(along_x, [(0, 0)] * (along_x.ndim - 3) + [(0, 0), (1, 1), (1, 1)])
    along_y = wide_y[..., :-2, :] + wide_y[..., 1:-1, :] + wide_y[..., 2:, :]
    return along_y[..., :-2] + along_y[..., 1:-1] + along_y[..., 2:]

def operate(field, stiff_root):
    weighted = stiff_root * field
    padded = jnp.pad(weighted, [(0, 0)] * (field.ndim - 3) + [(1, 1), (1, 1), (1, 1)])
    return stiff_root * (27.0 * weighted - box_sum(padded)) + MASS_SHIFT * field

def reference(start_modes, materials, stiffness_table):
    stiff_root = stiffness_root(materials, stiffness_table)

    def filter_one(field):
        before = field
        current = (operate(field, stiff_root) - CENTER * field) / HALF_WIDTH
        for degree_step in range(3):
            following = 2.0 * (operate(current, stiff_root) - CENTER * current) / HALF_WIDTH - before
            before, current = (current, following)
        return (current, operate(current, stiff_root))
    filtered, image = lax.map(filter_one, start_modes)
    modes = filtered.shape[0]
    flat_basis = filtered.reshape((modes, -1))
    flat_image = image.reshape((modes, -1))
    high = lax.Precision.HIGHEST
    gram = jnp.dot(flat_basis, flat_basis.T, precision=high)
    cross = jnp.dot(flat_basis, flat_image.T, precision=high)
    factor = jnp.linalg.cholesky(gram)
    identity = jnp.eye(modes, dtype=jnp.float32)
    inverse = lax.linalg.triangular_solve(factor, identity, left_side=True, lower=True)
    basis = jnp.dot(inverse, flat_basis, precision=high).reshape(filtered.shape)
    projected = jnp.dot(jnp.dot(inverse, cross, precision=high), inverse.T, precision=high)
    return (basis, projected)
```

```python
import functools
import math

import jax
import jax.numpy as jnp
from jax import lax
from jax.experimental import pallas as pl
from jax.experimental.pallas import tpu as pltpu
from jax.sharding import PartitionSpec as P

CENTER = 64.0
HALF_WIDTH = 56.0
MASS_SHIFT = 0.5
MESH = pl.DeviceIdType.MESH
HIGH = lax.Precision.HIGHEST
STEPS = 5


def kernel(blks, groups, x_ref, mat_ref, tab_ref, out_ref, proj_ref,
           coef, field, halo_out, halo_in, filt_out, image_out, filt_in, image_in,
           wide, back, part, part_in, tile_y, in_y, tile_z, in_z, tile_all, total,
           halo_send, halo_recv, filt_send, filt_recv, image_send, image_recv,
           back_send, back_recv, sum_send, sum_recv):
    modes, comps, planes, ny, nz = x_ref.shape
    every = modes * groups
    side = math.isqrt(blks)
    blk, me = lax.axis_index("blk"), lax.axis_index("mode")
    left, right = lax.rem(blk + blks - 1, blks), lax.rem(blk + 1, blks)
    my_z, my_y = lax.div(blk, side), lax.rem(blk, side)

    def mode_peer(step):
        return lax.rem(me + step, groups)

    def y_peer(step):
        return my_z * side + lax.rem(my_y + step, side)

    def z_peer(step):
        return lax.rem(my_z + step, side) * side + my_y

    barrier = pltpu.get_barrier_semaphore()

    def greet(to_blk, to_mode):
        pl.semaphore_signal(barrier, inc=1, device_id={"blk": to_blk, "mode": to_mode}, device_id_type=MESH)

    greet(left, me)
    greet(right, me)
    for step in range(1, groups):
        greet(blk, mode_peer(step))
    for step in range(1, side):
        greet(y_peer(step), me)
        greet(z_peer(step), me)

    scale = 2.0 / HALF_WIDTH
    for plane in range(planes):
        labels = mat_ref[plane]
        table = jnp.zeros((ny, nz), jnp.float32)
        for label in range(tab_ref.shape[0]):
            table = jnp.where(labels == label, tab_ref[label], table)
        root = jnp.sqrt(table)
        coef[0, plane] = root
        coef[1, plane] = scale * (27.0 * table + (MASS_SHIFT - CENTER))
        coef[2, plane] = scale * table
        coef[3, plane] = 1.0 / root
        coef[4, plane] = (27.0 * table + MASS_SHIFT) / root
    has_left = jnp.where(blk > 0, 1.0, 0.0).astype(jnp.float32)
    has_right = jnp.where(blk < blks - 1, 1.0, 0.0).astype(jnp.float32)
    top = planes - 1

    rows = lax.broadcasted_iota(jnp.int32, (ny, nz), 0)
    lanes = lax.broadcasted_iota(jnp.int32, (ny, nz), 1)

    def box(w):
        before = jnp.where(rows == 0, 0.0, pltpu.roll(w, 1, 0))
        after = jnp.where(rows == ny - 1, 0.0, pltpu.roll(w, ny - 1, 0))
        w = w + (before + after)
        before = jnp.where(lanes == 0, 0.0, pltpu.roll(w, 1, 1))
        after = jnp.where(lanes == nz - 1, 0.0, pltpu.roll(w, nz - 1, 1))
        return w + (before + after)

    def over_modes(body):
        def run(mode, carry):
            body(mode)
            return carry
        lax.fori_loop(0, modes, run, 0, unroll=2)

    def put(tiles, comp, plane, mode, value):
        for half in range(ny // 8):
            tiles[comp, plane * (ny // 8) + half, pl.ds(pl.multiple_of(mode * 8, 8), 8)] = value[8 * half:8 * half + 8]

    def halos(step, comp):
        return (
            pltpu.make_async_remote_copy(
                src_ref=halo_out.at[step, comp, 0], dst_ref=halo_in.at[step, comp, 1],
                send_sem=halo_send.at[step, comp, 0], recv_sem=halo_recv.at[step, comp, 1],
                device_id={"blk": left, "mode": me}, device_id_type=MESH),
            pltpu.make_async_remote_copy(
                src_ref=halo_out.at[step, comp, 1], dst_ref=halo_in.at[step, comp, 0],
                send_sem=halo_send.at[step, comp, 1], recv_sem=halo_recv.at[step, comp, 0],
                device_id={"blk": right, "mode": me}, device_id_type=MESH),
        )

    def spread(tiles_out, tiles_in, send, recv, comp):
        chunk = modes * 8
        for step in range(1, groups):
            peer = mode_peer(step)
            pltpu.make_async_remote_copy(
                src_ref=tiles_out.at[comp, peer],
                dst_ref=tiles_in.at[comp, pl.ds(pl.multiple_of(me * chunk, chunk), chunk)],
                send_sem=send.at[comp], recv_sem=recv.at[comp],
                device_id={"blk": blk, "mode": peer}, device_id_type=MESH).start()
        tiles_in[comp, pl.ds(pl.multiple_of(me * chunk, chunk), chunk)] = tiles_out[comp, me]

    def spread_wait(tiles_in, send, recv, comp):
        most = tiles_in.at[comp, pl.ds(0, (groups - 1) * modes * 8)]
        pltpu.make_async_copy(most, most, recv.at[comp]).wait()
        pltpu.make_async_copy(most, most, send.at[comp]).wait()

    def edges(step, comp):
        now = step % 2
        factor = 0.5 if step == 1 else 1.0

        def body(mode):
            for slot, plane, has in ((0, 0, has_left), (1, top, has_right)):
                if step == 0:
                    w = coef[0, plane] * x_ref[mode, comp, plane]
                else:
                    w = field[now, comp, plane, mode] - (factor * has) * coef[2, plane] * halo_in[step - 1, comp, slot, mode]
                field[now, comp, plane, mode] = w
                halo_out[step, comp, slot, mode] = box(w)
        over_modes(body)

    def inside(step, comp):
        now, other = step % 2, 1 - step % 2

        def body(mode):
            values, boxes = [], []
            for plane in range(planes):
                if step == 0 and 0 < plane < top:
                    w = coef[0, plane] * x_ref[mode, comp, plane]
                    field[now, comp, plane, mode] = w
                else:
                    w = field[now, comp, plane, mode]
                values.append(w)
                if plane == 0:
                    boxes.append(halo_out[step, comp, 0, mode])
                elif plane == top:
                    boxes.append(halo_out[step, comp, 1, mode])
                else:
                    boxes.append(box(w))
            for plane in range(planes):
                total_box = boxes[plane]
                if plane > 0:
                    total_box = total_box + boxes[plane - 1]
                if plane < top:
                    total_box = total_box + boxes[plane + 1]
                w = values[plane]
                if step == STEPS - 1:
                    put(filt_out, comp, plane, mode, w * coef[3, plane])
                    put(image_out, comp, plane, mode, coef[4, plane] * w - coef[0, plane] * total_box)
                else:
                    new = coef[1, plane] * w - coef[2, plane] * total_box
                    if step == 0:
                        new = 0.5 * new
                    else:
                        new = new - field[other, comp, plane, mode]
                    field[other, comp, plane, mode] = new
        over_modes(body)

    def close(comp):
        def body(mode):
            for slot, plane, has in ((0, 0, has_left), (1, top, has_right)):
                change = has * coef[0, plane] * halo_in[STEPS - 1, comp, slot, mode]
                for half in range(ny // 8):
                    at = (comp, plane * (ny // 8) + half, pl.ds(pl.multiple_of(mode * 8, 8), 8))
                    image_out[at] = image_out[at] - change[8 * half:8 * half + 8]
        over_modes(body)

    greeted = False
    for step in range(STEPS):
        for comp in range(comps):
            if step > 0:
                for copy in halos(step - 1, comp):
                    copy.wait()
            edges(step, comp)
            if not greeted:
                pl.semaphore_wait(barrier, 2 + (groups - 1) + 2 * (side - 1))
                greeted = True
            for copy in halos(step, comp):
                copy.start()
            inside(step, comp)
            if step == STEPS - 1:
                spread(filt_out, filt_in, filt_send, filt_recv, comp)
    for comp in range(comps):
        for copy in halos(STEPS - 1, comp):
            copy.wait()
        close(comp)
        spread(image_out, image_in, image_send, image_recv, comp)

    sums = jnp.zeros((every, 2 * every), jnp.float32)
    for comp in range(comps):
        spread_wait(filt_in, filt_send, filt_recv, comp)
        for row in range(8):
            wide[comp, pl.ds(every, every), pl.ds(row * nz, nz)] = filt_in[comp, pl.ds(row, every, stride=8)]
        spread_wait(image_in, image_send, image_recv, comp)
        for row in range(8):
            wide[comp, pl.ds(0, every), pl.ds(row * nz, nz)] = image_in[comp, pl.ds(row, every, stride=8)]
        both = wide[comp]
        sums = sums + lax.dot_general(both[every:], both, (((1,), (1,)), ((), ())),
                                      precision=HIGH, preferred_element_type=jnp.float32)
    part[...] = sums

    def exchange(phase, count, my_slot, source, target, own, device):
        for step in range(1, count):
            to_blk, to_mode, slot = device(step)
            pltpu.make_async_remote_copy(
                src_ref=source(slot), dst_ref=target.at[my_slot],
                send_sem=sum_send.at[phase], recv_sem=sum_recv.at[phase],
                device_id={"blk": to_blk, "mode": to_mode}, device_id_type=MESH).start()
        target[my_slot] = own
        most = target.at[pl.ds(0, count - 1)]
        pltpu.make_async_copy(most, most, sum_recv.at[phase]).wait()
        pltpu.make_async_copy(most, most, sum_send.at[phase]).wait()

    def added(slots, count):
        result = slots[0]
        for slot in range(1, count):
            result = result + slots[slot]
        return result

    exchange(0, groups, me, lambda slot: part.at[pl.ds(pl.multiple_of(slot * 8, 8), 8)], part_in,
             part[pl.ds(pl.multiple_of(me * 8, 8), 8)], lambda step: (blk, mode_peer(step), mode_peer(step)))
    own = added(part_in, groups)
    tile_y[...] = own
    exchange(1, side, my_y, lambda slot: tile_y, in_y, own, lambda step: (y_peer(step), me, 0))
    own = added(in_y, side)
    tile_z[...] = own
    exchange(2, side, my_z, lambda slot: tile_z, in_z, own, lambda step: (z_peer(step), me, 0))
    own = added(in_z, side)
    tile_all[...] = own
    exchange(3, groups, me, lambda slot: tile_all, total, own, lambda step: (blk, mode_peer(step), 0))

    sums = total[...].reshape((every, 2 * every))
    row_at = lax.broadcasted_iota(jnp.int32, (every, 2 * every), 0)
    lane_at = lax.broadcasted_iota(jnp.int32, (every, 2 * every), 1)
    cross = sums[:, :every]
    work = jnp.where(lane_at < every, jnp.where(lane_at == row_at, 1.0, 0.0), sums)
    blocks = [work[8 * j:8 * j + 8] for j in range(every // 8)]
    sub = lax.broadcasted_iota(jnp.int32, (8, 2 * every), 0)
    for k in range(every):
        j, r = divmod(k, 8)
        row = blocks[j][r:r + 1]
        row = row / row[:, every + k:every + k + 1]
        for i in range(j, every // 8):
            column = blocks[i][:, every + k:every + k + 1]
            change = column * row
            if i == j:
                change = jnp.where(sub > r, change, 0.0)
            blocks[i] = blocks[i] - change
    work = jnp.concatenate(blocks, axis=0)
    diagonal = jnp.sum(jnp.where(lane_at == row_at + every, work, 0.0), axis=1, keepdims=True)
    inverse = (work / jnp.sqrt(diagonal))[:, :every]

    def back_copies(comp):
        half = ny // 8
        for step in range(1, groups):
            peer = mode_peer(step)
            yield pltpu.make_async_remote_copy(
                src_ref=back.at[comp, pl.ds(peer * modes, modes)],
                dst_ref=out_ref.at[:, comp, lax.div(me, half), pl.ds(pl.multiple_of(lax.rem(me, half) * 8, 8), 8)],
                send_sem=back_send.at[comp], recv_sem=back_recv.at[comp],
                device_id={"blk": blk, "mode": peer}, device_id_type=MESH)

    def own_copy(comp):
        half = ny // 8
        return pltpu.make_async_copy(
            back.at[comp, pl.ds(me * modes, modes)],
            out_ref.at[:, comp, lax.div(me, half), pl.ds(pl.multiple_of(lax.rem(me, half) * 8, 8), 8)],
            back_send.at[comps + comp])

    for comp in range(comps):
        result = jnp.dot(inverse, wide[comp, pl.ds(every, every)], precision=HIGH, preferred_element_type=jnp.float32)
        for row in range(8):
            back[comp, :, row] = result[:, row * nz:(row + 1) * nz]
        for copy in back_copies(comp):
            copy.start()
        own_copy(comp).start()
    half = jnp.dot(inverse, cross, precision=HIGH, preferred_element_type=jnp.float32)
    proj_ref[...] = lax.dot_general(half, inverse, (((1,), (1,)), ((), ())), precision=HIGH,
                                    preferred_element_type=jnp.float32)
    for comp in range(comps):
        own_copy(comp).wait()
        most = back.at[comp, pl.ds(0, (groups - 1) * modes)]
        pltpu.make_async_copy(most, most, back_recv.at[comp]).wait()
        pltpu.make_async_copy(most, most, back_send.at[comp]).wait()


def shards(blks, groups, start_modes, materials, stiffness_table):
    modes, comps, planes, ny, nz = start_modes.shape
    every = modes * groups
    side = math.isqrt(blks)
    vmem, dma = pltpu.VMEM, pltpu.SemaphoreType.DMA
    f32 = jnp.float32
    whole = pl.BlockSpec(memory_space=pltpu.VMEM)
    halo = (STEPS, comps, 2, modes, ny, nz)
    tiles_out = (comps, groups, modes * 8, nz)
    tiles_in = (comps, every * 8, nz)
    tile = (8, 2 * every)
    return pl.pallas_call(
        functools.partial(kernel, blks, groups),
        out_shape=(jax.ShapeDtypeStruct(start_modes.shape, f32), jax.ShapeDtypeStruct((every, every), f32)),
        in_specs=[whole, whole, pl.BlockSpec(memory_space=pltpu.SMEM)],
        out_specs=(pl.BlockSpec(memory_space=pl.ANY), whole),
        scratch_shapes=[
            vmem((5, planes, ny, nz), f32),
            vmem((2, comps, planes, modes, ny, nz), f32),
            vmem(halo, f32), vmem(halo, f32),
            vmem(tiles_out, f32), vmem(tiles_out, f32),
            vmem(tiles_in, f32), vmem(tiles_in, f32),
            vmem((comps, 2 * every, 8 * nz), f32),
            vmem((comps, every, 8, nz), f32),
            vmem((every, 2 * every), f32), vmem((groups,) + tile, f32),
            vmem(tile, f32), vmem((side,) + tile, f32),
            vmem(tile, f32), vmem((side,) + tile, f32),
            vmem(tile, f32), vmem((groups,) + tile, f32),
            dma((STEPS, comps, 2)), dma((STEPS, comps, 2)),
            dma((comps,)), dma((comps,)), dma((comps,)), dma((comps,)),
            dma((2 * comps,)), dma((comps,)), dma((4,)), dma((4,)),
        ],
        compiler_params=pltpu.CompilerParams(
            collective_id=0, has_side_effects=True, vmem_limit_bytes=48 * 1024 * 1024),
    )(start_modes, materials, stiffness_table)


def solution(mesh):
    return jax.shard_map(
        functools.partial(shards, mesh.shape["blk"], mesh.shape["mode"]),
        mesh=mesh,
        in_specs=(P("mode", None, "blk", None, None), P("blk", None, None), P()),
        out_specs=(P("mode", None, "blk", None, None), P()),
        check_vma=False,
    )
```

```python
import functools
import math

import jax
import jax.numpy as jnp
from jax import lax
from jax.experimental import pallas as pl
from jax.experimental.pallas import tpu as pltpu
from jax.sharding import PartitionSpec as P

CENTER = 64.0
HALF_WIDTH = 56.0
MASS_SHIFT = 0.5
MESH = pl.DeviceIdType.MESH
HIGH = lax.Precision.HIGHEST
DEGREE = 4


def kernel(blks, groups, x_ref, mat_ref, tab_ref, out_ref, proj_ref,
           own, near, mats, table, table_in, coef, close_coef, field, edge_out, edge_in,
           filt_out, image_out, filt_in, image_in,
           back, part, part_in, tile_y, in_y, tile_z, in_z, tile_all, total,
           load, table_send, table_recv, near_send, near_recv, edge_send, edge_recv,
           filt_send, filt_recv, image_send, image_recv,
           back_send, back_recv, sum_send, sum_recv):
    modes, comps, planes, ny, nz = x_ref.shape
    every = modes * groups
    halves = ny // 8
    tiles = planes * halves
    side = math.isqrt(blks)
    blk, me = lax.axis_index("blk"), lax.axis_index("mode")
    left, right = lax.rem(blk + blks - 1, blks), lax.rem(blk + 1, blks)
    my_z, my_y = lax.div(blk, side), lax.rem(blk, side)

    def mode_peer(step):
        return lax.rem(me + step, groups)

    def y_peer(step):
        return my_z * side + lax.rem(my_y + step, side)

    def z_peer(step):
        return lax.rem(my_z + step, side) * side + my_y

    def remote(src, dst, send, recv, to_blk, to_mode):
        return pltpu.make_async_remote_copy(
            src_ref=src, dst_ref=dst, send_sem=send, recv_sem=recv,
            device_id={"blk": to_blk, "mode": to_mode}, device_id_type=MESH)

    barrier = pltpu.get_barrier_semaphore()

    def greet(to_blk, to_mode):
        pl.semaphore_signal(barrier, inc=1, device_id={"blk": to_blk, "mode": to_mode}, device_id_type=MESH)

    greet(left, me)
    greet(right, me)
    for step in range(1, side):
        greet(y_peer(step), me)
        greet(z_peer(step), me)
    for step in range(1, groups):
        greet(blk, mode_peer(step))

    load_mats = pltpu.make_async_copy(mat_ref, mats, load.at[comps])
    load_mats.start()
    load_own = [pltpu.make_async_copy(x_ref.at[:, comp], own.at[comp], load.at[comp]) for comp in range(comps)]
    for copy in load_own:
        copy.start()

    scale = 2.0 / HALF_WIDTH
    has_left = jnp.where(blk > 0, 1.0, 0.0).astype(jnp.float32)
    has_right = jnp.where(blk < blks - 1, 1.0, 0.0).astype(jnp.float32)

    def over_planes(first, count, body, unroll):
        def run(at, carry):
            body(first + at)
            return carry
        lax.fori_loop(0, count, run, 0, unroll=unroll)

    def all_modes(rows):
        return jnp.broadcast_to(rows[:, None, :], (ny, modes, nz))

    def coefficients(values, plane, has):
        root = jnp.sqrt(values)
        coef[0, plane] = all_modes(has * root)
        coef[1, plane] = all_modes(has * (scale * (27.0 * values + (MASS_SHIFT - CENTER))))
        coef[2, plane] = all_modes(has * (scale * values))
        return root

    load_mats.wait()

    def own_coefficients(plane):
        labels = mats[plane]
        values = jnp.zeros((ny, nz), jnp.float32)
        for label in range(tab_ref.shape[0]):
            values = jnp.where(labels == label, tab_ref[label], values)
        table[plane] = values
        root = coefficients(values, planes + plane, 1.0)
        close_coef[0, plane] = all_modes(1.0 / root)
        close_coef[1, plane] = all_modes((27.0 * values + MASS_SHIFT) / root)

    over_planes(0, planes, own_coefficients, 1)
    pl.semaphore_wait(barrier, 2 + (groups - 1) + 2 * (side - 1))

    to_sides = ((left, 1), (right, 0))
    table_copies = [remote(table, table_in.at[slot], table_send.at[slot], table_recv.at[slot], to, me)
                    for to, slot in to_sides]
    near_copies = [[remote(x_ref.at[:, comp], near.at[slot, comp], near_send.at[slot, comp], near_recv.at[slot, comp], to, me)
                    for to, slot in to_sides] for comp in range(comps)]
    edge_copies = [[remote(edge_out.at[comp, slot, pl.ds(0, 9 - slot)], edge_in.at[comp, slot, pl.ds(0, 9 - slot)],
                           edge_send.at[comp, slot], edge_recv.at[comp, slot], to, me)
                    for to, slot in to_sides] for comp in range(comps)]

    def start(copies):
        for copy in copies:
            copy.start()

    def finish(copies):
        for copy in copies:
            copy.wait()

    start(table_copies)
    start(near_copies[0])
    start(near_copies[1])
    finish(table_copies)

    def near_coefficients(plane):
        coefficients(table_in[0, plane], plane, has_left)
        coefficients(table_in[1, plane], 2 * planes + plane, has_right)

    over_planes(0, planes, near_coefficients, 1)

    lanes = lax.broadcasted_iota(jnp.int32, (ny, modes, nz), 2)
    none = jnp.zeros((1, modes, nz), jnp.float32)

    def box(u):
        v = u + (jnp.concatenate([none, u[:-1]], axis=0) + jnp.concatenate([u[1:], none], axis=0))
        before = jnp.where(lanes == 0, 0.0, pltpu.roll(v, 1, 2))
        after = jnp.where(lanes == nz - 1, 0.0, pltpu.roll(v, nz - 1, 2))
        return v + (before + after)

    def weigh(source, first):
        rows = source.reshape(modes * planes * ny, nz)

        def body(plane):
            for y in range(ny):
                field[0, first + plane, y] = coef[0, first + plane, y] * rows[pl.ds(plane * ny + y, modes, stride=planes * ny)]
        over_planes(0, planes, body, 1)

    def advance(step):
        now, other = step % 2, 1 - step % 2
        first = step + 1

        def body(plane):
            w = field[now, plane]
            u = field[now, plane - 1] + w + field[now, plane + 1]
            new = coef[1, plane] * w - coef[2, plane] * box(u)
            if step == 0:
                new = 0.5 * new
            else:
                new = new - field[other, plane]
            field[other, plane] = new
        over_planes(first, 3 * planes - 2 * first, body, 2)

    def tiles_of(target, comp, plane, value):
        for half in range(halves):
            target[comp, plane * halves + half] = value[8 * half:8 * half + 8]

    def finals(comp):
        first, last = field[0, planes], field[0, 2 * planes - 1]
        edge_out[comp, 1, :8] = box(first)[:8]
        lower = jnp.concatenate([jnp.zeros((8, modes, nz), jnp.float32), last[8:]], axis=0)
        edge_out[comp, 0] = box(lower)[7:]
        start(edge_copies[comp])
        for plane in range(planes):
            w = field[0, planes + plane]
            u = w
            if plane > 0:
                u = u + field[0, planes + plane - 1]
            if plane < planes - 1:
                u = u + field[0, planes + plane + 1]
            tiles_of(filt_out, comp, plane, w * close_coef[0, plane])
            tiles_of(image_out, comp, plane, close_coef[1, plane] * w - coef[0, planes + plane] * box(u))

    def spread(source, target, send, recv, comp, peer):
        remote(source.at[comp, peer], target.at[comp, :, pl.ds(pl.multiple_of(me * modes, modes), modes)],
               send.at[comp], recv.at[comp], blk, peer).start()

    def keep(source, target, comp):
        target[comp, :, pl.ds(pl.multiple_of(me * modes, modes), modes)] = source[comp, me]

    late = (0, 1, tiles - halves)

    def spread_early(comp):
        for step in range(1, groups):
            spread(filt_out, filt_in, filt_send, filt_recv, comp, mode_peer(step))
        for step in range(1, groups):
            peer = mode_peer(step)

            @pl.when((peer != late[0]) & (peer != late[1]) & (peer != late[2]))
            def _():
                spread(image_out, image_in, image_send, image_recv, comp, peer)
        keep(filt_out, filt_in, comp)

    def spread_late(comp):
        finish(edge_copies[comp])
        twice_left, twice_right = 2.0 * has_left, 2.0 * has_right
        image_out[comp, 0, 7] = image_out[comp, 0, 7] - twice_left * coef[0, planes, 7] * edge_in[comp, 0, 0]
        image_out[comp, 1] = image_out[comp, 1] - twice_left * coef[0, planes, pl.ds(8, 8)] * edge_in[comp, 0, pl.ds(1, 8)]
        image_out[comp, late[2]] = (image_out[comp, late[2]]
                                    - twice_right * coef[0, 2 * planes - 1, pl.ds(0, 8)] * edge_in[comp, 1, pl.ds(0, 8)])
        for tile in late:
            @pl.when(me != tile)
            def _():
                spread(image_out, image_in, image_send, image_recv, comp, tile)
        keep(image_out, image_in, comp)

    def spread_wait(target, send, recv, comp):
        most = target.at[comp, :, pl.ds(0, (groups - 1) * modes)]
        pltpu.make_async_copy(most, most, recv.at[comp]).wait()
        pltpu.make_async_copy(most, most, send.at[comp]).wait()

    for comp in range(comps):
        load_own[comp].wait()
        weigh(own.at[comp], planes)
        finish(near_copies[comp])
        weigh(near.at[0, comp], 0)
        weigh(near.at[1, comp], 2 * planes)
        for step in range(DEGREE):
            advance(step)
        finals(comp)
        if comp + 2 < comps:
            start(near_copies[comp + 2])
        spread_early(comp)
        if comp > 0:
            spread_late(comp - 1)

    def add_sums(sums, comp):
        spread_wait(filt_in, filt_send, filt_recv, comp)
        spread_wait(image_in, image_send, image_recv, comp)
        for row in range(0, 8, 2):
            filt = jnp.concatenate([filt_in[comp, row], filt_in[comp, row + 1]], axis=1)
            image = jnp.concatenate([image_in[comp, row], image_in[comp, row + 1]], axis=1)
            sums = sums + lax.dot_general(filt, jnp.concatenate([image, filt], axis=0), (((1,), (1,)), ((), ())),
                                          precision=HIGH, preferred_element_type=jnp.float32)
        return sums

    sums = jnp.zeros((every, 2 * every), jnp.float32)
    for comp in range(comps - 1):
        sums = add_sums(sums, comp)
    spread_late(comps - 1)
    part[...] = add_sums(sums, comps - 1)

    def exchange(phase, count, my_slot, source, target, own_tile, device):
        for step in range(1, count):
            to_blk, to_mode, slot = device(step)
            remote(source(slot), target.at[my_slot], sum_send.at[phase], sum_recv.at[phase], to_blk, to_mode).start()
        target[my_slot] = own_tile
        most = target.at[pl.ds(0, count - 1)]
        pltpu.make_async_copy(most, most, sum_recv.at[phase]).wait()
        pltpu.make_async_copy(most, most, sum_send.at[phase]).wait()

    def added(slots, count):
        result = slots[0]
        for slot in range(1, count):
            result = result + slots[slot]
        return result

    exchange(0, groups, me, lambda slot: part.at[pl.ds(pl.multiple_of(slot * 8, 8), 8)], part_in,
             part[pl.ds(pl.multiple_of(me * 8, 8), 8)], lambda step: (blk, mode_peer(step), mode_peer(step)))
    tile = added(part_in, groups)
    tile_y[...] = tile
    exchange(1, side, my_y, lambda slot: tile_y, in_y, tile, lambda step: (y_peer(step), me, 0))
    tile = added(in_y, side)
    tile_z[...] = tile
    exchange(2, side, my_z, lambda slot: tile_z, in_z, tile, lambda step: (z_peer(step), me, 0))
    tile = added(in_z, side)
    tile_all[...] = tile
    exchange(3, groups, me, lambda slot: tile_all, total, tile, lambda step: (blk, mode_peer(step), 0))

    sums = total[...].reshape((every, 2 * every))
    row_at = lax.broadcasted_iota(jnp.int32, (every, 2 * every), 0)
    lane_at = lax.broadcasted_iota(jnp.int32, (every, 2 * every), 1)
    cross = sums[:, :every]
    work = jnp.where(lane_at < every, jnp.where(lane_at == row_at, 1.0, 0.0), sums)
    blocks = [work[8 * j:8 * j + 8] for j in range(every // 8)]
    sub = lax.broadcasted_iota(jnp.int32, (8, 2 * every), 0)
    for k in range(every):
        j, r = divmod(k, 8)
        row = blocks[j][r:r + 1]
        row = row / row[:, every + k:every + k + 1]
        for i in range(j, every // 8):
            column = blocks[i][:, every + k:every + k + 1]
            change = column * row
            if i == j:
                change = jnp.where(sub > r, change, 0.0)
            blocks[i] = blocks[i] - change
    work = jnp.concatenate(blocks, axis=0)
    diagonal = jnp.sum(jnp.where(lane_at == row_at + every, work, 0.0), axis=1, keepdims=True)
    inverse = (work / jnp.sqrt(diagonal))[:, :every]

    def place():
        return lax.div(me, halves), pl.ds(pl.multiple_of(lax.rem(me, halves) * 8, 8), 8)

    def back_copies(comp):
        plane, rows = place()
        return [remote(back.at[comp, pl.ds(mode_peer(step) * modes, modes)], out_ref.at[:, comp, plane, rows],
                       back_send.at[comp], back_recv.at[comp], blk, mode_peer(step)) for step in range(1, groups)]

    def own_copy(comp):
        plane, rows = place()
        return pltpu.make_async_copy(back.at[comp, pl.ds(me * modes, modes)], out_ref.at[:, comp, plane, rows],
                                     back_send.at[comps + comp])

    for comp in range(comps):
        filt = jnp.concatenate([filt_in[comp, row] for row in range(8)], axis=1)
        result = jnp.dot(inverse, filt, precision=HIGH, preferred_element_type=jnp.float32)
        for row in range(8):
            back[comp, :, row] = result[:, row * nz:(row + 1) * nz]
        start(back_copies(comp))
        own_copy(comp).start()
    half = jnp.dot(inverse, cross, precision=HIGH, preferred_element_type=jnp.float32)
    product = lax.dot_general(half, inverse, (((1,), (1,)), ((), ())), precision=HIGH,
                              preferred_element_type=jnp.float32)
    proj_ref[...] = 0.5 * (product + product.T)
    for comp in range(comps):
        own_copy(comp).wait()
        most = back.at[comp, pl.ds(0, (groups - 1) * modes)]
        pltpu.make_async_copy(most, most, back_recv.at[comp]).wait()
        pltpu.make_async_copy(most, most, back_send.at[comp]).wait()


def shards(blks, groups, start_modes, materials, stiffness_table):
    modes, comps, planes, ny, nz = start_modes.shape
    every = modes * groups
    side = math.isqrt(blks)
    vmem, dma = pltpu.VMEM, pltpu.SemaphoreType.DMA
    f32 = jnp.float32
    slab = (modes, planes, ny, nz)
    edge = (comps, 2, 9, modes, nz)
    tiles_out = (comps, groups, 8, modes, nz)
    tiles_in = (comps, 8, every, nz)
    tile = (8, 2 * every)
    return pl.pallas_call(
        functools.partial(kernel, blks, groups),
        out_shape=(jax.ShapeDtypeStruct(start_modes.shape, f32), jax.ShapeDtypeStruct((every, every), f32)),
        in_specs=[pl.BlockSpec(memory_space=pl.ANY), pl.BlockSpec(memory_space=pl.ANY), pl.BlockSpec(memory_space=pltpu.SMEM)],
        out_specs=(pl.BlockSpec(memory_space=pl.ANY), pl.BlockSpec(memory_space=pltpu.VMEM)),
        scratch_shapes=[
            vmem((comps,) + slab, f32), vmem((2, comps) + slab, f32),
            vmem((planes, ny, nz), jnp.int32), vmem((planes, ny, nz), f32), vmem((2, planes, ny, nz), f32),
            vmem((3, 3 * planes, ny, modes, nz), f32), vmem((2, planes, ny, modes, nz), f32),
            vmem((2, 3 * planes, ny, modes, nz), f32),
            vmem(edge, f32), vmem(edge, f32),
            vmem(tiles_out, f32), vmem(tiles_out, f32),
            vmem(tiles_in, f32), vmem(tiles_in, f32),
            vmem((comps, every, 8, nz), f32),
            vmem((every, 2 * every), f32), vmem((groups,) + tile, f32),
            vmem(tile, f32), vmem((side,) + tile, f32),
            vmem(tile, f32), vmem((side,) + tile, f32),
            vmem(tile, f32), vmem((groups,) + tile, f32),
            dma((comps + 1,)), dma((2,)), dma((2,)),
            dma((2, comps)), dma((2, comps)), dma((comps, 2)), dma((comps, 2)),
            dma((comps,)), dma((comps,)), dma((comps,)), dma((comps,)),
            dma((2 * comps,)), dma((comps,)), dma((4,)), dma((4,)),
        ],
        compiler_params=pltpu.CompilerParams(
            collective_id=0, has_side_effects=True, vmem_limit_bytes=60 * 1024 * 1024),
    )(start_modes, materials, stiffness_table)


def solution(mesh):
    return jax.shard_map(
        functools.partial(shards, mesh.shape["blk"], mesh.shape["mode"]),
        mesh=mesh,
        in_specs=(P("mode", None, "blk", None, None), P("blk", None, None), P()),
        out_specs=(P("mode", None, "blk", None, None), P()),
        check_vma=False,
    )
```

```python
import functools
import math

import jax
import jax.numpy as jnp
from jax import lax
from jax.experimental import pallas as pl
from jax.experimental.pallas import tpu as pltpu
from jax.sharding import PartitionSpec as P

CENTER = 64.0
HALF_WIDTH = 56.0
MASS_SHIFT = 0.5
MESH = pl.DeviceIdType.MESH
HIGH = lax.Precision.HIGHEST
DEGREE = 4


def kernel(blks, groups, x_ref, mat_ref, tab_hbm, out_ref, proj_ref,
           tab_ref, own, mats, table, table_in, coef, close, field, odd, edge_out, edge_in,
           filt_out, image_out, filt_in, image_in,
           back, part, part_in, tile_y, in_y, tile_z, in_z, tile_all, total,
           load, table_send, table_recv, near_send, near_recv, edge_send, edge_recv,
           filt_send, filt_recv, image_send, image_recv,
           back_send, back_recv, sum_send, sum_recv):
    modes, comps, planes, ny, nz = x_ref.shape
    every = modes * groups
    halves = ny // 8
    side = math.isqrt(blks)
    blk, me = lax.axis_index("blk"), lax.axis_index("mode")
    left, right = lax.rem(blk + blks - 1, blks), lax.rem(blk + 1, blks)
    my_z, my_y = lax.div(blk, side), lax.rem(blk, side)
    no_left, no_right = blk == 0, blk == blks - 1

    def mode_peer(step):
        return lax.rem(me + step, groups)

    def y_peer(step):
        return my_z * side + lax.rem(my_y + step, side)

    def z_peer(step):
        return lax.rem(my_z + step, side) * side + my_y

    def tile_of(device):
        return lax.rem(device, 2) * 4 + lax.rem(lax.div(device, 2), 2) * 2 + lax.div(device, 4)

    my_tile = tile_of(me)

    def remote(src, dst, send, recv, to_blk, to_mode):
        return pltpu.make_async_remote_copy(
            src_ref=src, dst_ref=dst, send_sem=send, recv_sem=recv,
            device_id={"blk": to_blk, "mode": to_mode}, device_id_type=MESH)

    def arrived(ref, semaphore):
        pltpu.make_async_copy(ref, ref, semaphore).wait()

    owner_last, owner_first, owner_row = 3, 4, 0

    barrier = pltpu.get_barrier_semaphore()

    def greet(to_blk, to_mode):
        pl.semaphore_signal(barrier, inc=1, device_id={"blk": to_blk, "mode": to_mode}, device_id_type=MESH)

    greet(left, me)
    greet(right, me)
    for step in range(1, side):
        greet(y_peer(step), me)
        greet(z_peer(step), me)
    for step in range(1, groups):
        greet(blk, mode_peer(step))

    @pl.when(me == owner_last)
    def _():
        for mode in range(groups):
            greet(right, mode)

    @pl.when((me == owner_first) | (me == owner_row))
    def _():
        for mode in range(groups):
            greet(left, mode)

    load_mats = pltpu.make_async_copy(mat_ref, mats, load.at[comps])
    load_mats.start()
    load_tab = pltpu.make_async_copy(tab_hbm, tab_ref, load.at[comps + 1])
    load_tab.start()

    def load_own(comp):
        return pltpu.make_async_copy(x_ref.at[:, comp], own.at[comp], load.at[comp])

    for comp in range(comps):
        load_own(comp).start()

    def over(count, body, unroll=1):
        def run(at, carry):
            body(at)
            return carry
        lax.fori_loop(0, count, run, 0, unroll=unroll)

    @pl.when(no_left)
    def _():
        table_in[0] = jnp.zeros_like(table)

        def clear(plane):
            for comp in range(comps):
                field[comp, plane] = jnp.zeros((ny, modes, nz), jnp.float32)
        over(planes, clear)

    @pl.when(no_right)
    def _():
        table_in[1] = jnp.zeros_like(table)

        def clear(plane):
            for comp in range(comps):
                field[comp, 2 * planes + plane] = jnp.zeros((ny, modes, nz), jnp.float32)
        over(planes, clear)

    scale = 2.0 / HALF_WIDTH

    def all_modes(rows):
        return jnp.broadcast_to(rows[:, None, :], (ny, modes, nz))

    def coefficients(values, plane):
        coef[0, plane] = all_modes(scale * (27.0 * values + (MASS_SHIFT - CENTER)))
        coef[1, plane] = all_modes(scale * values)

    load_mats.wait()
    load_tab.wait()

    def own_root(plane):
        labels = mats[plane]
        values = jnp.zeros((ny, nz), jnp.float32)
        for label in range(tab_ref.shape[0]):
            values = jnp.where(labels == label, tab_ref[label], values)
        table[plane] = values
        close[0, plane] = all_modes(jnp.sqrt(values))

    over(planes, own_root)

    def weigh(comp):
        load_own(comp).wait()
        rows = own.at[comp].reshape(modes * planes * ny, nz)

        def body(plane):
            for y in range(ny):
                field[comp, planes + plane, y] = close[0, plane, y] * rows[pl.ds(plane * ny + y, modes, stride=planes * ny)]
        over(planes, body)

    weigh(0)
    pl.semaphore_wait(barrier, 5 + (groups - 1) + 2 * (side - 1))

    def table_copy(slot):
        return remote(table, table_in.at[slot], table_send.at[slot], table_recv.at[slot], (right, left)[slot], me)

    def near_copy(comp, slot):
        return remote(field.at[comp, pl.ds(planes, planes)], field.at[comp, pl.ds(2 * planes * slot, planes)],
                      near_send.at[slot, comp], near_recv.at[slot, comp], (right, left)[slot], me)

    def edge_copies(comp):
        mine = pl.ds(pl.multiple_of(me * modes, modes), modes)
        to_left = [remote(edge_out.at[comp, 1, pl.ds(0, 8)], edge_in.at[comp, :, mine],
                          edge_send.at[comp, 0], edge_recv.at[comp], left, owner_last)]
        to_right = [remote(edge_out.at[comp, 0, pl.ds(1, 8)], edge_in.at[comp, :, mine],
                           edge_send.at[comp, 1], edge_recv.at[comp], right, owner_first),
                    remote(edge_out.at[comp, 0, pl.ds(0, 1)], edge_in.at[comp, pl.ds(0, 1), mine],
                           edge_send.at[comp, 2], edge_recv.at[comp], right, owner_row)]
        return to_left, to_right

    @pl.when(jnp.logical_not(no_left))
    def _():
        table_copy(1).start()
        near_copy(0, 1).start()

    @pl.when(jnp.logical_not(no_right))
    def _():
        table_copy(0).start()
        near_copy(0, 0).start()

    for comp in range(1, comps):
        weigh(comp)

        @pl.when(jnp.logical_not(no_left))
        def _():
            near_copy(comp, 1).start()

        @pl.when(jnp.logical_not(no_right))
        def _():
            near_copy(comp, 0).start()

    def own_coefficients(plane):
        values = table[plane]
        coefficients(values, planes + plane)
        root = jnp.sqrt(values)
        close[1, plane] = all_modes(1.0 / root)
        close[2, plane] = all_modes((27.0 * values + MASS_SHIFT) / root)

    over(planes, own_coefficients)

    @pl.when(jnp.logical_not(no_left))
    def _():
        table_copy(0).wait_recv()
        table_copy(1).wait_send()

    @pl.when(jnp.logical_not(no_right))
    def _():
        table_copy(1).wait_recv()
        table_copy(0).wait_send()

    def near_coefficients(plane):
        coefficients(table_in[0, plane], plane)
        coefficients(table_in[1, plane], 2 * planes + plane)

    over(planes, near_coefficients)

    none = jnp.zeros((1, modes, nz), jnp.float32)

    def box_z(v):
        lanes = lax.broadcasted_iota(jnp.int32, v.shape, 2)
        before = jnp.where(lanes == 0, 0.0, pltpu.roll(v, 1, 2))
        after = jnp.where(lanes == nz - 1, 0.0, pltpu.roll(v, nz - 1, 2))
        return v + (before + after)

    def box(u):
        return box_z(u + (jnp.concatenate([none, u[:-1]], axis=0) + jnp.concatenate([u[1:], none], axis=0)))

    def advance(step, comp):
        even = field.at[comp]
        now, other = (even, odd) if step % 2 == 0 else (odd, even)
        first = step + 1

        def body(at):
            plane = first + at
            w = now[plane]
            u = now[plane - 1] + w + now[plane + 1]
            new = coef[0, plane] * w - coef[1, plane] * box(u)
            if step == 0:
                new = 0.5 * new
            else:
                new = new - other[plane]
            other[plane] = new
        over(3 * planes - 2 * first, body, 2)

    def finals(comp):
        first, last = field[comp, planes, :9], field[comp, 2 * planes - 1, 8:]
        edge_out[comp, 1, :8] = box_z(first[:8] + (first[1:] + jnp.concatenate([none, first[:7]], axis=0)))
        edge_out[comp, 0] = box_z(jnp.concatenate([none, last], axis=0) + (
            jnp.concatenate([last, none], axis=0) + jnp.concatenate([none, none, last[:-1]], axis=0)))
        to_left, to_right = edge_copies(comp)

        @pl.when(jnp.logical_not(no_left))
        def _():
            for copy in to_left:
                copy.start()

        @pl.when(jnp.logical_not(no_right))
        def _():
            for copy in to_right:
                copy.start()

        field[comp, planes - 1] = jnp.zeros((ny, modes, nz), jnp.float32)
        field[comp, 2 * planes] = jnp.zeros((ny, modes, nz), jnp.float32)

        def body(plane):
            at = planes + plane
            w = field[comp, at]
            filt = w * close[1, plane]
            image = close[2, plane] * w - close[0, plane] * box(field[comp, at - 1] + w + field[comp, at + 1])
            for half in range(halves):
                filt_out[comp, plane * halves + half] = filt[8 * half:8 * half + 8]
                image_out[comp, plane * halves + half] = image[8 * half:8 * half + 8]
        over(planes, body, 2)

    def my_modes():
        return pl.ds(pl.multiple_of(me * modes, modes), modes)

    def spread(source, target, send, recv, comp):
        for step in range(1, groups):
            peer = mode_peer(step)
            remote(source.at[comp, tile_of(peer)], target.at[comp, :, my_modes()],
                   send.at[comp], recv.at[comp], blk, peer).start()

    def spread_wait(target, send, recv, comp):
        most = target.at[comp, :, pl.ds(0, (groups - 1) * modes)]
        arrived(most, recv.at[comp])
        arrived(most, send.at[comp])

    def filter_one(comp):
        @pl.when(jnp.logical_not(no_left))
        def _():
            near_copy(comp, 0).wait_recv()
            near_copy(comp, 1).wait_send()

        @pl.when(jnp.logical_not(no_right))
        def _():
            near_copy(comp, 1).wait_recv()
            near_copy(comp, 0).wait_send()

        for step in range(DEGREE):
            advance(step, comp)
        finals(comp)
        spread(filt_out, filt_in, filt_send, filt_recv, comp)
        spread(image_out, image_in, image_send, image_recv, comp)
        filt_in[comp, :, my_modes()] = filt_out[comp, my_tile]
        image_in[comp, :, my_modes()] = image_out[comp, my_tile]

    over(comps, filter_one)

    def add_edges(comp):
        @pl.when((me == owner_last) & jnp.logical_not(no_right))
        def _():
            arrived(edge_in.at[comp], edge_recv.at[comp])
            for group in range(groups):
                at = pl.ds(group * modes, modes)
                image_in[comp, :, at] = image_in[comp, :, at] - (2.0 * close[0, planes - 1, :8]) * edge_in[comp, :, at]

        @pl.when((me == owner_first) & jnp.logical_not(no_left))
        def _():
            arrived(edge_in.at[comp], edge_recv.at[comp])
            for group in range(groups):
                at = pl.ds(group * modes, modes)
                image_in[comp, :, at] = image_in[comp, :, at] - (2.0 * close[0, 0, 8:]) * edge_in[comp, :, at]

        @pl.when((me == owner_row) & jnp.logical_not(no_left))
        def _():
            arrived(edge_in.at[comp, pl.ds(0, 1)], edge_recv.at[comp])
            for group in range(groups):
                at = pl.ds(group * modes, modes)
                image_in[comp, 7, at] = image_in[comp, 7, at] - (2.0 * close[0, 0, 7]) * edge_in[comp, 0, at]

    part[...] = jnp.zeros_like(part)

    def add_sums(comp):
        spread_wait(filt_in, filt_send, filt_recv, comp)
        spread_wait(image_in, image_send, image_recv, comp)
        add_edges(comp)
        sums = part[...]
        for row in range(0, 8, 2):
            filt = jnp.concatenate([filt_in[comp, row], filt_in[comp, row + 1]], axis=1)
            image = jnp.concatenate([image_in[comp, row], image_in[comp, row + 1]], axis=1)
            sums = sums + lax.dot_general(filt, jnp.concatenate([image, filt], axis=0), (((1,), (1,)), ((), ())),
                                          precision=HIGH, preferred_element_type=jnp.float32)
        part[...] = sums

    over(comps, add_sums)

    def exchange(phase, count, my_slot, source, target, own_tile, device):
        for step in range(1, count):
            to_blk, to_mode, slot = device(step)
            remote(source(slot), target.at[my_slot], sum_send.at[phase], sum_recv.at[phase], to_blk, to_mode).start()
        target[my_slot] = own_tile
        most = target.at[pl.ds(0, count - 1)]
        arrived(most, sum_recv.at[phase])
        arrived(most, sum_send.at[phase])

    def added(slots, count):
        result = slots[0]
        for slot in range(1, count):
            result = result + slots[slot]
        return result

    exchange(0, groups, me, lambda slot: part.at[pl.ds(pl.multiple_of(slot * 8, 8), 8)], part_in,
             part[pl.ds(pl.multiple_of(me * 8, 8), 8)], lambda step: (blk, mode_peer(step), mode_peer(step)))
    tile = added(part_in, groups)
    tile_y[...] = tile
    exchange(1, side, my_y, lambda slot: tile_y, in_y, tile, lambda step: (y_peer(step), me, 0))
    tile = added(in_y, side)
    tile_z[...] = tile
    exchange(2, side, my_z, lambda slot: tile_z, in_z, tile, lambda step: (z_peer(step), me, 0))
    tile = added(in_z, side)
    tile_all[...] = tile
    exchange(3, groups, me, lambda slot: tile_all, total, tile, lambda step: (blk, mode_peer(step), 0))

    sums = total[...].reshape((every, 2 * every))
    row_at = lax.broadcasted_iota(jnp.int32, (every, 2 * every), 0)
    lane_at = lax.broadcasted_iota(jnp.int32, (every, 2 * every), 1)
    cross = sums[:, :every]
    work = jnp.where(lane_at < every, jnp.where(lane_at == row_at, 1.0, 0.0), sums)
    blocks = [work[8 * j:8 * j + 8] for j in range(every // 8)]
    sub = lax.broadcasted_iota(jnp.int32, (8, 2 * every), 0)

    def column(block, lane):
        return jnp.take_along_axis(block, jnp.full((8, 2 * every), lane, jnp.int32), axis=1)

    def spread_row(block, row):
        return jnp.broadcast_to(block[row:row + 1], (8, 2 * every))

    for k in range(0, every, 2):
        j, r = divmod(k, 8)
        ones = [column(block, every + k) for block in blocks[j:]]
        twos = [column(block, every + k + 1) for block in blocks[j:]]
        row_one, row_two = spread_row(blocks[j], r), spread_row(blocks[j], r + 1)
        mixed = spread_row(ones[0], r + 1)
        over_one = 1.0 / spread_row(ones[0], r)
        factor = mixed * over_one
        over_two = 1.0 / (spread_row(twos[0], r + 1) - factor * mixed)
        new_two = row_two - factor * row_one
        scaled_one, scaled_two = row_one * over_one, new_two * over_two
        for i in range(j, every // 8):
            one, two = ones[i - j], twos[i - j]
            less = blocks[i] - (one * scaled_one + (two - one * factor) * scaled_two)
            if i == j:
                less = jnp.where(sub > r + 1, less, jnp.where(sub == r + 1, new_two, blocks[i]))
            blocks[i] = less
    work = jnp.concatenate(blocks, axis=0)
    diagonal = jnp.sum(jnp.where(lane_at == row_at + every, work, 0.0), axis=1, keepdims=True)
    inverse = (work / jnp.sqrt(diagonal))[:, :every]

    def place():
        return lax.div(my_tile, halves), pl.ds(pl.multiple_of(lax.rem(my_tile, halves) * 8, 8), 8)

    def back_copies(comp):
        plane, rows = place()
        return [remote(back.at[comp, pl.ds(mode_peer(step) * modes, modes)], out_ref.at[:, comp, plane, rows],
                       back_send.at[comp], back_recv.at[comp], blk, mode_peer(step)) for step in range(1, groups)]

    def own_copy(comp):
        plane, rows = place()
        return pltpu.make_async_copy(back.at[comp, pl.ds(me * modes, modes)], out_ref.at[:, comp, plane, rows],
                                     back_send.at[comps + comp])

    def give_back(comp):
        filt = jnp.concatenate([filt_in[comp, row] for row in range(8)], axis=1)
        result = jnp.dot(inverse, filt, precision=HIGH, preferred_element_type=jnp.float32)
        for row in range(8):
            back[comp, :, row] = result[:, row * nz:(row + 1) * nz]
        for copy in back_copies(comp):
            copy.start()
        own_copy(comp).start()

    for comp in range(comps):
        give_back(comp)
    half = jnp.dot(inverse, cross, precision=HIGH, preferred_element_type=jnp.float32)
    product = lax.dot_general(half, inverse, (((1,), (1,)), ((), ())), precision=HIGH,
                              preferred_element_type=jnp.float32)
    proj_ref[...] = 0.5 * (product + product.T)

    def finish(comp):
        to_left, to_right = edge_copies(comp)

        @pl.when(jnp.logical_not(no_left))
        def _():
            for copy in to_left:
                copy.wait_send()

        @pl.when(jnp.logical_not(no_right))
        def _():
            for copy in to_right:
                copy.wait_send()

        own_copy(comp).wait()
        most = back.at[comp, pl.ds(0, (groups - 1) * modes)]
        arrived(most, back_recv.at[comp])
        arrived(most, back_send.at[comp])

    over(comps, finish)


def shards(blks, groups, start_modes, materials, stiffness_table):
    modes, comps, planes, ny, nz = start_modes.shape
    every = modes * groups
    side = math.isqrt(blks)
    vmem, dma = pltpu.VMEM, pltpu.SemaphoreType.DMA
    f32 = jnp.float32
    plane = (ny, modes, nz)
    tiles_out = (comps, groups, 8, modes, nz)
    tiles_in = (comps, 8, every, nz)
    tile = (8, 2 * every)
    return pl.pallas_call(
        functools.partial(kernel, blks, groups),
        out_shape=(jax.ShapeDtypeStruct(start_modes.shape, f32), jax.ShapeDtypeStruct((every, every), f32)),
        in_specs=[pl.BlockSpec(memory_space=pltpu.HBM), pl.BlockSpec(memory_space=pltpu.HBM),
                  pl.BlockSpec(memory_space=pltpu.HBM)],
        out_specs=(pl.BlockSpec(memory_space=pl.ANY), pl.BlockSpec(memory_space=pltpu.VMEM)),
        scratch_shapes=[
            pltpu.SMEM(stiffness_table.shape, f32),
            vmem((comps, modes, planes, ny, nz), f32),
            vmem((planes, ny, nz), jnp.int32), vmem((planes, ny, nz), f32), vmem((2, planes, ny, nz), f32),
            vmem((2, 3 * planes) + plane, f32), vmem((3, planes) + plane, f32),
            vmem((comps, 3 * planes) + plane, f32), vmem((3 * planes,) + plane, f32),
            vmem((comps, 2, 9, modes, nz), f32), vmem(tiles_in, f32),
            vmem(tiles_out, f32), vmem(tiles_out, f32),
            vmem(tiles_in, f32), vmem(tiles_in, f32),
            vmem((comps, every, 8, nz), f32),
            vmem((every, 2 * every), f32), vmem((groups,) + tile, f32),
            vmem(tile, f32), vmem((side,) + tile, f32),
            vmem(tile, f32), vmem((side,) + tile, f32),
            vmem(tile, f32), vmem((groups,) + tile, f32),
            dma((comps + 2,)), dma((2,)), dma((2,)),
            dma((2, comps)), dma((2, comps)), dma((comps, 3)), dma((comps,)),
            dma((comps,)), dma((comps,)), dma((comps,)), dma((comps,)),
            dma((2 * comps,)), dma((comps,)), dma((4,)), dma((4,)),
        ],
        compiler_params=pltpu.CompilerParams(
            collective_id=0, has_side_effects=True, vmem_limit_bytes=48 * 1024 * 1024),
    )(pltpu.with_memory_space_constraint(start_modes, pltpu.HBM),
      pltpu.with_memory_space_constraint(materials, pltpu.HBM),
      pltpu.with_memory_space_constraint(stiffness_table, pltpu.HBM))


def solution(mesh):
    return jax.shard_map(
        functools.partial(shards, mesh.shape["blk"], mesh.shape["mode"]),
        mesh=mesh,
        in_specs=(P("mode", None, "blk", None, None), P("blk", None, None), P()),
        out_specs=(P("mode", None, "blk", None, None), P()),
        check_vma=False,
    )
```

```python
import functools
import math

import jax
import jax.numpy as jnp
from jax import lax
from jax.experimental import pallas as pl
from jax.experimental.pallas import tpu as pltpu
from jax.sharding import PartitionSpec as P

CENTER = 64.0
HALF_WIDTH = 56.0
MASS_SHIFT = 0.5
MESH = pl.DeviceIdType.MESH
HIGH = lax.Precision.HIGHEST
DEGREE = 4


def kernel(blks, groups, x_ref, mat_ref, tab_hbm, out_ref, proj_ref,
           tab_ref, own, mats, table, table_in, coef, close, field, odd, edge_out, edge_in,
           filt_out, image_out, filt_in, image_in, again_in, again, inverse_ref,
           back, part, part_in, tile_y, in_y, tile_z, in_z, tile_all, total,
           load, table_send, table_recv, near_send, near_recv, edge_send, edge_recv,
           filt_send, filt_recv, image_send, image_recv,
           back_send, back_recv, own_send, again_send, again_recv, sum_send, sum_recv):
    modes, comps, planes, ny, nz = x_ref.shape
    every = modes * groups
    halves = ny // 8
    side = math.isqrt(blks)
    blk, me = lax.axis_index("blk"), lax.axis_index("mode")
    left, right = lax.rem(blk + blks - 1, blks), lax.rem(blk + 1, blks)
    my_z, my_y = lax.div(blk, side), lax.rem(blk, side)
    no_left, no_right = blk == 0, blk == blks - 1

    def mode_peer(step):
        return lax.rem(me + step, groups)

    def y_peer(step):
        return my_z * side + lax.rem(my_y + step, side)

    def z_peer(step):
        return lax.rem(my_z + step, side) * side + my_y

    def tile_of(device):
        return lax.rem(device, 2) * 4 + lax.rem(lax.div(device, 2), 2) * 2 + lax.div(device, 4)

    my_tile = tile_of(me)

    def far_first(count):
        return sorted(range(1, count), key=lambda step: abs(2 * step - count))

    def remote(src, dst, send, recv, to_blk, to_mode):
        return pltpu.make_async_remote_copy(
            src_ref=src, dst_ref=dst, send_sem=send, recv_sem=recv,
            device_id={"blk": to_blk, "mode": to_mode}, device_id_type=MESH)

    def arrived(ref, semaphore):
        pltpu.make_async_copy(ref, ref, semaphore).wait()

    owner_last, owner_first, owner_row = 3, 4, 0

    load_mats = pltpu.make_async_copy(mat_ref, mats, load.at[comps])
    load_mats.start()
    load_tab = pltpu.make_async_copy(tab_hbm, tab_ref, load.at[comps + 1])
    load_tab.start()

    def load_own(comp):
        return pltpu.make_async_copy(x_ref.at[:, comp], own.at[comp], load.at[comp])

    for comp in range(comps):
        load_own(comp).start()

    barrier = pltpu.get_barrier_semaphore()

    def greet(to_blk, to_mode):
        pl.semaphore_signal(barrier, inc=1, device_id={"blk": to_blk, "mode": to_mode}, device_id_type=MESH)

    greet(left, me)
    greet(right, me)
    for step in range(1, side):
        greet(y_peer(step), me)
        greet(z_peer(step), me)
    for step in range(1, groups):
        greet(blk, mode_peer(step))

    @pl.when(me == owner_last)
    def _():
        for mode in range(groups):
            greet(right, mode)

    @pl.when((me == owner_first) | (me == owner_row))
    def _():
        for mode in range(groups):
            greet(left, mode)

    def over(count, body, unroll=1):
        def run(at, carry):
            body(at)
            return carry
        lax.fori_loop(0, count, run, 0, unroll=unroll)

    @pl.when(no_left)
    def _():
        table_in[0] = jnp.zeros_like(table)

        def clear(plane):
            for comp in range(comps):
                field[comp, plane] = jnp.zeros((ny, modes, nz), jnp.float32)
        over(planes, clear)

    @pl.when(no_right)
    def _():
        table_in[1] = jnp.zeros_like(table)

        def clear(plane):
            for comp in range(comps):
                field[comp, 2 * planes + plane] = jnp.zeros((ny, modes, nz), jnp.float32)
        over(planes, clear)

    scale = 2.0 / HALF_WIDTH

    def all_modes(rows):
        return jnp.broadcast_to(rows[:, None, :], (ny, modes, nz))

    def coefficients(values, plane):
        coef[0, plane] = all_modes(scale * (27.0 * values + (MASS_SHIFT - CENTER)))
        coef[1, plane] = all_modes(scale * values)

    load_mats.wait()
    load_tab.wait()

    def own_root(plane):
        labels = mats[plane]
        values = jnp.zeros((ny, nz), jnp.float32)
        for label in range(tab_ref.shape[0]):
            values = jnp.where(labels == label, tab_ref[label], values)
        table[plane] = values
        close[0, plane] = all_modes(jnp.sqrt(values))

    over(planes, own_root, planes)

    def weigh(comp):
        load_own(comp).wait()
        rows = own.at[comp].reshape(modes * planes * ny, nz)

        def body(plane):
            for y in range(ny):
                field[comp, planes + plane, y] = close[0, plane, y] * rows[pl.ds(plane * ny + y, modes, stride=planes * ny)]
        over(planes, body, 2)

    weigh(0)
    pl.semaphore_wait(barrier, 5 + (groups - 1) + 2 * (side - 1))

    def table_copy(slot):
        return remote(table, table_in.at[slot], table_send.at[slot], table_recv.at[slot], (right, left)[slot], me)

    def near_copy(comp, slot):
        return remote(field.at[comp, pl.ds(planes, planes)], field.at[comp, pl.ds(2 * planes * slot, planes)],
                      near_send.at[slot, comp], near_recv.at[slot, comp], (right, left)[slot], me)

    def edge_copies(comp):
        mine = pl.ds(pl.multiple_of(me * modes, modes), modes)
        to_left = [remote(edge_out.at[comp, 1, pl.ds(0, 8)], edge_in.at[comp, :, mine],
                          edge_send.at[comp, 0], edge_recv.at[comp], left, owner_last)]
        to_right = [remote(edge_out.at[comp, 0, pl.ds(1, 8)], edge_in.at[comp, :, mine],
                           edge_send.at[comp, 1], edge_recv.at[comp], right, owner_first),
                    remote(edge_out.at[comp, 0, pl.ds(0, 1)], edge_in.at[comp, pl.ds(0, 1), mine],
                           edge_send.at[comp, 2], edge_recv.at[comp], right, owner_row)]
        return to_left, to_right

    @pl.when(jnp.logical_not(no_left))
    def _():
        table_copy(1).start()
        near_copy(0, 1).start()

    @pl.when(jnp.logical_not(no_right))
    def _():
        table_copy(0).start()
        near_copy(0, 0).start()

    for comp in range(1, comps):
        weigh(comp)

        @pl.when(jnp.logical_not(no_left))
        def _():
            near_copy(comp, 1).start()

        @pl.when(jnp.logical_not(no_right))
        def _():
            near_copy(comp, 0).start()

    def own_coefficients(plane):
        values = table[plane]
        coefficients(values, planes + plane)
        root = jnp.sqrt(values)
        close[1, plane] = all_modes(1.0 / root)
        close[2, plane] = all_modes((27.0 * values + MASS_SHIFT) / root)

    over(planes, own_coefficients)

    @pl.when(jnp.logical_not(no_left))
    def _():
        table_copy(0).wait_recv()
        table_copy(1).wait_send()

    @pl.when(jnp.logical_not(no_right))
    def _():
        table_copy(1).wait_recv()
        table_copy(0).wait_send()

    def near_coefficients(plane):
        coefficients(table_in[0, plane], plane)
        coefficients(table_in[1, plane], 2 * planes + plane)

    over(planes, near_coefficients)

    none = jnp.zeros((1, modes, nz), jnp.float32)

    def box_z(v):
        lanes = lax.broadcasted_iota(jnp.int32, v.shape, 2)
        before = jnp.where(lanes == 0, 0.0, pltpu.roll(v, 1, 2))
        after = jnp.where(lanes == nz - 1, 0.0, pltpu.roll(v, nz - 1, 2))
        return v + (before + after)

    def box(u):
        return box_z(u + (jnp.concatenate([none, u[:-1]], axis=0) + jnp.concatenate([u[1:], none], axis=0)))

    def advance(step, comp):
        even = field.at[comp]
        now, other = (even, odd) if step % 2 == 0 else (odd, even)
        first = step + 1

        def body(at):
            plane = first + at
            w = now[plane]
            u = now[plane - 1] + w + now[plane + 1]
            new = coef[0, plane] * w - coef[1, plane] * box(u)
            if step == 0:
                new = 0.5 * new
            else:
                new = new - other[plane]
            other[plane] = new
        over(3 * planes - 2 * first, body, 2)

    def finals(comp):
        first, last = field[comp, planes, :9], field[comp, 2 * planes - 1, 8:]
        edge_out[comp, 1, :8] = box_z(first[:8] + (first[1:] + jnp.concatenate([none, first[:7]], axis=0)))
        edge_out[comp, 0] = box_z(jnp.concatenate([none, last], axis=0) + (
            jnp.concatenate([last, none], axis=0) + jnp.concatenate([none, none, last[:-1]], axis=0)))
        to_left, to_right = edge_copies(comp)

        @pl.when(jnp.logical_not(no_left))
        def _():
            for copy in to_left:
                copy.start()

        @pl.when(jnp.logical_not(no_right))
        def _():
            for copy in to_right:
                copy.start()

        field[comp, planes - 1] = jnp.zeros((ny, modes, nz), jnp.float32)
        field[comp, 2 * planes] = jnp.zeros((ny, modes, nz), jnp.float32)

        def body(plane):
            at = planes + plane
            w = field[comp, at]
            filt = w * close[1, plane]
            image = close[2, plane] * w - close[0, plane] * box(field[comp, at - 1] + w + field[comp, at + 1])
            for half in range(halves):
                filt_out[comp, plane * halves + half] = filt[8 * half:8 * half + 8]
                image_out[comp, plane * halves + half] = image[8 * half:8 * half + 8]
        over(planes, body, 2)

    def my_modes():
        return pl.ds(pl.multiple_of(me * modes, modes), modes)

    def spread(source, target, send, recv, comp):
        for step in range(1, groups):
            peer = mode_peer(step)
            remote(source.at[comp, tile_of(peer)], target.at[comp, :, my_modes()],
                   send.at[comp], recv.at[comp], blk, peer).start()

    def spread_wait(target, send, recv, comp):
        most = target.at[comp, :, pl.ds(0, (groups - 1) * modes)]
        arrived(most, recv.at[comp])
        arrived(most, send.at[comp])

    def filter_one(comp):
        @pl.when(jnp.logical_not(no_left))
        def _():
            near_copy(comp, 0).wait_recv()
            near_copy(comp, 1).wait_send()

        @pl.when(jnp.logical_not(no_right))
        def _():
            near_copy(comp, 1).wait_recv()
            near_copy(comp, 0).wait_send()

        for step in range(DEGREE):
            advance(step, comp)
        finals(comp)
        spread(filt_out, filt_in, filt_send, filt_recv, comp)
        spread(image_out, image_in, image_send, image_recv, comp)
        filt_in[comp, :, my_modes()] = filt_out[comp, my_tile]
        image_in[comp, :, my_modes()] = image_out[comp, my_tile]

    over(comps, filter_one)

    def add_edges(comp):
        @pl.when((me == owner_last) & jnp.logical_not(no_right))
        def _():
            arrived(edge_in.at[comp], edge_recv.at[comp])
            for group in range(groups):
                at = pl.ds(group * modes, modes)
                image_in[comp, :, at] = image_in[comp, :, at] - (2.0 * close[0, planes - 1, :8]) * edge_in[comp, :, at]

        @pl.when((me == owner_first) & jnp.logical_not(no_left))
        def _():
            arrived(edge_in.at[comp], edge_recv.at[comp])
            for group in range(groups):
                at = pl.ds(group * modes, modes)
                image_in[comp, :, at] = image_in[comp, :, at] - (2.0 * close[0, 0, 8:]) * edge_in[comp, :, at]

        @pl.when((me == owner_row) & jnp.logical_not(no_left))
        def _():
            arrived(edge_in.at[comp, pl.ds(0, 1)], edge_recv.at[comp])
            for group in range(groups):
                at = pl.ds(group * modes, modes)
                image_in[comp, 7, at] = image_in[comp, 7, at] - (2.0 * close[0, 0, 7]) * edge_in[comp, 0, at]

    part[...] = jnp.zeros_like(part)

    def add_sums(comp):
        spread_wait(filt_in, filt_send, filt_recv, comp)
        spread_wait(image_in, image_send, image_recv, comp)
        add_edges(comp)
        sums = part[...]
        for row in range(0, 8, 2):
            filt = jnp.concatenate([filt_in[comp, row], filt_in[comp, row + 1]], axis=1)
            image = jnp.concatenate([image_in[comp, row], image_in[comp, row + 1]], axis=1)
            sums = sums + lax.dot_general(filt, jnp.concatenate([image, filt], axis=0), (((1,), (1,)), ((), ())),
                                          precision=HIGH, preferred_element_type=jnp.float32)
        part[...] = sums

    over(comps, add_sums)

    opposite = mode_peer(groups // 2)
    core = lax.rem(me, 2)
    sibling = me + 1 - 2 * core

    def spread_again():
        def body(comp):
            for step in far_first(groups):
                peer = mode_peer(step)
                remote(filt_out.at[comp, tile_of(mode_peer(step + groups // 2))], again_in.at[comp, :, my_modes()],
                       again_send.at[comp], again_recv.at[comp], blk, peer).start()
            again_in[comp, :, my_modes()] = filt_out[comp, tile_of(opposite)]
        over(comps, body)

    def exchange(phase, count, my_slot, source, target, own_tile, device, meanwhile=None):
        for step in far_first(count):
            to_blk, to_mode, slot = device(step)
            remote(source(slot), target.at[my_slot], sum_send.at[phase], sum_recv.at[phase], to_blk, to_mode).start()
        target[my_slot] = own_tile
        if meanwhile is not None:
            meanwhile()
        arrived(target.at[pl.ds(0, count - 1)], sum_recv.at[phase])

    def added(slots, count):
        result = slots[0]
        for slot in range(1, count):
            result = result + slots[slot]
        return result

    exchange(0, groups, me, lambda slot: part.at[pl.ds(pl.multiple_of(slot * 8, 8), 8)], part_in,
             part[pl.ds(pl.multiple_of(me * 8, 8), 8)], lambda step: (blk, mode_peer(step), mode_peer(step)), spread_again)
    tile = added(part_in, groups)
    tile_y[...] = tile
    exchange(1, side, my_y, lambda slot: tile_y, in_y, tile, lambda step: (y_peer(step), me, 0))
    tile = added(in_y, side)
    tile_z[...] = tile
    exchange(2, side, my_z, lambda slot: tile_z, in_z, tile, lambda step: (z_peer(step), me, 0))
    tile = added(in_z, side)
    tile_all[...] = tile
    exchange(3, groups, me, lambda slot: tile_all, total, tile, lambda step: (blk, mode_peer(step), 0))

    sums = total[...].reshape((every, 2 * every))
    row_at = lax.broadcasted_iota(jnp.int32, (every, 2 * every), 0)
    lane_at = lax.broadcasted_iota(jnp.int32, (every, 2 * every), 1)
    cross = sums[:, :every]
    work = jnp.where(lane_at < every, jnp.where(lane_at == row_at, 1.0, 0.0), sums)
    blocks = [work[8 * j:8 * j + 8] for j in range(every // 8)]
    sub = lax.broadcasted_iota(jnp.int32, (8, 2 * every), 0)

    def column(block, lane):
        return jnp.take_along_axis(block, jnp.full((8, 2 * every), lane, jnp.int32), axis=1)

    def spread_row(block, row):
        return jnp.broadcast_to(block[row:row + 1], (8, 2 * every))

    for k in range(0, every, 2):
        j, r = divmod(k, 8)
        ones = [column(block, every + k) for block in blocks[j:]]
        twos = [column(block, every + k + 1) for block in blocks[j:]]
        row_one, row_two = spread_row(blocks[j], r), spread_row(blocks[j], r + 1)
        mixed = spread_row(ones[0], r + 1)
        over_one = 1.0 / spread_row(ones[0], r)
        factor = mixed * over_one
        over_two = 1.0 / (spread_row(twos[0], r + 1) - factor * mixed)
        new_two = row_two - factor * row_one
        scaled_one, scaled_two = row_one * over_one, new_two * over_two
        for i in range(j, every // 8):
            one, two = ones[i - j], twos[i - j]
            less = blocks[i] - (one * scaled_one + (two - one * factor) * scaled_two)
            if i == j:
                less = jnp.where(sub > r + 1, less, jnp.where(sub == r + 1, new_two, blocks[i]))
            blocks[i] = less
    work = jnp.concatenate(blocks, axis=0)
    diagonal = jnp.sum(jnp.where(lane_at == row_at + every, work, 0.0), axis=1, keepdims=True)
    inverse = (work / jnp.sqrt(diagonal))[:, :every]
    inverse_ref[...] = inverse

    def place(tile):
        return lax.div(tile, halves), pl.ds(pl.multiple_of(lax.rem(tile, halves) * 8, 8), 8)

    def back_copies(comp):
        plane, rows = place(my_tile)
        copies = []
        for step in far_first(groups):
            peer = mode_peer(step)
            copies.append((peer, remote(back.at[comp, pl.ds(peer * modes, modes)], out_ref.at[:, comp, plane, rows],
                                        back_send.at[comp], back_recv.at[comp], blk, peer)))
        return copies

    def own_copies(comp):
        plane, rows = place(my_tile)
        other_plane, other_rows = place(tile_of(opposite))
        return (pltpu.make_async_copy(back.at[comp, pl.ds(me * modes, modes)], out_ref.at[:, comp, plane, rows],
                                      own_send.at[0, comp]),
                pltpu.make_async_copy(again.at[comp, pl.ds(core * modes, modes)], out_ref.at[:, comp, other_plane, other_rows],
                                      own_send.at[1, comp]))

    def sibling_copy(comp):
        plane, rows = place(tile_of(opposite))
        return remote(again.at[comp, pl.ds((1 - core) * modes, modes)], out_ref.at[:, comp, plane, rows],
                      back_send.at[comp], back_recv.at[comp], blk, sibling)

    def give_back(comp):
        filt = jnp.concatenate([filt_in[comp, row] for row in range(8)], axis=1)
        result = jnp.dot(inverse, filt, precision=HIGH, preferred_element_type=jnp.float32)
        for row in range(8):
            back[comp, :, row] = result[:, row * nz:(row + 1) * nz]
        for peer, copy in back_copies(comp):
            @pl.when(lax.div(peer, 2) != lax.div(opposite, 2))
            def _():
                copy.start()
        own_copies(comp)[0].start()

    def give_sibling(comp):
        arrived(again_in.at[comp, :, pl.ds(0, (groups - 1) * modes)], again_recv.at[comp])
        arrived(again_in.at[comp, :, pl.ds(0, (groups - 1) * modes)], again_send.at[comp])
        filt = jnp.concatenate([again_in[comp, row] for row in range(8)], axis=1)
        mine = inverse_ref[pl.ds(pl.multiple_of((me - core) * modes, 2 * modes), 2 * modes), :]
        result = jnp.dot(mine, filt, precision=HIGH, preferred_element_type=jnp.float32)
        for row in range(8):
            again[comp, :, row] = result[:, row * nz:(row + 1) * nz]
        sibling_copy(comp).start()
        own_copies(comp)[1].start()

    for comp in range(comps):
        give_back(comp)
    for comp in range(comps):
        give_sibling(comp)
    half = jnp.dot(inverse, cross, precision=HIGH, preferred_element_type=jnp.float32)
    product = lax.dot_general(half, inverse, (((1,), (1,)), ((), ())), precision=HIGH,
                              preferred_element_type=jnp.float32)
    proj_ref[...] = 0.5 * (product + product.T)

    def finish(comp):
        to_left, to_right = edge_copies(comp)

        @pl.when(jnp.logical_not(no_left))
        def _():
            for copy in to_left:
                copy.wait_send()

        @pl.when(jnp.logical_not(no_right))
        def _():
            for copy in to_right:
                copy.wait_send()

        for copy in own_copies(comp):
            copy.wait()
        most = back.at[comp, pl.ds(0, (groups - 2) * modes)]
        arrived(most, back_recv.at[comp])
        arrived(most, back_send.at[comp])

    over(comps, finish)
    for phase, target, count in ((0, part_in, groups), (1, in_y, side), (2, in_z, side), (3, total, groups)):
        arrived(target.at[pl.ds(0, count - 1)], sum_send.at[phase])


def shards(blks, groups, start_modes, materials, stiffness_table):
    modes, comps, planes, ny, nz = start_modes.shape
    every = modes * groups
    side = math.isqrt(blks)
    vmem, dma = pltpu.VMEM, pltpu.SemaphoreType.DMA
    f32 = jnp.float32
    plane = (ny, modes, nz)
    tiles_out = (comps, groups, 8, modes, nz)
    tiles_in = (comps, 8, every, nz)
    tile = (8, 2 * every)
    return pl.pallas_call(
        functools.partial(kernel, blks, groups),
        out_shape=(jax.ShapeDtypeStruct(start_modes.shape, f32), jax.ShapeDtypeStruct((every, every), f32)),
        in_specs=[pl.BlockSpec(memory_space=pltpu.HBM), pl.BlockSpec(memory_space=pltpu.HBM),
                  pl.BlockSpec(memory_space=pltpu.HBM)],
        out_specs=(pl.BlockSpec(memory_space=pl.ANY), pl.BlockSpec(memory_space=pltpu.VMEM)),
        scratch_shapes=[
            pltpu.SMEM(stiffness_table.shape, f32),
            vmem((comps, modes, planes, ny, nz), f32),
            vmem((planes, ny, nz), jnp.int32), vmem((planes, ny, nz), f32), vmem((2, planes, ny, nz), f32),
            vmem((2, 3 * planes) + plane, f32), vmem((3, planes) + plane, f32),
            vmem((comps, 3 * planes) + plane, f32), vmem((3 * planes,) + plane, f32),
            vmem((comps, 2, 9, modes, nz), f32), vmem(tiles_in, f32),
            vmem(tiles_out, f32), vmem(tiles_out, f32),
            vmem(tiles_in, f32), vmem(tiles_in, f32),
            vmem(tiles_in, f32), vmem((comps, 2 * modes, 8, nz), f32), vmem((every, every), f32),
            vmem((comps, every, 8, nz), f32),
            vmem((every, 2 * every), f32), vmem((groups,) + tile, f32),
            vmem(tile, f32), vmem((side,) + tile, f32),
            vmem(tile, f32), vmem((side,) + tile, f32),
            vmem(tile, f32), vmem((groups,) + tile, f32),
            dma((comps + 2,)), dma((2,)), dma((2,)),
            dma((2, comps)), dma((2, comps)), dma((comps, 3)), dma((comps,)),
            dma((comps,)), dma((comps,)), dma((comps,)), dma((comps,)),
            dma((comps,)), dma((comps,)), dma((2, comps)), dma((comps,)), dma((comps,)), dma((4,)), dma((4,)),
        ],
        compiler_params=pltpu.CompilerParams(
            collective_id=0, has_side_effects=True, vmem_limit_bytes=48 * 1024 * 1024),
    )(pltpu.with_memory_space_constraint(start_modes, pltpu.HBM),
      pltpu.with_memory_space_constraint(materials, pltpu.HBM),
      pltpu.with_memory_space_constraint(stiffness_table, pltpu.HBM))


def solution(mesh):
    return jax.shard_map(
        functools.partial(shards, mesh.shape["blk"], mesh.shape["mode"]),
        mesh=mesh,
        in_specs=(P("mode", None, "blk", None, None), P("blk", None, None), P()),
        out_specs=(P("mode", None, "blk", None, None), P()),
        check_vma=False,
    )
```

```python
import functools
import math

import jax
import jax.numpy as jnp
from jax import lax
from jax.experimental import pallas as pl
from jax.experimental.pallas import tpu as pltpu
from jax.sharding import PartitionSpec as P

CENTER = 64.0
HALF_WIDTH = 56.0
MASS_SHIFT = 0.5
MESH = pl.DeviceIdType.MESH
HIGH = lax.Precision.HIGHEST
DEGREE = 4


def kernel(blks, groups, x_ref, mat_ref, tab_hbm, out_ref, proj_ref,
           tab_ref, own, mats, table, table_in, coef, close, field, odd, edge_out, edge_in,
           filt_out, image_out, filt_in, image_in, again_in, again, inverse_ref,
           back, part, part_in, in_y, in_z, total, tiles_sent,
           load, table_send, table_recv, near_send, near_recv, edge_send, edge_recv,
           filt_send, filt_recv, image_send, image_recv,
           back_send, back_recv, own_send, again_send, again_recv, sum_send, sum_recv):
    modes, comps, planes, ny, nz = x_ref.shape
    every = modes * groups
    halves = ny // 8
    side = math.isqrt(blks)
    blk, me = lax.axis_index("blk"), lax.axis_index("mode")
    left, right = lax.rem(blk + blks - 1, blks), lax.rem(blk + 1, blks)
    my_z, my_y = lax.div(blk, side), lax.rem(blk, side)
    no_left, no_right = blk == 0, blk == blks - 1

    def mode_peer(step):
        return lax.rem(me + step, groups)

    def y_peer(step):
        return my_z * side + lax.rem(my_y + step, side)

    def z_peer(step):
        return lax.rem(my_z + step, side) * side + my_y

    def tile_of(device):
        return lax.rem(device, 2) * 4 + lax.rem(lax.div(device, 2), 2) * 2 + lax.div(device, 4)

    my_tile = tile_of(me)

    def far_first(count):
        return sorted(range(1, count), key=lambda step: abs(2 * step - count))

    def remote(src, dst, send, recv, to_blk, to_mode):
        return pltpu.make_async_remote_copy(
            src_ref=src, dst_ref=dst, send_sem=send, recv_sem=recv,
            device_id={"blk": to_blk, "mode": to_mode}, device_id_type=MESH)

    def arrived(ref, semaphore):
        pltpu.make_async_copy(ref, ref, semaphore).wait()

    owner_last, owner_first, owner_row = 3, 4, 0

    load_mats = pltpu.make_async_copy(mat_ref, mats, load.at[comps])
    load_mats.start()
    load_tab = pltpu.make_async_copy(tab_hbm, tab_ref, load.at[comps + 1])
    load_tab.start()

    def load_own(comp):
        return pltpu.make_async_copy(x_ref.at[:, comp], own.at[comp], load.at[comp])

    for comp in range(comps):
        load_own(comp).start()

    barrier = pltpu.get_barrier_semaphore()

    def greet(to_blk, to_mode):
        pl.semaphore_signal(barrier, inc=1, device_id={"blk": to_blk, "mode": to_mode}, device_id_type=MESH)

    greet(left, me)
    greet(right, me)
    for step in range(1, side):
        greet(y_peer(step), me)
        greet(z_peer(step), me)
    for step in range(1, groups):
        greet(blk, mode_peer(step))

    @pl.when(me == owner_last)
    def _():
        for mode in range(groups):
            greet(right, mode)

    @pl.when((me == owner_first) | (me == owner_row))
    def _():
        for mode in range(groups):
            greet(left, mode)

    def over(count, body, unroll=1):
        def run(at, carry):
            body(at)
            return carry
        lax.fori_loop(0, count, run, 0, unroll=unroll)

    @pl.when(no_left)
    def _():
        table_in[0] = jnp.zeros_like(table)

        def clear(plane):
            for comp in range(comps):
                field[comp, plane] = jnp.zeros((ny, modes, nz), jnp.float32)
        over(planes, clear)

    @pl.when(no_right)
    def _():
        table_in[1] = jnp.zeros_like(table)

        def clear(plane):
            for comp in range(comps):
                field[comp, 2 * planes + plane] = jnp.zeros((ny, modes, nz), jnp.float32)
        over(planes, clear)

    scale = 2.0 / HALF_WIDTH

    def all_modes(rows):
        return jnp.broadcast_to(rows[:, None, :], (ny, modes, nz))

    def coefficients(values, plane):
        coef[0, plane] = all_modes(scale * (27.0 * values + (MASS_SHIFT - CENTER)))
        coef[1, plane] = all_modes(scale * values)

    load_mats.wait()
    load_tab.wait()

    def own_root(plane):
        labels = mats[plane]
        values = jnp.zeros((ny, nz), jnp.float32)
        for label in range(tab_ref.shape[0]):
            values = jnp.where(labels == label, tab_ref[label], values)
        table[plane] = values
        close[0, plane] = all_modes(jnp.sqrt(values))

    over(planes, own_root, planes)

    def weigh(comp):
        load_own(comp).wait()
        rows = own.at[comp].reshape(modes * planes * ny, nz)

        def body(plane):
            for y in range(ny):
                field[comp, planes + plane, y] = close[0, plane, y] * rows[pl.ds(plane * ny + y, modes, stride=planes * ny)]
        over(planes, body, 4)

    weigh(0)
    pl.semaphore_wait(barrier, 5 + (groups - 1) + 2 * (side - 1))

    def table_copy(slot):
        return remote(table, table_in.at[slot], table_send.at[slot], table_recv.at[slot], (right, left)[slot], me)

    def near_copy(comp, slot):
        return remote(field.at[comp, pl.ds(planes, planes)], field.at[comp, pl.ds(2 * planes * slot, planes)],
                      near_send.at[slot, comp], near_recv.at[slot, comp], (right, left)[slot], me)

    def edge_copies(comp):
        mine = pl.ds(pl.multiple_of(me * modes, modes), modes)
        to_left = [remote(edge_out.at[comp, 1, pl.ds(0, 8)], edge_in.at[comp, :, mine],
                          edge_send.at[comp, 0], edge_recv.at[comp], left, owner_last)]
        to_right = [remote(edge_out.at[comp, 0, pl.ds(1, 8)], edge_in.at[comp, :, mine],
                           edge_send.at[comp, 1], edge_recv.at[comp], right, owner_first),
                    remote(edge_out.at[comp, 0, pl.ds(0, 1)], edge_in.at[comp, pl.ds(0, 1), mine],
                           edge_send.at[comp, 2], edge_recv.at[comp], right, owner_row)]
        return to_left, to_right

    @pl.when(jnp.logical_not(no_left))
    def _():
        table_copy(1).start()
        near_copy(0, 1).start()

    @pl.when(jnp.logical_not(no_right))
    def _():
        table_copy(0).start()
        near_copy(0, 0).start()

    def start_near(comp):
        @pl.when(jnp.logical_not(no_left))
        def _():
            near_copy(comp, 1).start()

        @pl.when(jnp.logical_not(no_right))
        def _():
            near_copy(comp, 0).start()

    weigh(1)
    start_near(1)
    for comp in range(2, comps):
        weigh(comp)

    def own_coefficients(plane):
        values = table[plane]
        coefficients(values, planes + plane)
        root = jnp.sqrt(values)
        close[1, plane] = all_modes(1.0 / root)
        close[2, plane] = all_modes((27.0 * values + MASS_SHIFT) / root)

    over(planes, own_coefficients)

    @pl.when(jnp.logical_not(no_left))
    def _():
        table_copy(0).wait_recv()
        table_copy(1).wait_send()

    @pl.when(jnp.logical_not(no_right))
    def _():
        table_copy(1).wait_recv()
        table_copy(0).wait_send()

    def near_coefficients(plane):
        coefficients(table_in[0, plane], plane)
        coefficients(table_in[1, plane], 2 * planes + plane)

    over(planes, near_coefficients)

    none = jnp.zeros((1, modes, nz), jnp.float32)

    def box_z(v):
        lanes = lax.broadcasted_iota(jnp.int32, v.shape, 2)
        before = jnp.where(lanes == 0, 0.0, pltpu.roll(v, 1, 2))
        after = jnp.where(lanes == nz - 1, 0.0, pltpu.roll(v, nz - 1, 2))
        return v + (before + after)

    def box(u):
        return box_z(u + (jnp.concatenate([none, u[:-1]], axis=0) + jnp.concatenate([u[1:], none], axis=0)))

    def advance(step, comp):
        even = field.at[comp]
        now, other = (even, odd) if step % 2 == 0 else (odd, even)
        first = step + 1

        def body(at):
            plane = first + at
            w = now[plane]
            u = now[plane - 1] + w + now[plane + 1]
            new = coef[0, plane] * w - coef[1, plane] * box(u)
            if step == 0:
                new = 0.5 * new
            else:
                new = new - other[plane]
            other[plane] = new
        over(3 * planes - 2 * first, body, 3 * planes - 2 * first)

    def finals(comp):
        first, last = field[comp, planes, :9], field[comp, 2 * planes - 1, 8:]
        edge_out[comp, 1, :8] = box_z(first[:8] + (first[1:] + jnp.concatenate([none, first[:7]], axis=0)))
        edge_out[comp, 0] = box_z(jnp.concatenate([none, last], axis=0) + (
            jnp.concatenate([last, none], axis=0) + jnp.concatenate([none, none, last[:-1]], axis=0)))
        to_left, to_right = edge_copies(comp)

        @pl.when(jnp.logical_not(no_left))
        def _():
            for copy in to_left:
                copy.start()

        @pl.when(jnp.logical_not(no_right))
        def _():
            for copy in to_right:
                copy.start()

        field[comp, planes - 1] = jnp.zeros((ny, modes, nz), jnp.float32)
        field[comp, 2 * planes] = jnp.zeros((ny, modes, nz), jnp.float32)

        def body(plane):
            at = planes + plane
            w = field[comp, at]
            filt = w * close[1, plane]
            image = close[2, plane] * w - close[0, plane] * box(field[comp, at - 1] + w + field[comp, at + 1])
            for half in range(halves):
                filt_out[comp, plane * halves + half] = filt[8 * half:8 * half + 8]
                image_out[comp, plane * halves + half] = image[8 * half:8 * half + 8]
        over(planes, body, 4)

    def my_modes():
        return pl.ds(pl.multiple_of(me * modes, modes), modes)

    def spread(source, target, send, recv, comp):
        for step in range(1, groups):
            peer = mode_peer(step)
            remote(source.at[comp, tile_of(peer)], target.at[comp, :, my_modes()],
                   send.at[comp], recv.at[comp], blk, peer).start()

    def spread_wait(target, send, recv, comp):
        most = target.at[comp, :, pl.ds(0, (groups - 1) * modes)]
        arrived(most, recv.at[comp])
        arrived(most, send.at[comp])

    def filter_one(comp):
        @pl.when(jnp.logical_not(no_left))
        def _():
            near_copy(comp, 0).wait_recv()
            near_copy(comp, 1).wait_send()

        @pl.when(jnp.logical_not(no_right))
        def _():
            near_copy(comp, 1).wait_recv()
            near_copy(comp, 0).wait_send()

        for step in range(DEGREE):
            advance(step, comp)
        finals(comp)
        spread(filt_out, filt_in, filt_send, filt_recv, comp)

        @pl.when(comp + 1 < comps)
        def _():
            spread(image_out, image_in, image_send, image_recv, comp)

        @pl.when(comp + 2 < comps)
        def _():
            start_near(comp + 2)

        filt_in[comp, :, my_modes()] = filt_out[comp, my_tile]
        image_in[comp, :, my_modes()] = image_out[comp, my_tile]

    over(comps, filter_one)

    def add_edges(comp):
        @pl.when((me == owner_last) & jnp.logical_not(no_right))
        def _():
            arrived(edge_in.at[comp], edge_recv.at[comp])
            for group in range(groups):
                at = pl.ds(group * modes, modes)
                image_in[comp, :, at] = image_in[comp, :, at] - (2.0 * close[0, planes - 1, :8]) * edge_in[comp, :, at]

        @pl.when((me == owner_first) & jnp.logical_not(no_left))
        def _():
            arrived(edge_in.at[comp], edge_recv.at[comp])
            for group in range(groups):
                at = pl.ds(group * modes, modes)
                image_in[comp, :, at] = image_in[comp, :, at] - (2.0 * close[0, 0, 8:]) * edge_in[comp, :, at]

        @pl.when((me == owner_row) & jnp.logical_not(no_left))
        def _():
            arrived(edge_in.at[comp, pl.ds(0, 1)], edge_recv.at[comp])
            for group in range(groups):
                at = pl.ds(group * modes, modes)
                image_in[comp, 7, at] = image_in[comp, 7, at] - (2.0 * close[0, 0, 7]) * edge_in[comp, 0, at]

    def products(left, right):
        return lax.dot_general(left, right, (((1,), (1,)), ((), ())), precision=HIGH, preferred_element_type=jnp.float32)

    def pairs(ref, comp, first):
        return jnp.concatenate([ref[comp, first], ref[comp, first + 1]], axis=1)

    part[...] = jnp.zeros_like(part)

    def add_gram(comp):
        spread_wait(filt_in, filt_send, filt_recv, comp)
        sums = part[0]
        for row in range(0, 8, 2):
            filt = pairs(filt_in, comp, row)
            sums = sums + products(filt, jnp.concatenate([filt, filt], axis=0))
        part[0] = sums

    def add_cross(comp):
        spread_wait(image_in, image_send, image_recv, comp)
        add_edges(comp)
        sums = part[1, :, :every]
        for row in range(0, 8, 2):
            sums = sums + products(pairs(filt_in, comp, row), pairs(image_in, comp, row))
        part[1, :, :every] = sums

    over(comps, add_gram)

    opposite = mode_peer(groups // 2)
    core = lax.rem(me, 2)
    sibling = me + 1 - 2 * core

    def spread_again(comp):
        for step in far_first(groups):
            peer = mode_peer(step)
            remote(filt_out.at[comp, tile_of(mode_peer(step + groups // 2))], again_in.at[comp, :, my_modes()],
                   again_send.at[comp], again_recv.at[comp], blk, peer).start()
        again_in[comp, :, my_modes()] = filt_out[comp, tile_of(opposite)]

    def slots_of(which, phase):
        return ((part_in, groups, me), (in_y, side, my_y), (in_z, side, my_z), (total, groups, me))[phase]

    def send_sums(which, phase):
        target, count, my_slot = slots_of(which, phase)
        if phase == 0:
            own_tile = part[which, pl.ds(pl.multiple_of(me * 8, 8), 8)]
        else:
            before, before_count, _ = slots_of(which, phase - 1)
            own_tile = before[which, 0]
            for slot in range(1, before_count):
                own_tile = own_tile + before[which, slot]
            tiles_sent[which, phase - 1] = own_tile
        for step in far_first(count):
            if phase == 0 or phase == 3:
                to_blk, to_mode = blk, mode_peer(step)
            else:
                to_blk, to_mode = (y_peer, z_peer)[phase - 1](step), me
            if phase == 0:
                source = part.at[which, pl.ds(pl.multiple_of(mode_peer(step) * 8, 8), 8)]
            else:
                source = tiles_sent.at[which, phase - 1]
            remote(source, target.at[which, my_slot], sum_send.at[which, phase], sum_recv.at[which, phase],
                   to_blk, to_mode).start()
        target[which, my_slot] = own_tile

    def wait_sums(which, phase):
        target, count, _ = slots_of(which, phase)
        arrived(target.at[which, pl.ds(0, count - 1)], sum_recv.at[which, phase])

    send_sums(0, 0)
    spread(image_out, image_in, image_send, image_recv, comps - 1)
    over(comps - 1, spread_again)
    wait_sums(0, 0)
    send_sums(0, 1)
    over(comps, add_cross)
    send_sums(1, 0)
    spread_again(comps - 1)
    wait_sums(0, 1)
    send_sums(0, 2)
    wait_sums(1, 0)
    send_sums(1, 1)
    wait_sums(0, 2)
    send_sums(0, 3)
    wait_sums(1, 1)
    send_sums(1, 2)
    wait_sums(0, 3)

    sums = total[0].reshape((every, 2 * every))
    row_at = lax.broadcasted_iota(jnp.int32, (every, 2 * every), 0)
    lane_at = lax.broadcasted_iota(jnp.int32, (every, 2 * every), 1)
    work = jnp.where(lane_at < every, jnp.where(lane_at == row_at, 1.0, 0.0), sums)
    blocks = [work[8 * j:8 * j + 8] for j in range(every // 8)]
    sub = lax.broadcasted_iota(jnp.int32, (8, 2 * every), 0)

    def column(block, lane):
        return jnp.take_along_axis(block, jnp.full((8, 2 * every), lane, jnp.int32), axis=1)

    def spread_row(block, row):
        return jnp.broadcast_to(block[row:row + 1], (8, 2 * every))

    for k in range(0, every, 2):
        j, r = divmod(k, 8)
        ones = [column(block, every + k) for block in blocks[j:]]
        twos = [column(block, every + k + 1) for block in blocks[j:]]
        row_one, row_two = spread_row(blocks[j], r), spread_row(blocks[j], r + 1)
        mixed = spread_row(ones[0], r + 1)
        over_one = 1.0 / spread_row(ones[0], r)
        factor = mixed * over_one
        over_two = 1.0 / (spread_row(twos[0], r + 1) - factor * mixed)
        new_two = row_two - factor * row_one
        scaled_one, scaled_two = row_one * over_one, new_two * over_two
        for i in range(j, every // 8):
            one, two = ones[i - j], twos[i - j]
            less = blocks[i] - (one * scaled_one + (two - one * factor) * scaled_two)
            if i == j:
                less = jnp.where(sub > r + 1, less, jnp.where(sub == r + 1, new_two, blocks[i]))
            blocks[i] = less
    work = jnp.concatenate(blocks, axis=0)
    diagonal = jnp.sum(jnp.where(lane_at == row_at + every, work, 0.0), axis=1, keepdims=True)
    inverse = (work / jnp.sqrt(diagonal))[:, :every]
    inverse_ref[...] = inverse

    def place(tile):
        return lax.div(tile, halves), pl.ds(pl.multiple_of(lax.rem(tile, halves) * 8, 8), 8)

    def back_copies(comp):
        plane, rows = place(my_tile)
        copies = []
        for step in far_first(groups):
            peer = mode_peer(step)
            copies.append((peer, remote(back.at[comp, pl.ds(peer * modes, modes)], out_ref.at[:, comp, plane, rows],
                                        back_send.at[comp], back_recv.at[comp], blk, peer)))
        return copies

    def own_copies(comp):
        plane, rows = place(my_tile)
        other_plane, other_rows = place(tile_of(opposite))
        return (pltpu.make_async_copy(back.at[comp, pl.ds(me * modes, modes)], out_ref.at[:, comp, plane, rows],
                                      own_send.at[0, comp]),
                pltpu.make_async_copy(again.at[comp, pl.ds(core * modes, modes)], out_ref.at[:, comp, other_plane, other_rows],
                                      own_send.at[1, comp]))

    def sibling_copy(comp):
        plane, rows = place(tile_of(opposite))
        return remote(again.at[comp, pl.ds((1 - core) * modes, modes)], out_ref.at[:, comp, plane, rows],
                      back_send.at[comp], back_recv.at[comp], blk, sibling)

    def give_back(comp):
        filt = jnp.concatenate([filt_in[comp, row] for row in range(8)], axis=1)
        result = jnp.dot(inverse, filt, precision=HIGH, preferred_element_type=jnp.float32)
        for row in range(8):
            back[comp, :, row] = result[:, row * nz:(row + 1) * nz]
        for peer, copy in back_copies(comp):
            @pl.when(lax.div(peer, 2) != lax.div(opposite, 2))
            def _():
                copy.start()
        own_copies(comp)[0].start()

    def give_sibling(comp):
        arrived(again_in.at[comp, :, pl.ds(0, (groups - 1) * modes)], again_recv.at[comp])
        arrived(again_in.at[comp, :, pl.ds(0, (groups - 1) * modes)], again_send.at[comp])
        filt = jnp.concatenate([again_in[comp, row] for row in range(8)], axis=1)
        mine = inverse_ref[pl.ds(pl.multiple_of((me - core) * modes, 2 * modes), 2 * modes), :]
        result = jnp.dot(mine, filt, precision=HIGH, preferred_element_type=jnp.float32)
        for row in range(8):
            again[comp, :, row] = result[:, row * nz:(row + 1) * nz]
        sibling_copy(comp).start()
        own_copies(comp)[1].start()

    give_back(0)
    wait_sums(1, 2)
    send_sums(1, 3)
    for comp in range(1, comps):
        give_back(comp)
    for comp in range(comps):
        give_sibling(comp)
    wait_sums(1, 3)
    cross = total[1].reshape((every, 2 * every))[:, :every]
    half = jnp.dot(inverse, cross, precision=HIGH, preferred_element_type=jnp.float32)
    product = lax.dot_general(half, inverse, (((1,), (1,)), ((), ())), precision=HIGH,
                              preferred_element_type=jnp.float32)
    proj_ref[...] = 0.5 * (product + product.T)

    def finish(comp):
        to_left, to_right = edge_copies(comp)

        @pl.when(jnp.logical_not(no_left))
        def _():
            for copy in to_left:
                copy.wait_send()

        @pl.when(jnp.logical_not(no_right))
        def _():
            for copy in to_right:
                copy.wait_send()

        for copy in own_copies(comp):
            copy.wait()
        most = back.at[comp, pl.ds(0, (groups - 2) * modes)]
        arrived(most, back_recv.at[comp])
        arrived(most, back_send.at[comp])

    over(comps, finish)
    for which in range(2):
        for phase in range(4):
            target, count, _ = slots_of(which, phase)
            arrived(target.at[which, pl.ds(0, count - 1)], sum_send.at[which, phase])


def shards(blks, groups, start_modes, materials, stiffness_table):
    modes, comps, planes, ny, nz = start_modes.shape
    every = modes * groups
    side = math.isqrt(blks)
    vmem, dma = pltpu.VMEM, pltpu.SemaphoreType.DMA
    f32 = jnp.float32
    plane = (ny, modes, nz)
    tiles_out = (comps, groups, 8, modes, nz)
    tiles_in = (comps, 8, every, nz)
    tile = (8, 2 * every)
    return pl.pallas_call(
        functools.partial(kernel, blks, groups),
        out_shape=(jax.ShapeDtypeStruct(start_modes.shape, f32), jax.ShapeDtypeStruct((every, every), f32)),
        in_specs=[pl.BlockSpec(memory_space=pltpu.HBM), pl.BlockSpec(memory_space=pltpu.HBM),
                  pl.BlockSpec(memory_space=pltpu.HBM)],
        out_specs=(pl.BlockSpec(memory_space=pl.ANY), pl.BlockSpec(memory_space=pltpu.VMEM)),
        scratch_shapes=[
            pltpu.SMEM(stiffness_table.shape, f32),
            vmem((comps, modes, planes, ny, nz), f32),
            vmem((planes, ny, nz), jnp.int32), vmem((planes, ny, nz), f32), vmem((2, planes, ny, nz), f32),
            vmem((2, 3 * planes) + plane, f32), vmem((3, planes) + plane, f32),
            vmem((comps, 3 * planes) + plane, f32), vmem((3 * planes,) + plane, f32),
            vmem((comps, 2, 9, modes, nz), f32), vmem(tiles_in, f32),
            vmem(tiles_out, f32), vmem(tiles_out, f32),
            vmem(tiles_in, f32), vmem(tiles_in, f32),
            vmem(tiles_in, f32), vmem((comps, 2 * modes, 8, nz), f32), vmem((every, every), f32),
            vmem((comps, every, 8, nz), f32),
            vmem((2, every, 2 * every), f32), vmem((2, groups) + tile, f32), vmem((2, side) + tile, f32),
            vmem((2, side) + tile, f32), vmem((2, groups) + tile, f32), vmem((2, 3) + tile, f32),
            dma((comps + 2,)), dma((2,)), dma((2,)),
            dma((2, comps)), dma((2, comps)), dma((comps, 3)), dma((comps,)),
            dma((comps,)), dma((comps,)), dma((comps,)), dma((comps,)),
            dma((comps,)), dma((comps,)), dma((2, comps)), dma((comps,)), dma((comps,)), dma((2, 4)), dma((2, 4)),
        ],
        compiler_params=pltpu.CompilerParams(
            collective_id=0, has_side_effects=True, vmem_limit_bytes=48 * 1024 * 1024),
    )(pltpu.with_memory_space_constraint(start_modes, pltpu.HBM),
      pltpu.with_memory_space_constraint(materials, pltpu.HBM),
      pltpu.with_memory_space_constraint(stiffness_table, pltpu.HBM))


def solution(mesh):
    return jax.shard_map(
        functools.partial(shards, mesh.shape["blk"], mesh.shape["mode"]),
        mesh=mesh,
        in_specs=(P("mode", None, "blk", None, None), P("blk", None, None), P()),
        out_specs=(P("mode", None, "blk", None, None), P()),
        check_vma=False,
    )
```

```python
import functools
import math

import jax
import jax.numpy as jnp
from jax import lax
from jax.experimental import pallas as pl
from jax.experimental.pallas import tpu as pltpu
from jax.sharding import PartitionSpec as P

CENTER = 64.0
HALF_WIDTH = 56.0
MASS_SHIFT = 0.5
MESH = pl.DeviceIdType.MESH
HIGH = lax.Precision.HIGHEST
DEGREE = 4


def kernel(blks, groups, x_ref, mat_ref, tab_hbm, out_ref, proj_ref,
           tab_ref, own, mats, table, table_in, coef, close, field, odd, edge_out, edge_in,
           filt_out, image_out, filt_in, image_in, again_in, again, inverse_ref,
           back, part, part_in, in_y, in_z, total, tiles_sent,
           gram_part, gram_out, gram_in, plane_in, gram_total, gram_tiles,
           load, table_send, table_recv, near_send, near_recv, edge_send, edge_recv,
           filt_send, filt_recv, image_send, image_recv,
           back_send, back_recv, own_send, again_send, again_recv, sum_send, sum_recv, gram_send, gram_recv):
    modes, comps, planes, ny, nz = x_ref.shape
    every = modes * groups
    halves = ny // 8
    side = math.isqrt(blks)
    blk, me = lax.axis_index("blk"), lax.axis_index("mode")
    left, right = lax.rem(blk + blks - 1, blks), lax.rem(blk + 1, blks)
    my_z, my_y = lax.div(blk, side), lax.rem(blk, side)
    no_left, no_right = blk == 0, blk == blks - 1

    def mode_peer(step):
        return lax.rem(me + step, groups)

    def y_peer(step):
        return my_z * side + lax.rem(my_y + step, side)

    def z_peer(step):
        return lax.rem(my_z + step, side) * side + my_y

    def tile_of(device):
        return lax.rem(device, 2) * 4 + lax.rem(lax.div(device, 2), 2) * 2 + lax.div(device, 4)

    my_tile = tile_of(me)

    def far_first(count):
        return sorted(range(1, count), key=lambda step: abs(2 * step - count))

    def remote(src, dst, send, recv, to_blk, to_mode):
        return pltpu.make_async_remote_copy(
            src_ref=src, dst_ref=dst, send_sem=send, recv_sem=recv,
            device_id={"blk": to_blk, "mode": to_mode}, device_id_type=MESH)

    def arrived(ref, semaphore):
        pltpu.make_async_copy(ref, ref, semaphore).wait()

    owner_last, owner_first, owner_row = 3, 4, 0

    load_mats = pltpu.make_async_copy(mat_ref, mats, load.at[comps])
    load_mats.start()
    load_tab = pltpu.make_async_copy(tab_hbm, tab_ref, load.at[comps + 1])
    load_tab.start()

    def load_own(comp):
        return pltpu.make_async_copy(x_ref.at[:, comp], own.at[comp], load.at[comp])

    for comp in range(comps):
        load_own(comp).start()

    barrier = pltpu.get_barrier_semaphore()

    def greet(to_blk, to_mode):
        pl.semaphore_signal(barrier, inc=1, device_id={"blk": to_blk, "mode": to_mode}, device_id_type=MESH)

    around = sorted(((dz, dy) for dz in range(side) for dy in range(side) if dz or dy),
                    key=lambda at: -sum(min(d, side - d) for d in at))

    def plane_peer(dz, dy):
        return lax.rem(my_z + dz, side) * side + lax.rem(my_y + dy, side)

    for dz, dy in around:
        greet(plane_peer(dz, dy), me)
    for step in range(1, groups):
        greet(blk, mode_peer(step))

    @pl.when(me == owner_last)
    def _():
        for mode in range(groups):
            greet(right, mode)

    @pl.when((me == owner_first) | (me == owner_row))
    def _():
        for mode in range(groups):
            greet(left, mode)

    def over(count, body, unroll=1):
        def run(at, carry):
            body(at)
            return carry
        lax.fori_loop(0, count, run, 0, unroll=unroll)

    @pl.when(no_left)
    def _():
        table_in[0] = jnp.zeros_like(table)

        def clear(plane):
            for comp in range(comps):
                field[comp, plane] = jnp.zeros((ny, modes, nz), jnp.float32)
        over(planes, clear)

    @pl.when(no_right)
    def _():
        table_in[1] = jnp.zeros_like(table)

        def clear(plane):
            for comp in range(comps):
                field[comp, 2 * planes + plane] = jnp.zeros((ny, modes, nz), jnp.float32)
        over(planes, clear)

    scale = 2.0 / HALF_WIDTH

    def all_modes(rows):
        return jnp.broadcast_to(rows[:, None, :], (ny, modes, nz))

    def coefficients(values, plane):
        coef[0, plane] = all_modes(scale * (27.0 * values + (MASS_SHIFT - CENTER)))
        coef[1, plane] = all_modes(scale * values)

    load_mats.wait()
    load_tab.wait()

    def own_root(plane):
        labels = mats[plane]
        values = jnp.zeros((ny, nz), jnp.float32)
        for label in range(tab_ref.shape[0]):
            values = jnp.where(labels == label, tab_ref[label], values)
        table[plane] = values
        close[0, plane] = all_modes(jnp.sqrt(values))

    over(planes, own_root, planes)

    def weigh(comp):
        load_own(comp).wait()
        rows = own.at[comp].reshape(modes * planes * ny, nz)

        def body(plane):
            for y in range(ny):
                field[comp, planes + plane, y] = close[0, plane, y] * rows[pl.ds(plane * ny + y, modes, stride=planes * ny)]
        over(planes, body, 4)

    weigh(0)
    pl.semaphore_wait(barrier, 3 + (groups - 1) + (blks - 1))

    def table_copy(slot):
        return remote(table, table_in.at[slot], table_send.at[slot], table_recv.at[slot], (right, left)[slot], me)

    def near_copy(comp, slot):
        return remote(field.at[comp, pl.ds(planes, planes)], field.at[comp, pl.ds(2 * planes * slot, planes)],
                      near_send.at[slot, comp], near_recv.at[slot, comp], (right, left)[slot], me)

    def edge_copies(comp):
        mine = pl.ds(pl.multiple_of(me * modes, modes), modes)
        to_left = [remote(edge_out.at[comp, 1, pl.ds(0, 8)], edge_in.at[comp, :, mine],
                          edge_send.at[comp, 0], edge_recv.at[comp], left, owner_last)]
        to_right = [remote(edge_out.at[comp, 0, pl.ds(1, 8)], edge_in.at[comp, :, mine],
                           edge_send.at[comp, 1], edge_recv.at[comp], right, owner_first),
                    remote(edge_out.at[comp, 0, pl.ds(0, 1)], edge_in.at[comp, pl.ds(0, 1), mine],
                           edge_send.at[comp, 2], edge_recv.at[comp], right, owner_row)]
        return to_left, to_right

    @pl.when(jnp.logical_not(no_left))
    def _():
        table_copy(1).start()
        near_copy(0, 1).start()

    @pl.when(jnp.logical_not(no_right))
    def _():
        table_copy(0).start()
        near_copy(0, 0).start()

    def start_near(comp):
        @pl.when(jnp.logical_not(no_left))
        def _():
            near_copy(comp, 1).start()

        @pl.when(jnp.logical_not(no_right))
        def _():
            near_copy(comp, 0).start()

    weigh(1)
    start_near(1)
    for comp in range(2, comps):
        weigh(comp)

    def own_coefficients(plane):
        values = table[plane]
        coefficients(values, planes + plane)
        root = jnp.sqrt(values)
        close[1, plane] = all_modes(1.0 / root)
        close[2, plane] = all_modes((27.0 * values + MASS_SHIFT) / root)

    over(planes, own_coefficients)

    @pl.when(jnp.logical_not(no_left))
    def _():
        table_copy(0).wait_recv()
        table_copy(1).wait_send()

    @pl.when(jnp.logical_not(no_right))
    def _():
        table_copy(1).wait_recv()
        table_copy(0).wait_send()

    def near_coefficients(plane):
        coefficients(table_in[0, plane], plane)
        coefficients(table_in[1, plane], 2 * planes + plane)

    over(planes, near_coefficients)

    none = jnp.zeros((1, modes, nz), jnp.float32)

    def box_z(v):
        lanes = lax.broadcasted_iota(jnp.int32, v.shape, 2)
        before = jnp.where(lanes == 0, 0.0, pltpu.roll(v, 1, 2))
        after = jnp.where(lanes == nz - 1, 0.0, pltpu.roll(v, nz - 1, 2))
        return v + (before + after)

    def box(u):
        return box_z(u + (jnp.concatenate([none, u[:-1]], axis=0) + jnp.concatenate([u[1:], none], axis=0)))

    def advance(step, comp):
        even = field.at[comp]
        now, other = (even, odd) if step % 2 == 0 else (odd, even)
        first = step + 1

        def body(at):
            plane = first + at
            w = now[plane]
            u = now[plane - 1] + w + now[plane + 1]
            new = coef[0, plane] * w - coef[1, plane] * box(u)
            if step == 0:
                new = 0.5 * new
            else:
                new = new - other[plane]
            other[plane] = new
        over(3 * planes - 2 * first, body, 3 * planes - 2 * first)

    def my_modes():
        return pl.ds(pl.multiple_of(me * modes, modes), modes)

    def spread(source, target, send, recv, comp):
        for step in range(1, groups):
            peer = mode_peer(step)
            remote(source.at[comp, tile_of(peer)], target.at[comp, :, my_modes()],
                   send.at[comp], recv.at[comp], blk, peer).start()

    def spread_wait(target, send, recv, comp):
        most = target.at[comp, :, pl.ds(0, (groups - 1) * modes)]
        arrived(most, recv.at[comp])
        arrived(most, send.at[comp])

    def put(target, comp, plane, value):
        for half in range(halves):
            target[comp, plane * halves + half] = value[8 * half:8 * half + 8]

    def final_filter(comp):
        def body(plane):
            put(filt_out, comp, plane, field[comp, planes + plane] * close[1, plane])
        over(planes, body, planes)

    def final_image(comp):
        first, last = field[comp, planes, :9], field[comp, 2 * planes - 1, 8:]
        edge_out[comp, 1, :8] = box_z(first[:8] + (first[1:] + jnp.concatenate([none, first[:7]], axis=0)))
        edge_out[comp, 0] = box_z(jnp.concatenate([none, last], axis=0) + (
            jnp.concatenate([last, none], axis=0) + jnp.concatenate([none, none, last[:-1]], axis=0)))
        to_left, to_right = edge_copies(comp)

        @pl.when(jnp.logical_not(no_left))
        def _():
            for copy in to_left:
                copy.start()

        @pl.when(jnp.logical_not(no_right))
        def _():
            for copy in to_right:
                copy.start()

        field[comp, planes - 1] = jnp.zeros((ny, modes, nz), jnp.float32)
        field[comp, 2 * planes] = jnp.zeros((ny, modes, nz), jnp.float32)

        def body(plane):
            at = planes + plane
            w = field[comp, at]
            put(image_out, comp, plane,
                close[2, plane] * w - close[0, plane] * box(field[comp, at - 1] + w + field[comp, at + 1]))
        over(planes, body, 4)

    def filter_one(comp):
        @pl.when(jnp.logical_not(no_left))
        def _():
            near_copy(comp, 0).wait_recv()
            near_copy(comp, 1).wait_send()

        @pl.when(jnp.logical_not(no_right))
        def _():
            near_copy(comp, 1).wait_recv()
            near_copy(comp, 0).wait_send()

        for step in range(DEGREE):
            advance(step, comp)
        final_filter(comp)
        spread(filt_out, filt_in, filt_send, filt_recv, comp)

        @pl.when(comp > 0)
        def _():
            spread(image_out, image_in, image_send, image_recv, comp - 1)

        @pl.when(comp + 2 < comps)
        def _():
            start_near(comp + 2)

        final_image(comp)
        filt_in[comp, :, my_modes()] = filt_out[comp, my_tile]
        image_in[comp, :, my_modes()] = image_out[comp, my_tile]

    over(comps, filter_one)

    def add_edges(comp):
        @pl.when((me == owner_last) & jnp.logical_not(no_right))
        def _():
            arrived(edge_in.at[comp], edge_recv.at[comp])
            for group in range(groups):
                at = pl.ds(group * modes, modes)
                image_in[comp, :, at] = image_in[comp, :, at] - (2.0 * close[0, planes - 1, :8]) * edge_in[comp, :, at]

        @pl.when((me == owner_first) & jnp.logical_not(no_left))
        def _():
            arrived(edge_in.at[comp], edge_recv.at[comp])
            for group in range(groups):
                at = pl.ds(group * modes, modes)
                image_in[comp, :, at] = image_in[comp, :, at] - (2.0 * close[0, 0, 8:]) * edge_in[comp, :, at]

        @pl.when((me == owner_row) & jnp.logical_not(no_left))
        def _():
            arrived(edge_in.at[comp, pl.ds(0, 1)], edge_recv.at[comp])
            for group in range(groups):
                at = pl.ds(group * modes, modes)
                image_in[comp, 7, at] = image_in[comp, 7, at] - (2.0 * close[0, 0, 7]) * edge_in[comp, 0, at]

    def products(left, right):
        return lax.dot_general(left, right, (((1,), (1,)), ((), ())), precision=HIGH, preferred_element_type=jnp.float32)

    def pairs(ref, comp, first):
        return jnp.concatenate([ref[comp, first], ref[comp, first + 1]], axis=1)

    part[...] = jnp.zeros_like(part)
    gram_part[...] = jnp.zeros_like(gram_part)

    def add_gram(comp):
        spread_wait(filt_in, filt_send, filt_recv, comp)
        sums = gram_part[...]
        for row in range(0, 8, 2):
            filt = pairs(filt_in, comp, row)
            sums = sums + products(filt, filt)
        gram_part[...] = sums

    def add_cross(comp):
        spread_wait(image_in, image_send, image_recv, comp)
        add_edges(comp)
        sums = part[:, :every]
        for row in range(0, 8, 2):
            sums = sums + products(pairs(filt_in, comp, row), pairs(image_in, comp, row))
        part[:, :every] = sums

    over(comps, add_gram)

    opposite = mode_peer(groups // 2)
    core = lax.rem(me, 2)
    sibling = me + 1 - 2 * core

    def spread_again(comp):
        for step in far_first(groups):
            peer = mode_peer(step)
            remote(filt_out.at[comp, tile_of(mode_peer(step + groups // 2))], again_in.at[comp, :, my_modes()],
                   again_send.at[comp], again_recv.at[comp], blk, peer).start()
        again_in[comp, :, my_modes()] = filt_out[comp, tile_of(opposite)]

    low = pl.ds(0, 4)

    def pack_gram():
        sums = gram_part[...]
        packed = jnp.concatenate([sums[:every // 2], sums[every // 2:]], axis=1)
        for group in range(groups):
            gram_out[group, :4] = packed[4 * group:4 * group + 4]

    def send_gram_scatter():
        for step in far_first(groups):
            remote(gram_out.at[mode_peer(step), low], gram_in.at[me, low], gram_send.at[0], gram_recv.at[0],
                   blk, mode_peer(step)).start()
        gram_in[me, :4] = gram_out[me, :4]

    def send_gram_plane():
        tile = gram_in[0, :4]
        for group in range(1, groups):
            tile = tile + gram_in[group, :4]
        gram_tiles[0, :4] = tile
        for dz, dy in around:
            remote(gram_tiles.at[0, low], plane_in.at[blk, low], gram_send.at[1], gram_recv.at[1],
                   plane_peer(dz, dy), me).start()
        plane_in[blk, :4] = tile

    def send_gram_gather():
        tiles = [plane_in[slot, :4] for slot in range(blks)]
        while len(tiles) > 1:
            tiles = [tiles[at] + tiles[at + 1] for at in range(0, len(tiles), 2)]
        gram_tiles[1, :4] = tiles[0]
        for step in far_first(groups):
            remote(gram_tiles.at[1, low], gram_total.at[me, low], gram_send.at[2], gram_recv.at[2],
                   blk, mode_peer(step)).start()
        gram_total[me, :4] = tiles[0]

    def wait_gram(phase, semaphores):
        target, count = ((gram_in, groups), (plane_in, blks), (gram_total, groups))[phase]
        arrived(target.at[pl.ds(0, count - 1), low], semaphores.at[phase])

    def slots_of(phase):
        return ((part_in, groups, me), (in_y, side, my_y), (in_z, side, my_z), (total, groups, me))[phase]

    def send_sums(phase):
        target, count, my_slot = slots_of(phase)
        if phase == 0:
            own_tile = part[pl.ds(pl.multiple_of(me * 8, 8), 8)]
        else:
            before, before_count, _ = slots_of(phase - 1)
            own_tile = before[0]
            for slot in range(1, before_count):
                own_tile = own_tile + before[slot]
            tiles_sent[phase - 1] = own_tile
        for step in far_first(count):
            if phase == 0 or phase == 3:
                to_blk, to_mode = blk, mode_peer(step)
            else:
                to_blk, to_mode = (y_peer, z_peer)[phase - 1](step), me
            if phase == 0:
                source = part.at[pl.ds(pl.multiple_of(mode_peer(step) * 8, 8), 8)]
            else:
                source = tiles_sent.at[phase - 1]
            remote(source, target.at[my_slot], sum_send.at[phase], sum_recv.at[phase], to_blk, to_mode).start()
        target[my_slot] = own_tile

    def wait_sums(phase):
        target, count, _ = slots_of(phase)
        arrived(target.at[pl.ds(0, count - 1)], sum_recv.at[phase])

    pack_gram()
    send_gram_scatter()
    spread(image_out, image_in, image_send, image_recv, comps - 1)
    over(comps - 1, spread_again)
    wait_gram(0, gram_recv)
    send_gram_plane()
    over(comps, add_cross)
    send_sums(0)
    spread_again(comps - 1)
    wait_gram(1, gram_recv)
    send_gram_gather()
    wait_sums(0)
    send_sums(1)
    wait_gram(2, gram_recv)

    packed = jnp.concatenate([gram_total[group, :4] for group in range(groups)], axis=0)
    gram = jnp.concatenate([packed[:, :every], packed[:, every:]], axis=0)
    row_at = lax.broadcasted_iota(jnp.int32, (every, 2 * every), 0)
    lane_at = lax.broadcasted_iota(jnp.int32, (every, 2 * every), 1)
    work = jnp.concatenate([jnp.where(lane_at == row_at, 1.0, 0.0)[:, :every], gram], axis=1)
    blocks = [work[8 * j:8 * j + 8] for j in range(every // 8)]
    sub = lax.broadcasted_iota(jnp.int32, (8, 2 * every), 0)

    def column(block, lane):
        return jnp.take_along_axis(block, jnp.full((8, 2 * every), lane, jnp.int32), axis=1)

    def spread_row(block, row):
        return jnp.broadcast_to(block[row:row + 1], (8, 2 * every))

    for k in range(0, every, 2):
        if k == every // 2:
            wait_sums(1)
            send_sums(2)
        j, r = divmod(k, 8)
        ones = [column(block, every + k) for block in blocks[j:]]
        twos = [column(block, every + k + 1) for block in blocks[j:]]
        row_one, row_two = spread_row(blocks[j], r), spread_row(blocks[j], r + 1)
        mixed = spread_row(ones[0], r + 1)
        over_one = 1.0 / spread_row(ones[0], r)
        factor = mixed * over_one
        over_two = 1.0 / (spread_row(twos[0], r + 1) - factor * mixed)
        new_two = row_two - factor * row_one
        scaled_one, scaled_two = row_one * over_one, new_two * over_two
        for i in range(j, every // 8):
            one, two = ones[i - j], twos[i - j]
            less = blocks[i] - (one * scaled_one + (two - one * factor) * scaled_two)
            if i == j:
                less = jnp.where(sub > r + 1, less, jnp.where(sub == r + 1, new_two, blocks[i]))
            blocks[i] = less
    work = jnp.concatenate(blocks, axis=0)
    diagonal = jnp.sum(jnp.where(lane_at == row_at + every, work, 0.0), axis=1, keepdims=True)
    inverse = (work / jnp.sqrt(diagonal))[:, :every]
    inverse_ref[...] = inverse

    def place(tile):
        return lax.div(tile, halves), pl.ds(pl.multiple_of(lax.rem(tile, halves) * 8, 8), 8)

    def back_copies(comp):
        plane, rows = place(my_tile)
        copies = []
        for step in far_first(groups):
            peer = mode_peer(step)
            copies.append((peer, remote(back.at[comp, pl.ds(peer * modes, modes)], out_ref.at[:, comp, plane, rows],
                                        back_send.at[comp], back_recv.at[comp], blk, peer)))
        return copies

    def own_copies(comp):
        plane, rows = place(my_tile)
        other_plane, other_rows = place(tile_of(opposite))
        return (pltpu.make_async_copy(back.at[comp, pl.ds(me * modes, modes)], out_ref.at[:, comp, plane, rows],
                                      own_send.at[0, comp]),
                pltpu.make_async_copy(again.at[comp, pl.ds(core * modes, modes)], out_ref.at[:, comp, other_plane, other_rows],
                                      own_send.at[1, comp]))

    def sibling_copy(comp):
        plane, rows = place(tile_of(opposite))
        return remote(again.at[comp, pl.ds((1 - core) * modes, modes)], out_ref.at[:, comp, plane, rows],
                      back_send.at[comp], back_recv.at[comp], blk, sibling)

    def give_back(comp):
        filt = jnp.concatenate([filt_in[comp, row] for row in range(8)], axis=1)
        result = jnp.dot(inverse, filt, precision=HIGH, preferred_element_type=jnp.float32)
        for row in range(8):
            back[comp, :, row] = result[:, row * nz:(row + 1) * nz]
        for peer, copy in back_copies(comp):
            @pl.when(lax.div(peer, 2) != lax.div(opposite, 2))
            def _():
                copy.start()
        own_copies(comp)[0].start()

    def give_sibling(comp):
        arrived(again_in.at[comp, :, pl.ds(0, (groups - 1) * modes)], again_recv.at[comp])
        arrived(again_in.at[comp, :, pl.ds(0, (groups - 1) * modes)], again_send.at[comp])
        filt = jnp.concatenate([again_in[comp, row] for row in range(8)], axis=1)
        mine = inverse_ref[pl.ds(pl.multiple_of((me - core) * modes, 2 * modes), 2 * modes), :]
        result = jnp.dot(mine, filt, precision=HIGH, preferred_element_type=jnp.float32)
        for row in range(8):
            again[comp, :, row] = result[:, row * nz:(row + 1) * nz]
        sibling_copy(comp).start()
        own_copies(comp)[1].start()

    for comp in range(comps):
        give_back(comp)
    wait_sums(2)
    send_sums(3)
    for comp in range(comps):
        give_sibling(comp)
    wait_sums(3)
    cross = total[...].reshape((every, 2 * every))[:, :every]
    half = jnp.dot(inverse, cross, precision=HIGH, preferred_element_type=jnp.float32)
    product = lax.dot_general(half, inverse, (((1,), (1,)), ((), ())), precision=HIGH,
                              preferred_element_type=jnp.float32)
    proj_ref[...] = 0.5 * (product + product.T)

    def finish(comp):
        to_left, to_right = edge_copies(comp)

        @pl.when(jnp.logical_not(no_left))
        def _():
            for copy in to_left:
                copy.wait_send()

        @pl.when(jnp.logical_not(no_right))
        def _():
            for copy in to_right:
                copy.wait_send()

        for copy in own_copies(comp):
            copy.wait()
        most = back.at[comp, pl.ds(0, (groups - 2) * modes)]
        arrived(most, back_recv.at[comp])
        arrived(most, back_send.at[comp])

    over(comps, finish)
    for phase in range(3):
        wait_gram(phase, gram_send)
    for phase in range(4):
        target, count, _ = slots_of(phase)
        arrived(target.at[pl.ds(0, count - 1)], sum_send.at[phase])


def shards(blks, groups, start_modes, materials, stiffness_table):
    modes, comps, planes, ny, nz = start_modes.shape
    every = modes * groups
    side = math.isqrt(blks)
    vmem, dma = pltpu.VMEM, pltpu.SemaphoreType.DMA
    f32 = jnp.float32
    plane = (ny, modes, nz)
    tiles_out = (comps, groups, 8, modes, nz)
    tiles_in = (comps, 8, every, nz)
    tile = (8, 2 * every)
    return pl.pallas_call(
        functools.partial(kernel, blks, groups),
        out_shape=(jax.ShapeDtypeStruct(start_modes.shape, f32), jax.ShapeDtypeStruct((every, every), f32)),
        in_specs=[pl.BlockSpec(memory_space=pltpu.HBM), pl.BlockSpec(memory_space=pltpu.HBM),
                  pl.BlockSpec(memory_space=pltpu.HBM)],
        out_specs=(pl.BlockSpec(memory_space=pl.ANY), pl.BlockSpec(memory_space=pltpu.VMEM)),
        scratch_shapes=[
            pltpu.SMEM(stiffness_table.shape, f32),
            vmem((comps, modes, planes, ny, nz), f32),
            vmem((planes, ny, nz), jnp.int32), vmem((planes, ny, nz), f32), vmem((2, planes, ny, nz), f32),
            vmem((2, 3 * planes) + plane, f32), vmem((3, planes) + plane, f32),
            vmem((comps, 3 * planes) + plane, f32), vmem((3 * planes,) + plane, f32),
            vmem((comps, 2, 9, modes, nz), f32), vmem(tiles_in, f32),
            vmem(tiles_out, f32), vmem(tiles_out, f32),
            vmem(tiles_in, f32), vmem(tiles_in, f32),
            vmem(tiles_in, f32), vmem((comps, 2 * modes, 8, nz), f32), vmem((every, every), f32),
            vmem((comps, every, 8, nz), f32),
            vmem((every, 2 * every), f32), vmem((groups,) + tile, f32), vmem((side,) + tile, f32),
            vmem((side,) + tile, f32), vmem((groups,) + tile, f32), vmem((3,) + tile, f32),
            vmem((every, every), f32), vmem((groups,) + tile, f32), vmem((groups,) + tile, f32),
            vmem((blks,) + tile, f32), vmem((groups,) + tile, f32), vmem((2,) + tile, f32),
            dma((comps + 2,)), dma((2,)), dma((2,)),
            dma((2, comps)), dma((2, comps)), dma((comps, 3)), dma((comps,)),
            dma((comps,)), dma((comps,)), dma((comps,)), dma((comps,)),
            dma((comps,)), dma((comps,)), dma((2, comps)), dma((comps,)), dma((comps,)), dma((4,)), dma((4,)), dma((3,)), dma((3,)),
        ],
        compiler_params=pltpu.CompilerParams(
            collective_id=0, has_side_effects=True, vmem_limit_bytes=48 * 1024 * 1024),
    )(pltpu.with_memory_space_constraint(start_modes, pltpu.HBM),
      pltpu.with_memory_space_constraint(materials, pltpu.HBM),
      pltpu.with_memory_space_constraint(stiffness_table, pltpu.HBM))


def solution(mesh):
    return jax.shard_map(
        functools.partial(shards, mesh.shape["blk"], mesh.shape["mode"]),
        mesh=mesh,
        in_specs=(P("mode", None, "blk", None, None), P("blk", None, None), P()),
        out_specs=(P("mode", None, "blk", None, None), P()),
        check_vma=False,
    )
```

```python
import functools
import math

import jax
import jax.numpy as jnp
from jax import lax
from jax.experimental import pallas as pl
from jax.experimental.pallas import tpu as pltpu
from jax.sharding import PartitionSpec as P

CENTER = 64.0
HALF_WIDTH = 56.0
MASS_SHIFT = 0.5
MESH = pl.DeviceIdType.MESH
HIGH = lax.Precision.HIGHEST
DEGREE = 4


def kernel(blks, groups, x_ref, mat_ref, tab_hbm, out_ref, proj_ref,
           tab_ref, own, mats, table, table_in, coef, close, field, odd, edge_out, edge_in,
           filt_out, image_out, filt_in, image_in, again_in, again, inverse_ref,
           back, part, part_in, in_y, in_z, total, tiles_sent,
           load, table_send, table_recv, near_send, near_recv, edge_send, edge_recv,
           filt_send, filt_recv, image_send, image_recv,
           back_send, back_recv, own_send, again_send, again_recv, sum_send, sum_recv):
    modes, comps, planes, ny, nz = x_ref.shape
    every = modes * groups
    halves = ny // 8
    side = math.isqrt(blks)
    blk, me = lax.axis_index("blk"), lax.axis_index("mode")
    left, right = lax.rem(blk + blks - 1, blks), lax.rem(blk + 1, blks)
    my_z, my_y = lax.div(blk, side), lax.rem(blk, side)
    no_left, no_right = blk == 0, blk == blks - 1

    def mode_peer(step):
        return lax.rem(me + step, groups)

    def y_peer(step):
        return my_z * side + lax.rem(my_y + step, side)

    def z_peer(step):
        return lax.rem(my_z + step, side) * side + my_y

    def tile_of(device):
        return lax.rem(device, 2) * 4 + lax.rem(lax.div(device, 2), 2) * 2 + lax.div(device, 4)

    my_tile = tile_of(me)

    def far_first(count):
        return sorted(range(1, count), key=lambda step: abs(2 * step - count))

    def remote(src, dst, send, recv, to_blk, to_mode):
        return pltpu.make_async_remote_copy(
            src_ref=src, dst_ref=dst, send_sem=send, recv_sem=recv,
            device_id={"blk": to_blk, "mode": to_mode}, device_id_type=MESH)

    def arrived(ref, semaphore):
        pltpu.make_async_copy(ref, ref, semaphore).wait()

    owner_last, owner_first, owner_row = 3, 4, 0

    load_mats = pltpu.make_async_copy(mat_ref, mats, load.at[comps])
    load_mats.start()
    load_tab = pltpu.make_async_copy(tab_hbm, tab_ref, load.at[comps + 1])
    load_tab.start()

    def load_own(comp):
        return pltpu.make_async_copy(x_ref.at[:, comp], own.at[comp], load.at[comp])

    for comp in range(comps):
        load_own(comp).start()

    barrier = pltpu.get_barrier_semaphore()

    def greet(to_blk, to_mode):
        pl.semaphore_signal(barrier, inc=1, device_id={"blk": to_blk, "mode": to_mode}, device_id_type=MESH)

    greet(left, me)
    greet(right, me)
    for step in range(1, side):
        greet(y_peer(step), me)
        greet(z_peer(step), me)
    for step in range(1, groups):
        greet(blk, mode_peer(step))

    @pl.when(me == owner_last)
    def _():
        for mode in range(groups):
            greet(right, mode)

    @pl.when((me == owner_first) | (me == owner_row))
    def _():
        for mode in range(groups):
            greet(left, mode)

    def over(count, body, unroll=1):
        def run(at, carry):
            body(at)
            return carry
        lax.fori_loop(0, count, run, 0, unroll=unroll)

    @pl.when(no_left)
    def _():
        table_in[0] = jnp.zeros_like(table)

        def clear(plane):
            for comp in range(comps):
                field[comp, plane] = jnp.zeros((ny, modes, nz), jnp.float32)
        over(planes, clear)

    @pl.when(no_right)
    def _():
        table_in[1] = jnp.zeros_like(table)

        def clear(plane):
            for comp in range(comps):
                field[comp, 2 * planes + plane] = jnp.zeros((ny, modes, nz), jnp.float32)
        over(planes, clear)

    scale = 2.0 / HALF_WIDTH

    def all_modes(rows):
        return jnp.broadcast_to(rows[:, None, :], (ny, modes, nz))

    def coefficients(values, plane):
        coef[0, plane] = all_modes(scale * (27.0 * values + (MASS_SHIFT - CENTER)))
        coef[1, plane] = all_modes(scale * values)

    load_mats.wait()
    load_tab.wait()

    def own_root(plane):
        labels = mats[plane]
        values = jnp.zeros((ny, nz), jnp.float32)
        for label in range(tab_ref.shape[0]):
            values = jnp.where(labels == label, tab_ref[label], values)
        table[plane] = values
        close[0, plane] = all_modes(jnp.sqrt(values))

    over(planes, own_root, planes)

    def weigh(comp):
        load_own(comp).wait()
        rows = own.at[comp].reshape(modes * planes * ny, nz)

        def body(plane):
            for y in range(ny):
                field[comp, planes + plane, y] = close[0, plane, y] * rows[pl.ds(plane * ny + y, modes, stride=planes * ny)]
        over(planes, body, 4)

    weigh(0)
    pl.semaphore_wait(barrier, 5 + (groups - 1) + 2 * (side - 1))

    def table_copy(slot):
        return remote(table, table_in.at[slot], table_send.at[slot], table_recv.at[slot], (right, left)[slot], me)

    def near_copy(comp, slot):
        return remote(field.at[comp, pl.ds(planes, planes)], field.at[comp, pl.ds(2 * planes * slot, planes)],
                      near_send.at[slot, comp], near_recv.at[slot, comp], (right, left)[slot], me)

    def edge_copies(comp):
        mine = pl.ds(pl.multiple_of(me * modes, modes), modes)
        to_left = [remote(edge_out.at[comp, 1, pl.ds(0, 8)], edge_in.at[comp, :, mine],
                          edge_send.at[comp, 0], edge_recv.at[comp], left, owner_last)]
        to_right = [remote(edge_out.at[comp, 0, pl.ds(1, 8)], edge_in.at[comp, :, mine],
                           edge_send.at[comp, 1], edge_recv.at[comp], right, owner_first),
                    remote(edge_out.at[comp, 0, pl.ds(0, 1)], edge_in.at[comp, pl.ds(0, 1), mine],
                           edge_send.at[comp, 2], edge_recv.at[comp], right, owner_row)]
        return to_left, to_right

    @pl.when(jnp.logical_not(no_left))
    def _():
        table_copy(1).start()
        near_copy(0, 1).start()

    @pl.when(jnp.logical_not(no_right))
    def _():
        table_copy(0).start()
        near_copy(0, 0).start()

    def start_near(comp):
        @pl.when(jnp.logical_not(no_left))
        def _():
            near_copy(comp, 1).start()

        @pl.when(jnp.logical_not(no_right))
        def _():
            near_copy(comp, 0).start()

    weigh(1)
    start_near(1)
    for comp in range(2, comps):
        weigh(comp)

    def own_coefficients(plane):
        values = table[plane]
        coefficients(values, planes + plane)
        root = jnp.sqrt(values)
        close[1, plane] = all_modes(1.0 / root)
        close[2, plane] = all_modes((27.0 * values + MASS_SHIFT) / root)

    over(planes, own_coefficients)

    @pl.when(jnp.logical_not(no_left))
    def _():
        table_copy(0).wait_recv()
        table_copy(1).wait_send()

    @pl.when(jnp.logical_not(no_right))
    def _():
        table_copy(1).wait_recv()
        table_copy(0).wait_send()

    def near_coefficients(plane):
        coefficients(table_in[0, plane], plane)
        coefficients(table_in[1, plane], 2 * planes + plane)

    over(planes, near_coefficients)

    none = jnp.zeros((1, modes, nz), jnp.float32)

    def box_z(v):
        lanes = lax.broadcasted_iota(jnp.int32, v.shape, 2)
        before = jnp.where(lanes == 0, 0.0, pltpu.roll(v, 1, 2))
        after = jnp.where(lanes == nz - 1, 0.0, pltpu.roll(v, nz - 1, 2))
        return v + (before + after)

    def box(u):
        return box_z(u + (jnp.concatenate([none, u[:-1]], axis=0) + jnp.concatenate([u[1:], none], axis=0)))

    def advance(step, comp):
        even = field.at[comp]
        now, other = (even, odd) if step % 2 == 0 else (odd, even)
        first = step + 1

        def body(at):
            plane = first + at
            w = now[plane]
            u = now[plane - 1] + w + now[plane + 1]
            new = coef[0, plane] * w - coef[1, plane] * box(u)
            if step == 0:
                new = 0.5 * new
            else:
                new = new - other[plane]
            other[plane] = new
        over(3 * planes - 2 * first, body, 3 * planes - 2 * first)

    def my_modes():
        return pl.ds(pl.multiple_of(me * modes, modes), modes)

    def spread(source, target, send, recv, comp):
        for step in range(1, groups):
            peer = mode_peer(step)
            remote(source.at[comp, tile_of(peer)], target.at[comp, :, my_modes()],
                   send.at[comp], recv.at[comp], blk, peer).start()

    def spread_wait(target, send, recv, comp):
        most = target.at[comp, :, pl.ds(0, (groups - 1) * modes)]
        arrived(most, recv.at[comp])
        arrived(most, send.at[comp])

    def put(target, comp, plane, value):
        for half in range(halves):
            target[comp, plane * halves + half] = value[8 * half:8 * half + 8]

    def final_filter(comp):
        def body(plane):
            put(filt_out, comp, plane, field[comp, planes + plane] * close[1, plane])
        over(planes, body, planes)

    def final_image(comp):
        first, last = field[comp, planes, :9], field[comp, 2 * planes - 1, 8:]
        edge_out[comp, 1, :8] = box_z(first[:8] + (first[1:] + jnp.concatenate([none, first[:7]], axis=0)))
        edge_out[comp, 0] = box_z(jnp.concatenate([none, last], axis=0) + (
            jnp.concatenate([last, none], axis=0) + jnp.concatenate([none, none, last[:-1]], axis=0)))
        to_left, to_right = edge_copies(comp)

        @pl.when(jnp.logical_not(no_left))
        def _():
            for copy in to_left:
                copy.start()

        @pl.when(jnp.logical_not(no_right))
        def _():
            for copy in to_right:
                copy.start()

        field[comp, planes - 1] = jnp.zeros((ny, modes, nz), jnp.float32)
        field[comp, 2 * planes] = jnp.zeros((ny, modes, nz), jnp.float32)

        def body(plane):
            at = planes + plane
            w = field[comp, at]
            put(image_out, comp, plane,
                close[2, plane] * w - close[0, plane] * box(field[comp, at - 1] + w + field[comp, at + 1]))
        over(planes, body, 4)

    def filter_one(comp):
        @pl.when(jnp.logical_not(no_left))
        def _():
            near_copy(comp, 0).wait_recv()
            near_copy(comp, 1).wait_send()

        @pl.when(jnp.logical_not(no_right))
        def _():
            near_copy(comp, 1).wait_recv()
            near_copy(comp, 0).wait_send()

        for step in range(DEGREE):
            advance(step, comp)
        final_filter(comp)
        spread(filt_out, filt_in, filt_send, filt_recv, comp)

        @pl.when(comp > 0)
        def _():
            spread(image_out, image_in, image_send, image_recv, comp - 1)

        @pl.when(comp + 2 < comps)
        def _():
            start_near(comp + 2)

        final_image(comp)
        filt_in[comp, :, my_modes()] = filt_out[comp, my_tile]
        image_in[comp, :, my_modes()] = image_out[comp, my_tile]

    over(comps, filter_one)

    def add_edges(comp):
        @pl.when((me == owner_last) & jnp.logical_not(no_right))
        def _():
            arrived(edge_in.at[comp], edge_recv.at[comp])
            for group in range(groups):
                at = pl.ds(group * modes, modes)
                image_in[comp, :, at] = image_in[comp, :, at] - (2.0 * close[0, planes - 1, :8]) * edge_in[comp, :, at]

        @pl.when((me == owner_first) & jnp.logical_not(no_left))
        def _():
            arrived(edge_in.at[comp], edge_recv.at[comp])
            for group in range(groups):
                at = pl.ds(group * modes, modes)
                image_in[comp, :, at] = image_in[comp, :, at] - (2.0 * close[0, 0, 8:]) * edge_in[comp, :, at]

        @pl.when((me == owner_row) & jnp.logical_not(no_left))
        def _():
            arrived(edge_in.at[comp, pl.ds(0, 1)], edge_recv.at[comp])
            for group in range(groups):
                at = pl.ds(group * modes, modes)
                image_in[comp, 7, at] = image_in[comp, 7, at] - (2.0 * close[0, 0, 7]) * edge_in[comp, 0, at]

    def products(left, right):
        return lax.dot_general(left, right, (((1,), (1,)), ((), ())), precision=HIGH, preferred_element_type=jnp.float32)

    def pairs(ref, comp, first):
        return jnp.concatenate([ref[comp, first], ref[comp, first + 1]], axis=1)

    part[...] = jnp.zeros_like(part)

    def add_gram(comp):
        spread_wait(filt_in, filt_send, filt_recv, comp)
        sums = part[0]
        for row in range(0, 8, 2):
            filt = pairs(filt_in, comp, row)
            sums = sums + products(filt, jnp.concatenate([filt, filt], axis=0))
        part[0] = sums

    def add_cross(comp):
        spread_wait(image_in, image_send, image_recv, comp)
        add_edges(comp)
        sums = part[1, :, :every]
        for row in range(0, 8, 2):
            sums = sums + products(pairs(filt_in, comp, row), pairs(image_in, comp, row))
        part[1, :, :every] = sums

    over(comps, add_gram)

    opposite = mode_peer(groups // 2)
    core = lax.rem(me, 2)
    sibling = me + 1 - 2 * core

    def spread_again(comp):
        for step in far_first(groups):
            peer = mode_peer(step)
            remote(filt_out.at[comp, tile_of(mode_peer(step + groups // 2))], again_in.at[comp, :, my_modes()],
                   again_send.at[comp], again_recv.at[comp], blk, peer).start()
        again_in[comp, :, my_modes()] = filt_out[comp, tile_of(opposite)]

    def slots_of(which, phase):
        return ((part_in, groups, me), (in_y, side, my_y), (in_z, side, my_z), (total, groups, me))[phase]

    def send_sums(which, phase):
        target, count, my_slot = slots_of(which, phase)
        if phase == 0:
            own_tile = part[which, pl.ds(pl.multiple_of(me * 8, 8), 8)]
        else:
            before, before_count, _ = slots_of(which, phase - 1)
            own_tile = before[which, 0]
            for slot in range(1, before_count):
                own_tile = own_tile + before[which, slot]
            tiles_sent[which, phase - 1] = own_tile
        for step in far_first(count):
            if phase == 0 or phase == 3:
                to_blk, to_mode = blk, mode_peer(step)
            else:
                to_blk, to_mode = (y_peer, z_peer)[phase - 1](step), me
            if phase == 0:
                source = part.at[which, pl.ds(pl.multiple_of(mode_peer(step) * 8, 8), 8)]
            else:
                source = tiles_sent.at[which, phase - 1]
            remote(source, target.at[which, my_slot], sum_send.at[which, phase], sum_recv.at[which, phase],
                   to_blk, to_mode).start()
        target[which, my_slot] = own_tile

    def wait_sums(which, phase):
        target, count, _ = slots_of(which, phase)
        arrived(target.at[which, pl.ds(0, count - 1)], sum_recv.at[which, phase])

    send_sums(0, 0)
    spread(image_out, image_in, image_send, image_recv, comps - 1)
    over(comps - 1, spread_again)
    wait_sums(0, 0)
    send_sums(0, 1)
    over(comps, add_cross)
    send_sums(1, 0)
    spread_again(comps - 1)
    wait_sums(0, 1)
    send_sums(0, 2)
    wait_sums(1, 0)
    send_sums(1, 1)
    wait_sums(0, 2)
    send_sums(0, 3)
    wait_sums(1, 1)
    send_sums(1, 2)
    wait_sums(0, 3)

    sums = total[0].reshape((every, 2 * every))
    row_at = lax.broadcasted_iota(jnp.int32, (every, 2 * every), 0)
    lane_at = lax.broadcasted_iota(jnp.int32, (every, 2 * every), 1)
    work = jnp.where(lane_at < every, jnp.where(lane_at == row_at, 1.0, 0.0), sums)
    blocks = [work[8 * j:8 * j + 8] for j in range(every // 8)]
    sub = lax.broadcasted_iota(jnp.int32, (8, 2 * every), 0)

    def column(block, lane):
        return jnp.take_along_axis(block, jnp.full((8, 2 * every), lane, jnp.int32), axis=1)

    def spread_row(block, row):
        return jnp.broadcast_to(block[row:row + 1], (8, 2 * every))

    for k in range(0, every, 2):
        j, r = divmod(k, 8)
        ones = [column(block, every + k) for block in blocks[j:]]
        twos = [column(block, every + k + 1) for block in blocks[j:]]
        row_one, row_two = spread_row(blocks[j], r), spread_row(blocks[j], r + 1)
        mixed = spread_row(ones[0], r + 1)
        over_one = 1.0 / spread_row(ones[0], r)
        factor = mixed * over_one
        over_two = 1.0 / (spread_row(twos[0], r + 1) - factor * mixed)
        new_two = row_two - factor * row_one
        scaled_one, scaled_two = row_one * over_one, new_two * over_two
        for i in range(j, every // 8):
            one, two = ones[i - j], twos[i - j]
            less = blocks[i] - (one * scaled_one + (two - one * factor) * scaled_two)
            if i == j:
                less = jnp.where(sub > r + 1, less, jnp.where(sub == r + 1, new_two, blocks[i]))
            blocks[i] = less
    work = jnp.concatenate(blocks, axis=0)
    diagonal = jnp.sum(jnp.where(lane_at == row_at + every, work, 0.0), axis=1, keepdims=True)
    inverse = (work / jnp.sqrt(diagonal))[:, :every]
    inverse_ref[...] = inverse

    def place(tile):
        return lax.div(tile, halves), pl.ds(pl.multiple_of(lax.rem(tile, halves) * 8, 8), 8)

    def back_copies(comp):
        plane, rows = place(my_tile)
        copies = []
        for step in far_first(groups):
            peer = mode_peer(step)
            copies.append((peer, remote(back.at[comp, pl.ds(peer * modes, modes)], out_ref.at[:, comp, plane, rows],
                                        back_send.at[comp], back_recv.at[comp], blk, peer)))
        return copies

    def own_copies(comp):
        plane, rows = place(my_tile)
        other_plane, other_rows = place(tile_of(opposite))
        return (pltpu.make_async_copy(back.at[comp, pl.ds(me * modes, modes)], out_ref.at[:, comp, plane, rows],
                                      own_send.at[0, comp]),
                pltpu.make_async_copy(again.at[comp, pl.ds(core * modes, modes)], out_ref.at[:, comp, other_plane, other_rows],
                                      own_send.at[1, comp]))

    def sibling_copy(comp):
        plane, rows = place(tile_of(opposite))
        return remote(again.at[comp, pl.ds((1 - core) * modes, modes)], out_ref.at[:, comp, plane, rows],
                      back_send.at[comp], back_recv.at[comp], blk, sibling)

    def give_back(comp):
        filt = jnp.concatenate([filt_in[comp, row] for row in range(8)], axis=1)
        result = jnp.dot(inverse, filt, precision=HIGH, preferred_element_type=jnp.float32)
        for row in range(8):
            back[comp, :, row] = result[:, row * nz:(row + 1) * nz]
        for peer, copy in back_copies(comp):
            @pl.when(lax.div(peer, 2) != lax.div(opposite, 2))
            def _():
                copy.start()
        own_copies(comp)[0].start()

    def give_sibling(comp):
        arrived(again_in.at[comp, :, pl.ds(0, (groups - 1) * modes)], again_recv.at[comp])
        arrived(again_in.at[comp, :, pl.ds(0, (groups - 1) * modes)], again_send.at[comp])
        filt = jnp.concatenate([again_in[comp, row] for row in range(8)], axis=1)
        mine = inverse_ref[pl.ds(pl.multiple_of((me - core) * modes, 2 * modes), 2 * modes), :]
        result = jnp.dot(mine, filt, precision=HIGH, preferred_element_type=jnp.float32)
        for row in range(8):
            again[comp, :, row] = result[:, row * nz:(row + 1) * nz]
        sibling_copy(comp).start()
        own_copies(comp)[1].start()

    give_back(0)
    wait_sums(1, 2)
    send_sums(1, 3)
    for comp in range(1, comps):
        give_back(comp)
    for comp in range(comps):
        give_sibling(comp)
    wait_sums(1, 3)
    cross = total[1].reshape((every, 2 * every))[:, :every]
    half = jnp.dot(inverse, cross, precision=HIGH, preferred_element_type=jnp.float32)
    product = lax.dot_general(half, inverse, (((1,), (1,)), ((), ())), precision=HIGH,
                              preferred_element_type=jnp.float32)
    proj_ref[...] = 0.5 * (product + product.T)

    def finish(comp):
        to_left, to_right = edge_copies(comp)

        @pl.when(jnp.logical_not(no_left))
        def _():
            for copy in to_left:
                copy.wait_send()

        @pl.when(jnp.logical_not(no_right))
        def _():
            for copy in to_right:
                copy.wait_send()

        for copy in own_copies(comp):
            copy.wait()
        most = back.at[comp, pl.ds(0, (groups - 2) * modes)]
        arrived(most, back_recv.at[comp])
        arrived(most, back_send.at[comp])

    over(comps, finish)
    for which in range(2):
        for phase in range(4):
            target, count, _ = slots_of(which, phase)
            arrived(target.at[which, pl.ds(0, count - 1)], sum_send.at[which, phase])


def shards(blks, groups, start_modes, materials, stiffness_table):
    modes, comps, planes, ny, nz = start_modes.shape
    every = modes * groups
    side = math.isqrt(blks)
    vmem, dma = pltpu.VMEM, pltpu.SemaphoreType.DMA
    f32 = jnp.float32
    plane = (ny, modes, nz)
    tiles_out = (comps, groups, 8, modes, nz)
    tiles_in = (comps, 8, every, nz)
    tile = (8, 2 * every)
    return pl.pallas_call(
        functools.partial(kernel, blks, groups),
        out_shape=(jax.ShapeDtypeStruct(start_modes.shape, f32), jax.ShapeDtypeStruct((every, every), f32)),
        in_specs=[pl.BlockSpec(memory_space=pltpu.HBM), pl.BlockSpec(memory_space=pltpu.HBM),
                  pl.BlockSpec(memory_space=pltpu.HBM)],
        out_specs=(pl.BlockSpec(memory_space=pl.ANY), pl.BlockSpec(memory_space=pltpu.VMEM)),
        scratch_shapes=[
            pltpu.SMEM(stiffness_table.shape, f32),
            vmem((comps, modes, planes, ny, nz), f32),
            vmem((planes, ny, nz), jnp.int32), vmem((planes, ny, nz), f32), vmem((2, planes, ny, nz), f32),
            vmem((2, 3 * planes) + plane, f32), vmem((3, planes) + plane, f32),
            vmem((comps, 3 * planes) + plane, f32), vmem((3 * planes,) + plane, f32),
            vmem((comps, 2, 9, modes, nz), f32), vmem(tiles_in, f32),
            vmem(tiles_out, f32), vmem(tiles_out, f32),
            vmem(tiles_in, f32), vmem(tiles_in, f32),
            vmem(tiles_in, f32), vmem((comps, 2 * modes, 8, nz), f32), vmem((every, every), f32),
            vmem((comps, every, 8, nz), f32),
            vmem((2, every, 2 * every), f32), vmem((2, groups) + tile, f32), vmem((2, side) + tile, f32),
            vmem((2, side) + tile, f32), vmem((2, groups) + tile, f32), vmem((2, 3) + tile, f32),
            dma((comps + 2,)), dma((2,)), dma((2,)),
            dma((2, comps)), dma((2, comps)), dma((comps, 3)), dma((comps,)),
            dma((comps,)), dma((comps,)), dma((comps,)), dma((comps,)),
            dma((comps,)), dma((comps,)), dma((2, comps)), dma((comps,)), dma((comps,)), dma((2, 4)), dma((2, 4)),
        ],
        compiler_params=pltpu.CompilerParams(
            collective_id=0, has_side_effects=True, vmem_limit_bytes=48 * 1024 * 1024),
    )(pltpu.with_memory_space_constraint(start_modes, pltpu.HBM),
      pltpu.with_memory_space_constraint(materials, pltpu.HBM),
      pltpu.with_memory_space_constraint(stiffness_table, pltpu.HBM))


def solution(mesh):
    return jax.shard_map(
        functools.partial(shards, mesh.shape["blk"], mesh.shape["mode"]),
        mesh=mesh,
        in_specs=(P("mode", None, "blk", None, None), P("blk", None, None), P()),
        out_specs=(P("mode", None, "blk", None, None), P()),
        check_vma=False,
    )
```

```python
import functools
import math

import jax
import jax.numpy as jnp
from jax import lax
from jax.experimental import pallas as pl
from jax.experimental.pallas import tpu as pltpu
from jax.sharding import PartitionSpec as P

CENTER = 64.0
HALF_WIDTH = 56.0
MASS_SHIFT = 0.5
MESH = pl.DeviceIdType.MESH
HIGH = lax.Precision.HIGHEST
DEGREE = 4


def kernel(blks, groups, x_ref, mat_ref, tab_hbm, out_ref, proj_ref,
           tab_ref, own, mats, table, table_in, coef, close, field, odd, edge_out, edge_in,
           filt_out, image_out, filt_in, image_in, again_in, again, inverse_ref,
           back, part, part_in, in_y, in_z, total, tiles_sent,
           load, table_send, table_recv, near_send, near_recv, edge_send, edge_recv,
           filt_send, filt_recv, image_send, image_recv,
           back_send, back_recv, own_send, again_send, again_recv, sum_send, sum_recv):
    modes, comps, planes, ny, nz = x_ref.shape
    every = modes * groups
    halves = ny // 8
    side = math.isqrt(blks)
    blk, me = lax.axis_index("blk"), lax.axis_index("mode")
    left, right = lax.rem(blk + blks - 1, blks), lax.rem(blk + 1, blks)
    my_z, my_y = lax.div(blk, side), lax.rem(blk, side)
    no_left, no_right = blk == 0, blk == blks - 1

    def mode_peer(step):
        return lax.rem(me + step, groups)

    def y_peer(step):
        return my_z * side + lax.rem(my_y + step, side)

    def z_peer(step):
        return lax.rem(my_z + step, side) * side + my_y

    def tile_of(device):
        return lax.rem(device, 2) * 4 + lax.rem(lax.div(device, 2), 2) * 2 + lax.div(device, 4)

    my_tile = tile_of(me)

    def far_first(count):
        return sorted(range(1, count), key=lambda step: abs(2 * step - count))

    def remote(src, dst, send, recv, to_blk, to_mode):
        return pltpu.make_async_remote_copy(
            src_ref=src, dst_ref=dst, send_sem=send, recv_sem=recv,
            device_id={"blk": to_blk, "mode": to_mode}, device_id_type=MESH)

    def arrived(ref, semaphore):
        pltpu.make_async_copy(ref, ref, semaphore).wait()

    owner_last, owner_first, owner_row = 3, 4, 0

    load_mats = pltpu.make_async_copy(mat_ref, mats, load.at[comps])
    load_mats.start()
    load_tab = pltpu.make_async_copy(tab_hbm, tab_ref, load.at[comps + 1])
    load_tab.start()

    def load_own(comp):
        return pltpu.make_async_copy(x_ref.at[:, comp], own.at[comp], load.at[comp])

    for comp in range(comps):
        load_own(comp).start()

    barrier = pltpu.get_barrier_semaphore()

    def greet(to_blk, to_mode):
        pl.semaphore_signal(barrier, inc=1, device_id={"blk": to_blk, "mode": to_mode}, device_id_type=MESH)

    greet(left, me)
    greet(right, me)
    for step in range(1, side):
        greet(y_peer(step), me)
        greet(z_peer(step), me)
    for step in range(1, groups):
        greet(blk, mode_peer(step))

    @pl.when(me == owner_last)
    def _():
        for mode in range(groups):
            greet(right, mode)

    @pl.when((me == owner_first) | (me == owner_row))
    def _():
        for mode in range(groups):
            greet(left, mode)

    def over(count, body, unroll=1):
        def run(at, carry):
            body(at)
            return carry
        lax.fori_loop(0, count, run, 0, unroll=unroll)

    @pl.when(no_left)
    def _():
        table_in[0] = jnp.zeros_like(table)

        def clear(plane):
            for comp in range(comps):
                field[comp, plane] = jnp.zeros((ny, modes, nz), jnp.float32)
        over(planes, clear)

    @pl.when(no_right)
    def _():
        table_in[1] = jnp.zeros_like(table)

        def clear(plane):
            for comp in range(comps):
                field[comp, 2 * planes + plane] = jnp.zeros((ny, modes, nz), jnp.float32)
        over(planes, clear)

    scale = 2.0 / HALF_WIDTH

    def all_modes(rows):
        return jnp.broadcast_to(rows[:, None, :], (ny, modes, nz))

    def coefficients(values, plane):
        coef[0, plane] = all_modes(scale * (27.0 * values + (MASS_SHIFT - CENTER)))
        coef[1, plane] = all_modes(scale * values)

    load_mats.wait()
    load_tab.wait()

    def own_root(plane):
        labels = mats[plane]
        values = jnp.zeros((ny, nz), jnp.float32)
        for label in range(tab_ref.shape[0]):
            values = jnp.where(labels == label, tab_ref[label], values)
        table[plane] = values
        close[0, plane] = all_modes(jnp.sqrt(values))

    over(planes, own_root, planes)

    def weigh(comp):
        load_own(comp).wait()
        rows = own.at[comp].reshape(modes * planes * ny, nz)

        def body(plane):
            for y in range(ny):
                field[comp, planes + plane, y] = close[0, plane, y] * rows[pl.ds(plane * ny + y, modes, stride=planes * ny)]
        over(planes, body, 4)

    weigh(0)
    pl.semaphore_wait(barrier, 5 + (groups - 1) + 2 * (side - 1))

    def table_copy(slot):
        return remote(table, table_in.at[slot], table_send.at[slot], table_recv.at[slot], (right, left)[slot], me)

    def near_copy(comp, slot):
        return remote(field.at[comp, pl.ds(planes, planes)], field.at[comp, pl.ds(2 * planes * slot, planes)],
                      near_send.at[slot, comp], near_recv.at[slot, comp], (right, left)[slot], me)

    def edge_copies(comp):
        mine = pl.ds(pl.multiple_of(me * modes, modes), modes)
        to_left = [remote(edge_out.at[comp, 1, pl.ds(0, 8)], edge_in.at[comp, :, mine],
                          edge_send.at[comp, 0], edge_recv.at[comp], left, owner_last)]
        to_right = [remote(edge_out.at[comp, 0, pl.ds(1, 8)], edge_in.at[comp, :, mine],
                           edge_send.at[comp, 1], edge_recv.at[comp], right, owner_first),
                    remote(edge_out.at[comp, 0, pl.ds(0, 1)], edge_in.at[comp, pl.ds(0, 1), mine],
                           edge_send.at[comp, 2], edge_recv.at[comp], right, owner_row)]
        return to_left, to_right

    @pl.when(jnp.logical_not(no_left))
    def _():
        table_copy(1).start()
        near_copy(0, 1).start()

    @pl.when(jnp.logical_not(no_right))
    def _():
        table_copy(0).start()
        near_copy(0, 0).start()

    def start_near(comp):
        @pl.when(jnp.logical_not(no_left))
        def _():
            near_copy(comp, 1).start()

        @pl.when(jnp.logical_not(no_right))
        def _():
            near_copy(comp, 0).start()

    weigh(1)
    start_near(1)
    for comp in range(2, comps):
        weigh(comp)

    def own_coefficients(plane):
        values = table[plane]
        coefficients(values, planes + plane)
        root = jnp.sqrt(values)
        close[1, plane] = all_modes(1.0 / root)
        close[2, plane] = all_modes((27.0 * values + MASS_SHIFT) / root)

    over(planes, own_coefficients)

    @pl.when(jnp.logical_not(no_left))
    def _():
        table_copy(0).wait_recv()
        table_copy(1).wait_send()

    @pl.when(jnp.logical_not(no_right))
    def _():
        table_copy(1).wait_recv()
        table_copy(0).wait_send()

    def near_coefficients(plane):
        coefficients(table_in[0, plane], plane)
        coefficients(table_in[1, plane], 2 * planes + plane)

    over(planes, near_coefficients)

    none = jnp.zeros((1, modes, nz), jnp.float32)

    def box_z(v):
        lanes = lax.broadcasted_iota(jnp.int32, v.shape, 2)
        before = jnp.where(lanes == 0, 0.0, pltpu.roll(v, 1, 2))
        after = jnp.where(lanes == nz - 1, 0.0, pltpu.roll(v, nz - 1, 2))
        return v + (before + after)

    def box(u):
        return box_z(u + (jnp.concatenate([none, u[:-1]], axis=0) + jnp.concatenate([u[1:], none], axis=0)))

    def advance(step, comp):
        even = field.at[comp]
        now, other = (even, odd) if step % 2 == 0 else (odd, even)
        first = step + 1

        def body(at):
            plane = first + at
            w = now[plane]
            u = now[plane - 1] + w + now[plane + 1]
            new = coef[0, plane] * w - coef[1, plane] * box(u)
            if step == 0:
                new = 0.5 * new
            else:
                new = new - other[plane]
            other[plane] = new
        over(3 * planes - 2 * first, body, 3 * planes - 2 * first)

    def my_modes():
        return pl.ds(pl.multiple_of(me * modes, modes), modes)

    def spread(source, target, send, recv, comp):
        for step in range(1, groups):
            peer = mode_peer(step)
            remote(source.at[comp, tile_of(peer)], target.at[comp, :, my_modes()],
                   send.at[comp], recv.at[comp], blk, peer).start()

    def spread_wait(target, send, recv, comp):
        most = target.at[comp, :, pl.ds(0, (groups - 1) * modes)]
        arrived(most, recv.at[comp])
        arrived(most, send.at[comp])

    def put(target, comp, plane, value):
        for half in range(halves):
            target[comp, plane * halves + half] = value[8 * half:8 * half + 8]

    def final_filter(comp):
        def body(plane):
            put(filt_out, comp, plane, field[comp, planes + plane] * close[1, plane])
        over(planes, body, planes)

    def final_image(comp):
        first, last = field[comp, planes, :9], field[comp, 2 * planes - 1, 8:]
        edge_out[comp, 1, :8] = box_z(first[:8] + (first[1:] + jnp.concatenate([none, first[:7]], axis=0)))
        edge_out[comp, 0] = box_z(jnp.concatenate([none, last], axis=0) + (
            jnp.concatenate([last, none], axis=0) + jnp.concatenate([none, none, last[:-1]], axis=0)))
        to_left, to_right = edge_copies(comp)

        @pl.when(jnp.logical_not(no_left))
        def _():
            for copy in to_left:
                copy.start()

        @pl.when(jnp.logical_not(no_right))
        def _():
            for copy in to_right:
                copy.start()

        field[comp, planes - 1] = jnp.zeros((ny, modes, nz), jnp.float32)
        field[comp, 2 * planes] = jnp.zeros((ny, modes, nz), jnp.float32)

        def body(plane):
            at = planes + plane
            w = field[comp, at]
            put(image_out, comp, plane,
                close[2, plane] * w - close[0, plane] * box(field[comp, at - 1] + w + field[comp, at + 1]))
        over(planes, body, 4)

    def filter_one(comp):
        @pl.when(jnp.logical_not(no_left))
        def _():
            near_copy(comp, 0).wait_recv()
            near_copy(comp, 1).wait_send()

        @pl.when(jnp.logical_not(no_right))
        def _():
            near_copy(comp, 1).wait_recv()
            near_copy(comp, 0).wait_send()

        for step in range(DEGREE):
            advance(step, comp)
        final_filter(comp)
        spread(filt_out, filt_in, filt_send, filt_recv, comp)

        @pl.when(comp + 1 == comps)
        def _():
            spread(image_out, image_in, image_send, image_recv, comp - 1)

        @pl.when(comp + 2 < comps)
        def _():
            start_near(comp + 2)

        final_image(comp)

        @pl.when(comp + 2 < comps)
        def _():
            spread(image_out, image_in, image_send, image_recv, comp)

        filt_in[comp, :, my_modes()] = filt_out[comp, my_tile]
        image_in[comp, :, my_modes()] = image_out[comp, my_tile]

    over(comps, filter_one)

    def add_edges(comp):
        @pl.when((me == owner_last) & jnp.logical_not(no_right))
        def _():
            arrived(edge_in.at[comp], edge_recv.at[comp])
            for group in range(groups):
                at = pl.ds(group * modes, modes)
                image_in[comp, :, at] = image_in[comp, :, at] - (2.0 * close[0, planes - 1, :8]) * edge_in[comp, :, at]

        @pl.when((me == owner_first) & jnp.logical_not(no_left))
        def _():
            arrived(edge_in.at[comp], edge_recv.at[comp])
            for group in range(groups):
                at = pl.ds(group * modes, modes)
                image_in[comp, :, at] = image_in[comp, :, at] - (2.0 * close[0, 0, 8:]) * edge_in[comp, :, at]

        @pl.when((me == owner_row) & jnp.logical_not(no_left))
        def _():
            arrived(edge_in.at[comp, pl.ds(0, 1)], edge_recv.at[comp])
            for group in range(groups):
                at = pl.ds(group * modes, modes)
                image_in[comp, 7, at] = image_in[comp, 7, at] - (2.0 * close[0, 0, 7]) * edge_in[comp, 0, at]

    def products(left, right):
        return lax.dot_general(left, right, (((1,), (1,)), ((), ())), precision=HIGH, preferred_element_type=jnp.float32)

    def pairs(ref, comp, first):
        return jnp.concatenate([ref[comp, first], ref[comp, first + 1]], axis=1)

    part[...] = jnp.zeros_like(part)

    def add_gram(comp):
        spread_wait(filt_in, filt_send, filt_recv, comp)
        sums = part[0]
        for row in range(0, 8, 2):
            filt = pairs(filt_in, comp, row)
            sums = sums + products(filt, jnp.concatenate([filt, filt], axis=0))
        part[0] = sums

    def add_cross(comp):
        spread_wait(image_in, image_send, image_recv, comp)
        add_edges(comp)
        sums = part[1, :, :every]
        for row in range(0, 8, 2):
            sums = sums + products(pairs(filt_in, comp, row), pairs(image_in, comp, row))
        part[1, :, :every] = sums

    over(comps, add_gram)

    opposite = mode_peer(groups // 2)
    core = lax.rem(me, 2)
    sibling = me + 1 - 2 * core

    def spread_again(comp):
        for step in far_first(groups):
            peer = mode_peer(step)
            remote(filt_out.at[comp, tile_of(mode_peer(step + groups // 2))], again_in.at[comp, :, my_modes()],
                   again_send.at[comp], again_recv.at[comp], blk, peer).start()
        again_in[comp, :, my_modes()] = filt_out[comp, tile_of(opposite)]

    def slots_of(which, phase):
        return ((part_in, groups, me), (in_y, side, my_y), (in_z, side, my_z), (total, groups, me))[phase]

    def send_sums(which, phase):
        target, count, my_slot = slots_of(which, phase)
        if phase == 0:
            own_tile = part[which, pl.ds(pl.multiple_of(me * 8, 8), 8)]
        else:
            before, before_count, _ = slots_of(which, phase - 1)
            own_tile = before[which, 0]
            for slot in range(1, before_count):
                own_tile = own_tile + before[which, slot]
            tiles_sent[which, phase - 1] = own_tile
        for step in far_first(count):
            if phase == 0 or phase == 3:
                to_blk, to_mode = blk, mode_peer(step)
            else:
                to_blk, to_mode = (y_peer, z_peer)[phase - 1](step), me
            if phase == 0:
                source = part.at[which, pl.ds(pl.multiple_of(mode_peer(step) * 8, 8), 8)]
            else:
                source = tiles_sent.at[which, phase - 1]
            remote(source, target.at[which, my_slot], sum_send.at[which, phase], sum_recv.at[which, phase],
                   to_blk, to_mode).start()
        target[which, my_slot] = own_tile

    def wait_sums(which, phase):
        target, count, _ = slots_of(which, phase)
        arrived(target.at[which, pl.ds(0, count - 1)], sum_recv.at[which, phase])

    send_sums(0, 0)
    spread(image_out, image_in, image_send, image_recv, comps - 1)
    over(comps - 1, spread_again)
    wait_sums(0, 0)
    send_sums(0, 1)
    over(comps, add_cross)
    send_sums(1, 0)
    spread_again(comps - 1)
    wait_sums(0, 1)
    send_sums(0, 2)
    wait_sums(1, 0)
    send_sums(1, 1)
    wait_sums(0, 2)
    send_sums(0, 3)
    wait_sums(1, 1)
    send_sums(1, 2)
    wait_sums(0, 3)

    sums = total[0].reshape((every, 2 * every))
    row_at = lax.broadcasted_iota(jnp.int32, (every, 2 * every), 0)
    lane_at = lax.broadcasted_iota(jnp.int32, (every, 2 * every), 1)
    work = jnp.where(lane_at < every, jnp.where(lane_at == row_at, 1.0, 0.0), sums)
    blocks = [work[8 * j:8 * j + 8] for j in range(every // 8)]
    sub = lax.broadcasted_iota(jnp.int32, (8, 2 * every), 0)

    def column(block, lane):
        return jnp.take_along_axis(block, jnp.full((8, 2 * every), lane, jnp.int32), axis=1)

    def spread_row(block, row):
        return jnp.broadcast_to(block[row:row + 1], (8, 2 * every))

    for k in range(0, every, 2):
        j, r = divmod(k, 8)
        ones = [column(block, every + k) for block in blocks[j:]]
        twos = [column(block, every + k + 1) for block in blocks[j:]]
        row_one, row_two = spread_row(blocks[j], r), spread_row(blocks[j], r + 1)
        mixed = spread_row(ones[0], r + 1)
        over_one = 1.0 / spread_row(ones[0], r)
        factor = mixed * over_one
        over_two = 1.0 / (spread_row(twos[0], r + 1) - factor * mixed)
        new_two = row_two - factor * row_one
        scaled_one, scaled_two = row_one * over_one, new_two * over_two
        for i in range(j, every // 8):
            one, two = ones[i - j], twos[i - j]
            less = blocks[i] - (one * scaled_one + (two - one * factor) * scaled_two)
            if i == j:
                less = jnp.where(sub > r + 1, less, jnp.where(sub == r + 1, new_two, blocks[i]))
            blocks[i] = less
    work = jnp.concatenate(blocks, axis=0)
    diagonal = jnp.sum(jnp.where(lane_at == row_at + every, work, 0.0), axis=1, keepdims=True)
    inverse = (work / jnp.sqrt(diagonal))[:, :every]
    inverse_ref[...] = inverse

    def place(tile):
        return lax.div(tile, halves), pl.ds(pl.multiple_of(lax.rem(tile, halves) * 8, 8), 8)

    def back_copies(comp):
        plane, rows = place(my_tile)
        copies = []
        for step in far_first(groups):
            peer = mode_peer(step)
            copies.append((peer, remote(back.at[comp, pl.ds(peer * modes, modes)], out_ref.at[:, comp, plane, rows],
                                        back_send.at[comp], back_recv.at[comp], blk, peer)))
        return copies

    def own_copies(comp):
        plane, rows = place(my_tile)
        other_plane, other_rows = place(tile_of(opposite))
        return (pltpu.make_async_copy(back.at[comp, pl.ds(me * modes, modes)], out_ref.at[:, comp, plane, rows],
                                      own_send.at[0, comp]),
                pltpu.make_async_copy(again.at[comp, pl.ds(core * modes, modes)], out_ref.at[:, comp, other_plane, other_rows],
                                      own_send.at[1, comp]))

    def sibling_copy(comp):
        plane, rows = place(tile_of(opposite))
        return remote(again.at[comp, pl.ds((1 - core) * modes, modes)], out_ref.at[:, comp, plane, rows],
                      back_send.at[comp], back_recv.at[comp], blk, sibling)

    def give_back(comp):
        filt = jnp.concatenate([filt_in[comp, row] for row in range(8)], axis=1)
        result = jnp.dot(inverse, filt, precision=HIGH, preferred_element_type=jnp.float32)
        for row in range(8):
            back[comp, :, row] = result[:, row * nz:(row + 1) * nz]
        for peer, copy in back_copies(comp):
            @pl.when(lax.div(peer, 2) != lax.div(opposite, 2))
            def _():
                copy.start()
        own_copies(comp)[0].start()

    def give_sibling(comp):
        arrived(again_in.at[comp, :, pl.ds(0, (groups - 1) * modes)], again_recv.at[comp])
        arrived(again_in.at[comp, :, pl.ds(0, (groups - 1) * modes)], again_send.at[comp])
        filt = jnp.concatenate([again_in[comp, row] for row in range(8)], axis=1)
        mine = inverse_ref[pl.ds(pl.multiple_of((me - core) * modes, 2 * modes), 2 * modes), :]
        result = jnp.dot(mine, filt, precision=HIGH, preferred_element_type=jnp.float32)
        for row in range(8):
            again[comp, :, row] = result[:, row * nz:(row + 1) * nz]
        sibling_copy(comp).start()
        own_copies(comp)[1].start()

    give_back(0)
    wait_sums(1, 2)
    send_sums(1, 3)
    for comp in range(1, comps):
        give_back(comp)
    for comp in range(comps):
        give_sibling(comp)
    wait_sums(1, 3)
    cross = total[1].reshape((every, 2 * every))[:, :every]
    half = jnp.dot(inverse, cross, precision=HIGH, preferred_element_type=jnp.float32)
    product = lax.dot_general(half, inverse, (((1,), (1,)), ((), ())), precision=HIGH,
                              preferred_element_type=jnp.float32)
    proj_ref[...] = 0.5 * (product + product.T)

    def finish(comp):
        to_left, to_right = edge_copies(comp)

        @pl.when(jnp.logical_not(no_left))
        def _():
            for copy in to_left:
                copy.wait_send()

        @pl.when(jnp.logical_not(no_right))
        def _():
            for copy in to_right:
                copy.wait_send()

        for copy in own_copies(comp):
            copy.wait()
        most = back.at[comp, pl.ds(0, (groups - 2) * modes)]
        arrived(most, back_recv.at[comp])
        arrived(most, back_send.at[comp])

    over(comps, finish)
    for which in range(2):
        for phase in range(4):
            target, count, _ = slots_of(which, phase)
            arrived(target.at[which, pl.ds(0, count - 1)], sum_send.at[which, phase])


def shards(blks, groups, start_modes, materials, stiffness_table):
    modes, comps, planes, ny, nz = start_modes.shape
    every = modes * groups
    side = math.isqrt(blks)
    vmem, dma = pltpu.VMEM, pltpu.SemaphoreType.DMA
    f32 = jnp.float32
    plane = (ny, modes, nz)
    tiles_out = (comps, groups, 8, modes, nz)
    tiles_in = (comps, 8, every, nz)
    tile = (8, 2 * every)
    return pl.pallas_call(
        functools.partial(kernel, blks, groups),
        out_shape=(jax.ShapeDtypeStruct(start_modes.shape, f32), jax.ShapeDtypeStruct((every, every), f32)),
        in_specs=[pl.BlockSpec(memory_space=pltpu.HBM), pl.BlockSpec(memory_space=pltpu.HBM),
                  pl.BlockSpec(memory_space=pltpu.HBM)],
        out_specs=(pl.BlockSpec(memory_space=pl.ANY), pl.BlockSpec(memory_space=pltpu.VMEM)),
        scratch_shapes=[
            pltpu.SMEM(stiffness_table.shape, f32),
            vmem((comps, modes, planes, ny, nz), f32),
            vmem((planes, ny, nz), jnp.int32), vmem((planes, ny, nz), f32), vmem((2, planes, ny, nz), f32),
            vmem((2, 3 * planes) + plane, f32), vmem((3, planes) + plane, f32),
            vmem((comps, 3 * planes) + plane, f32), vmem((3 * planes,) + plane, f32),
            vmem((comps, 2, 9, modes, nz), f32), vmem(tiles_in, f32),
            vmem(tiles_out, f32), vmem(tiles_out, f32),
            vmem(tiles_in, f32), vmem(tiles_in, f32),
            vmem(tiles_in, f32), vmem((comps, 2 * modes, 8, nz), f32), vmem((every, every), f32),
            vmem((comps, every, 8, nz), f32),
            vmem((2, every, 2 * every), f32), vmem((2, groups) + tile, f32), vmem((2, side) + tile, f32),
            vmem((2, side) + tile, f32), vmem((2, groups) + tile, f32), vmem((2, 3) + tile, f32),
            dma((comps + 2,)), dma((2,)), dma((2,)),
            dma((2, comps)), dma((2, comps)), dma((comps, 3)), dma((comps,)),
            dma((comps,)), dma((comps,)), dma((comps,)), dma((comps,)),
            dma((comps,)), dma((comps,)), dma((2, comps)), dma((comps,)), dma((comps,)), dma((2, 4)), dma((2, 4)),
        ],
        compiler_params=pltpu.CompilerParams(
            collective_id=0, has_side_effects=True, vmem_limit_bytes=48 * 1024 * 1024),
    )(pltpu.with_memory_space_constraint(start_modes, pltpu.HBM),
      pltpu.with_memory_space_constraint(materials, pltpu.HBM),
      pltpu.with_memory_space_constraint(stiffness_table, pltpu.HBM))


def solution(mesh):
    return jax.shard_map(
        functools.partial(shards, mesh.shape["blk"], mesh.shape["mode"]),
        mesh=mesh,
        in_specs=(P("mode", None, "blk", None, None), P("blk", None, None), P()),
        out_specs=(P("mode", None, "blk", None, None), P()),
        check_vma=False,
    )
```

```python
import functools
import math

import jax
import jax.numpy as jnp
from jax import lax
from jax.experimental import pallas as pl
from jax.experimental.pallas import tpu as pltpu
from jax.sharding import PartitionSpec as P

CENTER = 64.0
HALF_WIDTH = 56.0
MASS_SHIFT = 0.5
MESH = pl.DeviceIdType.MESH
HIGH = lax.Precision.HIGHEST
DEGREE = 4


def kernel(blks, groups, x_ref, mat_ref, tab_hbm, out_ref, proj_ref,
           tab_ref, own, mats, table, table_in, coef, close, field, odd, edge_out, edge_in,
           filt_out, image_out, filt_in, image_in, again_in, again, inverse_ref,
           back, part, part_in, in_y, in_z, total, tiles_sent,
           load, table_send, table_recv, near_send, near_recv, edge_send, edge_recv,
           filt_send, filt_recv, image_send, image_recv,
           back_send, back_recv, own_send, again_send, again_recv, sum_send, sum_recv):
    modes, comps, planes, ny, nz = x_ref.shape
    every = modes * groups
    halves = ny // 8
    side = math.isqrt(blks)
    blk, me = lax.axis_index("blk"), lax.axis_index("mode")
    left, right = lax.rem(blk + blks - 1, blks), lax.rem(blk + 1, blks)
    my_z, my_y = lax.div(blk, side), lax.rem(blk, side)
    no_left, no_right = blk == 0, blk == blks - 1

    def mode_peer(step):
        return lax.rem(me + step, groups)

    def y_peer(step):
        return my_z * side + lax.rem(my_y + step, side)

    def z_peer(step):
        return lax.rem(my_z + step, side) * side + my_y

    def tile_of(device):
        return lax.rem(device, 2) * 4 + lax.rem(lax.div(device, 2), 2) * 2 + lax.div(device, 4)

    my_tile = tile_of(me)

    def far_first(count):
        return sorted(range(1, count), key=lambda step: abs(2 * step - count))

    def remote(src, dst, send, recv, to_blk, to_mode):
        return pltpu.make_async_remote_copy(
            src_ref=src, dst_ref=dst, send_sem=send, recv_sem=recv,
            device_id={"blk": to_blk, "mode": to_mode}, device_id_type=MESH)

    def arrived(ref, semaphore):
        pltpu.make_async_copy(ref, ref, semaphore).wait()

    owner_last, owner_first, owner_row = 3, 4, 0

    load_mats = pltpu.make_async_copy(mat_ref, mats, load.at[comps])
    load_mats.start()
    load_tab = pltpu.make_async_copy(tab_hbm, tab_ref, load.at[comps + 1])
    load_tab.start()

    def load_own(comp):
        return pltpu.make_async_copy(x_ref.at[:, comp], own.at[comp], load.at[comp])

    for comp in range(comps):
        load_own(comp).start()

    barrier = pltpu.get_barrier_semaphore()

    def greet(to_blk, to_mode):
        pl.semaphore_signal(barrier, inc=1, device_id={"blk": to_blk, "mode": to_mode}, device_id_type=MESH)

    greet(left, me)
    greet(right, me)
    for step in range(1, side):
        greet(y_peer(step), me)
        greet(z_peer(step), me)
    for step in range(1, groups):
        greet(blk, mode_peer(step))

    @pl.when(me == owner_last)
    def _():
        for mode in range(groups):
            greet(right, mode)

    @pl.when((me == owner_first) | (me == owner_row))
    def _():
        for mode in range(groups):
            greet(left, mode)

    def over(count, body, unroll=1):
        def run(at, carry):
            body(at)
            return carry
        lax.fori_loop(0, count, run, 0, unroll=unroll)

    @pl.when(no_left)
    def _():
        table_in[0] = jnp.zeros_like(table)

        def clear(plane):
            for comp in range(comps):
                field[comp, plane] = jnp.zeros((ny, modes, nz), jnp.float32)
        over(planes, clear)

    @pl.when(no_right)
    def _():
        table_in[1] = jnp.zeros_like(table)

        def clear(plane):
            for comp in range(comps):
                field[comp, 2 * planes + plane] = jnp.zeros((ny, modes, nz), jnp.float32)
        over(planes, clear)

    scale = 2.0 / HALF_WIDTH

    def all_modes(rows):
        return jnp.broadcast_to(rows[:, None, :], (ny, modes, nz))

    def coefficients(values, plane):
        coef[0, plane] = all_modes(scale * (27.0 * values + (MASS_SHIFT - CENTER)))
        coef[1, plane] = all_modes(scale * values)

    load_mats.wait()
    load_tab.wait()

    def own_root(plane):
        labels = mats[plane]
        values = jnp.zeros((ny, nz), jnp.float32)
        for label in range(tab_ref.shape[0]):
            values = jnp.where(labels == label, tab_ref[label], values)
        table[plane] = values
        close[0, plane] = all_modes(jnp.sqrt(values))

    over(planes, own_root, planes)

    def weigh(comp):
        load_own(comp).wait()
        rows = own.at[comp].reshape(modes * planes * ny, nz)

        def body(plane):
            for y in range(ny):
                field[comp, planes + plane, y] = close[0, plane, y] * rows[pl.ds(plane * ny + y, modes, stride=planes * ny)]
        over(planes, body, 4)

    weigh(0)
    pl.semaphore_wait(barrier, 5 + (groups - 1) + 2 * (side - 1))

    def table_copy(slot):
        return remote(table, table_in.at[slot], table_send.at[slot], table_recv.at[slot], (right, left)[slot], me)

    def near_copy(comp, slot):
        return remote(field.at[comp, pl.ds(planes, planes)], field.at[comp, pl.ds(2 * planes * slot, planes)],
                      near_send.at[slot, comp], near_recv.at[slot, comp], (right, left)[slot], me)

    def edge_copies(comp):
        mine = pl.ds(pl.multiple_of(me * modes, modes), modes)
        to_left = [remote(edge_out.at[comp, 1, pl.ds(0, 8)], edge_in.at[comp, :, mine],
                          edge_send.at[comp, 0], edge_recv.at[comp], left, owner_last)]
        to_right = [remote(edge_out.at[comp, 0, pl.ds(1, 8)], edge_in.at[comp, :, mine],
                           edge_send.at[comp, 1], edge_recv.at[comp], right, owner_first),
                    remote(edge_out.at[comp, 0, pl.ds(0, 1)], edge_in.at[comp, pl.ds(0, 1), mine],
                           edge_send.at[comp, 2], edge_recv.at[comp], right, owner_row)]
        return to_left, to_right

    @pl.when(jnp.logical_not(no_left))
    def _():
        table_copy(1).start()
        near_copy(0, 1).start()

    @pl.when(jnp.logical_not(no_right))
    def _():
        table_copy(0).start()
        near_copy(0, 0).start()

    def start_near(comp):
        @pl.when(jnp.logical_not(no_left))
        def _():
            near_copy(comp, 1).start()

        @pl.when(jnp.logical_not(no_right))
        def _():
            near_copy(comp, 0).start()

    weigh(1)
    start_near(1)
    for comp in range(2, comps):
        weigh(comp)

    def own_coefficients(plane):
        values = table[plane]
        coefficients(values, planes + plane)
        root = jnp.sqrt(values)
        close[1, plane] = all_modes(1.0 / root)
        close[2, plane] = all_modes((27.0 * values + MASS_SHIFT) / root)

    over(planes, own_coefficients)

    @pl.when(jnp.logical_not(no_left))
    def _():
        table_copy(0).wait_recv()
        table_copy(1).wait_send()

    @pl.when(jnp.logical_not(no_right))
    def _():
        table_copy(1).wait_recv()
        table_copy(0).wait_send()

    def near_coefficients(plane):
        coefficients(table_in[0, plane], plane)
        coefficients(table_in[1, plane], 2 * planes + plane)

    over(planes, near_coefficients)

    none = jnp.zeros((1, modes, nz), jnp.float32)

    def box_z(v):
        lanes = lax.broadcasted_iota(jnp.int32, v.shape, 2)
        before = jnp.where(lanes == 0, 0.0, pltpu.roll(v, 1, 2))
        after = jnp.where(lanes == nz - 1, 0.0, pltpu.roll(v, nz - 1, 2))
        return v + (before + after)

    def box(u):
        return box_z(u + (jnp.concatenate([none, u[:-1]], axis=0) + jnp.concatenate([u[1:], none], axis=0)))

    def put(target, comp, plane, value):
        for half in range(halves):
            target[comp, plane * halves + half] = value[8 * half:8 * half + 8]

    def advance(step, comp):
        even = field.at[comp]
        now, other = (even, odd) if step % 2 == 0 else (odd, even)
        first = step + 1

        def body(at):
            plane = first + at
            w = now[plane]
            u = now[plane - 1] + w + now[plane + 1]
            new = coef[0, plane] * w - coef[1, plane] * box(u)
            if step == 0:
                new = 0.5 * new
            else:
                new = new - other[plane]
            other[plane] = new
            if step == DEGREE - 1:
                put(filt_out, comp, plane - planes, new * close[1, plane - planes])
        over(3 * planes - 2 * first, body, 3 * planes - 2 * first)

    def my_modes():
        return pl.ds(pl.multiple_of(me * modes, modes), modes)

    def spread(source, target, send, recv, comp):
        for step in range(1, groups):
            peer = mode_peer(step)
            remote(source.at[comp, tile_of(peer)], target.at[comp, :, my_modes()],
                   send.at[comp], recv.at[comp], blk, peer).start()

    def spread_wait(target, send, recv, comp):
        most = target.at[comp, :, pl.ds(0, (groups - 1) * modes)]
        arrived(most, recv.at[comp])
        arrived(most, send.at[comp])

    def final_image(comp):
        first, last = field[comp, planes, :9], field[comp, 2 * planes - 1, 8:]
        edge_out[comp, 1, :8] = box_z(first[:8] + (first[1:] + jnp.concatenate([none, first[:7]], axis=0)))
        edge_out[comp, 0] = box_z(jnp.concatenate([none, last], axis=0) + (
            jnp.concatenate([last, none], axis=0) + jnp.concatenate([none, none, last[:-1]], axis=0)))
        to_left, to_right = edge_copies(comp)

        @pl.when(jnp.logical_not(no_left))
        def _():
            for copy in to_left:
                copy.start()

        @pl.when(jnp.logical_not(no_right))
        def _():
            for copy in to_right:
                copy.start()

        field[comp, planes - 1] = jnp.zeros((ny, modes, nz), jnp.float32)
        field[comp, 2 * planes] = jnp.zeros((ny, modes, nz), jnp.float32)

        def body(plane):
            at = planes + plane
            w = field[comp, at]
            put(image_out, comp, plane,
                close[2, plane] * w - close[0, plane] * box(field[comp, at - 1] + w + field[comp, at + 1]))
        over(planes, body, 4)

    def filter_one(comp):
        @pl.when(jnp.logical_not(no_left))
        def _():
            near_copy(comp, 0).wait_recv()
            near_copy(comp, 1).wait_send()

        @pl.when(jnp.logical_not(no_right))
        def _():
            near_copy(comp, 1).wait_recv()
            near_copy(comp, 0).wait_send()

        for step in range(DEGREE):
            advance(step, comp)
        spread(filt_out, filt_in, filt_send, filt_recv, comp)

        @pl.when(comp + 1 == comps)
        def _():
            spread(image_out, image_in, image_send, image_recv, comp - 1)

        @pl.when(comp + 2 < comps)
        def _():
            start_near(comp + 2)

        final_image(comp)

        @pl.when(comp + 2 < comps)
        def _():
            spread(image_out, image_in, image_send, image_recv, comp)

        filt_in[comp, :, my_modes()] = filt_out[comp, my_tile]
        image_in[comp, :, my_modes()] = image_out[comp, my_tile]

    over(comps, filter_one)

    def add_edges(comp):
        @pl.when((me == owner_last) & jnp.logical_not(no_right))
        def _():
            arrived(edge_in.at[comp], edge_recv.at[comp])
            for group in range(groups):
                at = pl.ds(group * modes, modes)
                image_in[comp, :, at] = image_in[comp, :, at] - (2.0 * close[0, planes - 1, :8]) * edge_in[comp, :, at]

        @pl.when((me == owner_first) & jnp.logical_not(no_left))
        def _():
            arrived(edge_in.at[comp], edge_recv.at[comp])
            for group in range(groups):
                at = pl.ds(group * modes, modes)
                image_in[comp, :, at] = image_in[comp, :, at] - (2.0 * close[0, 0, 8:]) * edge_in[comp, :, at]

        @pl.when((me == owner_row) & jnp.logical_not(no_left))
        def _():
            arrived(edge_in.at[comp, pl.ds(0, 1)], edge_recv.at[comp])
            for group in range(groups):
                at = pl.ds(group * modes, modes)
                image_in[comp, 7, at] = image_in[comp, 7, at] - (2.0 * close[0, 0, 7]) * edge_in[comp, 0, at]

    def products(left, right):
        return lax.dot_general(left, right, (((1,), (1,)), ((), ())), precision=HIGH, preferred_element_type=jnp.float32)

    def pairs(ref, comp, first):
        return jnp.concatenate([ref[comp, first], ref[comp, first + 1]], axis=1)

    part[...] = jnp.zeros_like(part)

    def add_gram(comp):
        spread_wait(filt_in, filt_send, filt_recv, comp)
        sums = part[0]
        for row in range(0, 8, 2):
            filt = pairs(filt_in, comp, row)
            sums = sums + products(filt, jnp.concatenate([filt, filt], axis=0))
        part[0] = sums

    def add_cross(comp):
        spread_wait(image_in, image_send, image_recv, comp)
        add_edges(comp)
        sums = part[1, :, :every]
        for row in range(0, 8, 2):
            sums = sums + products(pairs(filt_in, comp, row), pairs(image_in, comp, row))
        part[1, :, :every] = sums

    over(comps, add_gram)

    opposite = mode_peer(groups // 2)
    core = lax.rem(me, 2)
    sibling = me + 1 - 2 * core

    def spread_again(comp):
        for step in far_first(groups):
            peer = mode_peer(step)
            remote(filt_out.at[comp, tile_of(mode_peer(step + groups // 2))], again_in.at[comp, :, my_modes()],
                   again_send.at[comp], again_recv.at[comp], blk, peer).start()
        again_in[comp, :, my_modes()] = filt_out[comp, tile_of(opposite)]

    def slots_of(which, phase):
        return ((part_in, groups, me), (in_y, side, my_y), (in_z, side, my_z), (total, groups, me))[phase]

    def send_sums(which, phase):
        target, count, my_slot = slots_of(which, phase)
        if phase == 0:
            own_tile = part[which, pl.ds(pl.multiple_of(me * 8, 8), 8)]
        else:
            before, before_count, _ = slots_of(which, phase - 1)
            own_tile = before[which, 0]
            for slot in range(1, before_count):
                own_tile = own_tile + before[which, slot]
            tiles_sent[which, phase - 1] = own_tile
        for step in far_first(count):
            if phase == 0 or phase == 3:
                to_blk, to_mode = blk, mode_peer(step)
            else:
                to_blk, to_mode = (y_peer, z_peer)[phase - 1](step), me
            if phase == 0:
                source = part.at[which, pl.ds(pl.multiple_of(mode_peer(step) * 8, 8), 8)]
            else:
                source = tiles_sent.at[which, phase - 1]
            remote(source, target.at[which, my_slot], sum_send.at[which, phase], sum_recv.at[which, phase],
                   to_blk, to_mode).start()
        target[which, my_slot] = own_tile

    def wait_sums(which, phase):
        target, count, _ = slots_of(which, phase)
        arrived(target.at[which, pl.ds(0, count - 1)], sum_recv.at[which, phase])

    send_sums(0, 0)
    spread(image_out, image_in, image_send, image_recv, comps - 1)
    over(comps - 1, spread_again)
    wait_sums(0, 0)
    send_sums(0, 1)
    over(comps, add_cross)
    send_sums(1, 0)
    spread_again(comps - 1)
    wait_sums(0, 1)
    send_sums(0, 2)
    wait_sums(1, 0)
    send_sums(1, 1)
    wait_sums(0, 2)
    send_sums(0, 3)
    wait_sums(1, 1)
    send_sums(1, 2)
    wait_sums(0, 3)

    sums = total[0].reshape((every, 2 * every))
    row_at = lax.broadcasted_iota(jnp.int32, (every, 2 * every), 0)
    lane_at = lax.broadcasted_iota(jnp.int32, (every, 2 * every), 1)
    work = jnp.where(lane_at < every, jnp.where(lane_at == row_at, 1.0, 0.0), sums)
    blocks = [work[8 * j:8 * j + 8] for j in range(every // 8)]
    sub = lax.broadcasted_iota(jnp.int32, (8, 2 * every), 0)

    def column(block, lane):
        return jnp.take_along_axis(block, jnp.full((8, 2 * every), lane, jnp.int32), axis=1)

    def spread_row(block, row):
        return jnp.broadcast_to(block[row:row + 1], (8, 2 * every))

    for k in range(0, every, 2):
        j, r = divmod(k, 8)
        ones = [column(block, every + k) for block in blocks[j:]]
        twos = [column(block, every + k + 1) for block in blocks[j:]]
        row_one, row_two = spread_row(blocks[j], r), spread_row(blocks[j], r + 1)
        mixed = spread_row(ones[0], r + 1)
        over_one = 1.0 / spread_row(ones[0], r)
        factor = mixed * over_one
        over_two = 1.0 / (spread_row(twos[0], r + 1) - factor * mixed)
        new_two = row_two - factor * row_one
        scaled_one, scaled_two = row_one * over_one, new_two * over_two
        for i in range(j, every // 8):
            one, two = ones[i - j], twos[i - j]
            less = blocks[i] - (one * scaled_one + (two - one * factor) * scaled_two)
            if i == j:
                less = jnp.where(sub > r + 1, less, jnp.where(sub == r + 1, new_two, blocks[i]))
            blocks[i] = less
    work = jnp.concatenate(blocks, axis=0)
    diagonal = jnp.sum(jnp.where(lane_at == row_at + every, work, 0.0), axis=1, keepdims=True)
    inverse = (work / jnp.sqrt(diagonal))[:, :every]
    inverse_ref[...] = inverse

    def place(tile):
        return lax.div(tile, halves), pl.ds(pl.multiple_of(lax.rem(tile, halves) * 8, 8), 8)

    def back_copies(comp):
        plane, rows = place(my_tile)
        copies = []
        for step in far_first(groups):
            peer = mode_peer(step)
            copies.append((peer, remote(back.at[comp, pl.ds(peer * modes, modes)], out_ref.at[:, comp, plane, rows],
                                        back_send.at[comp], back_recv.at[comp], blk, peer)))
        return copies

    def own_copies(comp):
        plane, rows = place(my_tile)
        other_plane, other_rows = place(tile_of(opposite))
        return (pltpu.make_async_copy(back.at[comp, pl.ds(me * modes, modes)], out_ref.at[:, comp, plane, rows],
                                      own_send.at[0, comp]),
                pltpu.make_async_copy(again.at[comp, pl.ds(core * modes, modes)], out_ref.at[:, comp, other_plane, other_rows],
                                      own_send.at[1, comp]))

    def sibling_copy(comp):
        plane, rows = place(tile_of(opposite))
        return remote(again.at[comp, pl.ds((1 - core) * modes, modes)], out_ref.at[:, comp, plane, rows],
                      back_send.at[comp], back_recv.at[comp], blk, sibling)

    def give_back(comp):
        filt = jnp.concatenate([filt_in[comp, row] for row in range(8)], axis=1)
        result = jnp.dot(inverse, filt, precision=HIGH, preferred_element_type=jnp.float32)
        for row in range(8):
            back[comp, :, row] = result[:, row * nz:(row + 1) * nz]
        for peer, copy in back_copies(comp):
            @pl.when(lax.div(peer, 2) != lax.div(opposite, 2))
            def _():
                copy.start()
        own_copies(comp)[0].start()

    def give_sibling(comp):
        arrived(again_in.at[comp, :, pl.ds(0, (groups - 1) * modes)], again_recv.at[comp])
        arrived(again_in.at[comp, :, pl.ds(0, (groups - 1) * modes)], again_send.at[comp])
        filt = jnp.concatenate([again_in[comp, row] for row in range(8)], axis=1)
        mine = inverse_ref[pl.ds(pl.multiple_of((me - core) * modes, 2 * modes), 2 * modes), :]
        result = jnp.dot(mine, filt, precision=HIGH, preferred_element_type=jnp.float32)
        for row in range(8):
            again[comp, :, row] = result[:, row * nz:(row + 1) * nz]
        sibling_copy(comp).start()
        own_copies(comp)[1].start()

    give_back(0)
    wait_sums(1, 2)
    send_sums(1, 3)
    for comp in range(1, comps):
        give_back(comp)
    for comp in range(comps):
        give_sibling(comp)
    wait_sums(1, 3)
    cross = total[1].reshape((every, 2 * every))[:, :every]
    half = jnp.dot(inverse, cross, precision=HIGH, preferred_element_type=jnp.float32)
    product = lax.dot_general(half, inverse, (((1,), (1,)), ((), ())), precision=HIGH,
                              preferred_element_type=jnp.float32)
    proj_ref[...] = 0.5 * (product + product.T)

    def finish(comp):
        to_left, to_right = edge_copies(comp)

        @pl.when(jnp.logical_not(no_left))
        def _():
            for copy in to_left:
                copy.wait_send()

        @pl.when(jnp.logical_not(no_right))
        def _():
            for copy in to_right:
                copy.wait_send()

        for copy in own_copies(comp):
            copy.wait()
        most = back.at[comp, pl.ds(0, (groups - 2) * modes)]
        arrived(most, back_recv.at[comp])
        arrived(most, back_send.at[comp])

    over(comps, finish)
    for which in range(2):
        for phase in range(4):
            target, count, _ = slots_of(which, phase)
            arrived(target.at[which, pl.ds(0, count - 1)], sum_send.at[which, phase])


def shards(blks, groups, start_modes, materials, stiffness_table):
    modes, comps, planes, ny, nz = start_modes.shape
    every = modes * groups
    side = math.isqrt(blks)
    vmem, dma = pltpu.VMEM, pltpu.SemaphoreType.DMA
    f32 = jnp.float32
    plane = (ny, modes, nz)
    tiles_out = (comps, groups, 8, modes, nz)
    tiles_in = (comps, 8, every, nz)
    tile = (8, 2 * every)
    return pl.pallas_call(
        functools.partial(kernel, blks, groups),
        out_shape=(jax.ShapeDtypeStruct(start_modes.shape, f32), jax.ShapeDtypeStruct((every, every), f32)),
        in_specs=[pl.BlockSpec(memory_space=pltpu.HBM), pl.BlockSpec(memory_space=pltpu.HBM),
                  pl.BlockSpec(memory_space=pltpu.HBM)],
        out_specs=(pl.BlockSpec(memory_space=pl.ANY), pl.BlockSpec(memory_space=pltpu.VMEM)),
        scratch_shapes=[
            pltpu.SMEM(stiffness_table.shape, f32),
            vmem((comps, modes, planes, ny, nz), f32),
            vmem((planes, ny, nz), jnp.int32), vmem((planes, ny, nz), f32), vmem((2, planes, ny, nz), f32),
            vmem((2, 3 * planes) + plane, f32), vmem((3, planes) + plane, f32),
            vmem((comps, 3 * planes) + plane, f32), vmem((3 * planes,) + plane, f32),
            vmem((comps, 2, 9, modes, nz), f32), vmem(tiles_in, f32),
            vmem(tiles_out, f32), vmem(tiles_out, f32),
            vmem(tiles_in, f32), vmem(tiles_in, f32),
            vmem(tiles_in, f32), vmem((comps, 2 * modes, 8, nz), f32), vmem((every, every), f32),
            vmem((comps, every, 8, nz), f32),
            vmem((2, every, 2 * every), f32), vmem((2, groups) + tile, f32), vmem((2, side) + tile, f32),
            vmem((2, side) + tile, f32), vmem((2, groups) + tile, f32), vmem((2, 3) + tile, f32),
            dma((comps + 2,)), dma((2,)), dma((2,)),
            dma((2, comps)), dma((2, comps)), dma((comps, 3)), dma((comps,)),
            dma((comps,)), dma((comps,)), dma((comps,)), dma((comps,)),
            dma((comps,)), dma((comps,)), dma((2, comps)), dma((comps,)), dma((comps,)), dma((2, 4)), dma((2, 4)),
        ],
        compiler_params=pltpu.CompilerParams(
            collective_id=0, has_side_effects=True, vmem_limit_bytes=48 * 1024 * 1024),
    )(pltpu.with_memory_space_constraint(start_modes, pltpu.HBM),
      pltpu.with_memory_space_constraint(materials, pltpu.HBM),
      pltpu.with_memory_space_constraint(stiffness_table, pltpu.HBM))


def solution(mesh):
    return jax.shard_map(
        functools.partial(shards, mesh.shape["blk"], mesh.shape["mode"]),
        mesh=mesh,
        in_specs=(P("mode", None, "blk", None, None), P("blk", None, None), P()),
        out_specs=(P("mode", None, "blk", None, None), P()),
        check_vma=False,
    )
```
